32 devices in a mesh: tile: 8 (over y, x, core), trc: 4 (over z).
Axes of the slice: x: 2, y: 2, z: 4, core: 2. Of those that a mesh axis runs over, the one named last changes fastest.
Arguments:
- tracers: float32 [16, 8, 64, 128], P('trc', None, 'tile'), may hold values from -6 to 6
- flux_pool: float32 [4, 2, 3, 8, 64, 128], P('trc', None, None, None, 'tile'), may hold values from -0.45 to 0.45
- mass_pool: float32 [4, 2, 8, 64, 128], P('trc', None, None, 'tile'), may hold values from 1 to 2
- owner: int32 [2, 8], P(None, 'tile'), may hold values from 0 to 3
- conv_cols: int32 [8, 256], P('tile'), may hold values from 0 to 1023, as said below
- conv_steps: int32 [8, 256], P('tile'), may hold values from 1 to 3
- conv_rate: float32 [8, 7, 256], P('tile'), may hold values from 0.05 to 0.5
Outputs:
- advected: float32 [16, 8, 64, 128], P('trc', None, 'tile')
The draws below stay inside these ranges and needn't reach their ends.
Inputs may be any that keep to these rules, and one draw needn't show every extreme that they name: `conv_cols`: the 256 columns listed for one tile are all different.
All inputs are finite; a program needn't handle non-finite values.
Results may differ from the reference program's by a relative error of at most 0.0003.
Values sent between devices are 32-bit elements; how exact they have to be, the bound alone decides.
A program may use at most 64 MiB of HBM per device.

```python
import math
import jax
import jax.numpy as jnp
from jax import lax

CX = 8
NY = 128
NZ = 8
STEPS = 2
TRACERS = 16
NX = 64
CONV = 256
N_TILE = 8
N_TRC = 4


def draw_conv_cols(key, part):
    column_total = CX * NY
    keys_all = jax.random.split(key, N_TILE)
    orders = jax.vmap(lambda single_key: jax.random.permutation(single_key, column_total))(keys_all)[:, :CONV]
    leading = orders[:, 0]
    tile_ids = jnp.arange(N_TILE)
    offsets = jnp.where(tile_ids == 0, column_total - 1 - leading, jnp.where(tile_ids == 1, -leading, 0))
    return ((orders + offsets[:, None]) % column_total).astype(jnp.int32)


def draw_conv_steps(key, part):
    heaviness = jax.random.randint(jax.random.fold_in(key, 1), (N_TILE, 1), 0, 3)
    raw_draw = jax.random.randint(jax.random.fold_in(key, 2), (N_TILE, CONV), 0, 3)
    counts = 1 + jnp.minimum(raw_draw, heaviness)
    counts = counts.at[0, 0].set(3).at[0, 1].set(1)
    return counts.astype(jnp.int32)


def plant(array, stream_key, least, largest):
    longest = array.shape.index(max(array.shape))
    spots = []
    for shift in (0, 1):
        where = [jax.random.randint(jax.random.fold_in(stream_key, axis), (), 0, length) for axis, length in enumerate(array.shape)]
        where[longest] = (where[longest] + shift) % array.shape[longest]
        spots.append(tuple(where))
    return array.at[spots[0]].set(least).at[spots[1]].set(largest)


def level_of(stream_key, dims, pieces, low, top_value):
    loudness = 1.0
    for axis_at, parts in pieces:
        heights = jax.random.uniform(jax.random.fold_in(jax.random.fold_in(stream_key, 6), axis_at), (parts,), jnp.float32, low / len(pieces), top_value / len(pieces))
        loudness = loudness * jnp.repeat(jnp.exp(heights), dims[axis_at] // parts).reshape((-1,) + (1,) * (len(dims) - 1 - axis_at))
    return loudness


def noise(own_key, extent, width, reach, cuts=(), dtype=jnp.bfloat16):
    values = jax.random.normal(own_key, extent, jnp.float32) * width
    if len(cuts) > 0:
        values = level_of(own_key, extent, cuts, -0.22, 0.18) * values
    return jnp.clip(values, min=-reach, max=reach).astype(dtype)


def setup_inputs(seed: int = 0) -> dict:
    streams_of = jax.random.split(jax.random.key(seed), 8)
    tracers = noise(streams_of[0], (TRACERS, NZ, NX, NY), 1.0, 6.0, ((0, 4), (2, 8)), jnp.float32)
    flux_pool = jnp.clip(jax.random.uniform(streams_of[1], (N_TRC, STEPS, 3, NZ, NX, NY), jnp.float32, -0.45, 0.45) * level_of(streams_of[1], (N_TRC, STEPS, 3, NZ, NX, NY), ((0, 4), (4, 8)), -0.4, 0.0), -0.45, 0.45)
    mass_pool = jnp.clip(1.0 + 1.0 * jax.random.uniform(streams_of[2], (N_TRC, STEPS, NZ, NX, NY), jnp.float32) ** level_of(streams_of[2], (N_TRC, STEPS, NZ, NX, NY), ((0, 4), (3, 8)), -0.2, 0.2), 1.0, 2.0)
    owner = plant(jax.random.randint(streams_of[3], (STEPS, N_TILE), 0, N_TRC), jax.random.fold_in(streams_of[3], 1), 0, N_TRC - 1).astype(jnp.int32)
    conv_cols = draw_conv_cols(jax.random.fold_in(streams_of[7], 71), 0)
    conv_steps = draw_conv_steps(jax.random.fold_in(streams_of[7], 71), 0)
    conv_rate = jnp.clip(jnp.exp(math.log(0.5) - 2.3025851 * jax.random.uniform(streams_of[6], (N_TILE, NZ - 1, CONV), jnp.float32) ** level_of(streams_of[6], (N_TILE, NZ - 1, CONV), ((0, 8),), -0.2, 0.2)), 0.05, 0.5)
    return dict(tracers=tracers, flux_pool=flux_pool, mass_pool=mass_pool, owner=owner, conv_cols=conv_cols, conv_steps=conv_steps, conv_rate=conv_rate)


def slab(values_in, first_index, how_many, along):
    position = along % values_in.ndim
    return lax.slice_in_dim(values_in, first_index, first_index + how_many, axis=position)


def pad_axis(values_in, along, pad_low, pad_high, pad_mode):
    widths = [(0, 0)] * values_in.ndim
    widths[along % values_in.ndim] = (pad_low, pad_high)
    return jnp.pad(values_in, widths, mode=pad_mode)


def closed_faces(face_flux, along):
    position = along % face_flux.ndim
    face_count = face_flux.shape[position]
    dims_shape = [1] * face_flux.ndim
    dims_shape[position] = face_count
    kept_mask = (jnp.arange(face_count) < face_count - 1).reshape(dims_shape)
    return jnp.where(kept_mask, face_flux, 0.0)


def parabola_sweep(padded, mass_pad, face_flux, along, length):
    count_edges = length + 3
    outer_left = slab(padded, 0, count_edges, along)
    inner_left = slab(padded, 1, count_edges, along)
    inner_right = slab(padded, 2, count_edges, along)
    outer_right = slab(padded, 3, count_edges, along)
    edge_values = (7.0 / 12.0) * (inner_left + inner_right) - (1.0 / 12.0) * (outer_left + outer_right)
    edge_values = jnp.clip(edge_values, jnp.minimum(inner_left, inner_right), jnp.maximum(inner_left, inner_right))
    count_cells = length + 2
    centre = slab(padded, 2, count_cells, along)
    left_edge = slab(edge_values, 0, count_cells, along)
    right_edge = slab(edge_values, 1, count_cells, along)
    extremum = (right_edge - centre) * (centre - left_edge) <= 0.0
    left_edge = jnp.where(extremum, centre, left_edge)
    right_edge = jnp.where(extremum, centre, right_edge)
    edge_jump = right_edge - left_edge
    curvature = 6.0 * (centre - 0.5 * (left_edge + right_edge))
    new_left = jnp.where(edge_jump * curvature > edge_jump * edge_jump, 3.0 * centre - 2.0 * right_edge, left_edge)
    new_right = jnp.where(-edge_jump * edge_jump > edge_jump * curvature, 3.0 * centre - 2.0 * left_edge, right_edge)
    edge_jump = new_right - new_left
    curvature = 6.0 * (centre - 0.5 * (new_left + new_right))
    face_count = length + 1
    upwind_mass = slab(mass_pad, 0, face_count, along)
    downwind_mass = slab(mass_pad, 1, face_count, along)
    forward = jnp.maximum(face_flux, 0.0) / upwind_mass
    backward = jnp.maximum(-face_flux, 0.0) / downwind_mass
    from_left = slab(new_right, 0, face_count, along) - 0.5 * forward * (
        slab(edge_jump, 0, face_count, along) - (1.0 - forward * (2.0 / 3.0)) * slab(curvature, 0, face_count, along))
    from_right = slab(new_left, 1, face_count, along) + 0.5 * backward * (
        slab(edge_jump, 1, face_count, along) + (1.0 - backward * (2.0 / 3.0)) * slab(curvature, 1, face_count, along))
    transport = face_flux * jnp.where(face_flux > 0.0, from_left, from_right)
    interior = slab(padded, 3, length, along)
    air_mass = slab(mass_pad, 1, length, along)
    return interior - (slab(transport, 1, length, along) - slab(transport, 0, length, along)) / air_mass


def local_sweep(tracer, face_flux, air_mass, along):
    length = tracer.shape[along]
    return parabola_sweep(pad_axis(tracer, along, 3, 3, "edge"), pad_axis(air_mass, along, 1, 1, "edge"),
                          pad_axis(closed_faces(face_flux, along), along, 1, 0, "constant"), along, length)


def convect(columns, rates, level_axis):
    lower_levels = slab(columns, 0, columns.shape[level_axis] - 1, level_axis)
    moved = rates * lower_levels
    return columns + pad_axis(moved, level_axis, 1, 0, "constant") - pad_axis(moved, level_axis, 0, 1, "constant")


def advect_tracer(single_tracer, x_flux, y_flux, z_flux, air_mass):
    result = parabola_sweep(pad_axis(single_tracer, -2, 3, 3, "wrap"), pad_axis(air_mass, -2, 1, 1, "wrap"),
                            pad_axis(x_flux, -2, 1, 0, "wrap"), -2, single_tracer.shape[-2])
    result = local_sweep(result, y_flux, air_mass, -1)
    return local_sweep(result, z_flux, air_mass, -3)


def reference(tracers, flux_pool, mass_pool, owner, conv_cols, conv_steps, conv_rate):
    flux_tiled = flux_pool.reshape(N_TRC, STEPS, 3, NZ, N_TILE, CX, NY)
    mass_tiled = mass_pool.reshape(N_TRC, STEPS, NZ, N_TILE, CX, NY)
    tile_ids = jnp.arange(N_TILE)
    tile_rows = tile_ids[:, None]
    rates = jnp.transpose(conv_rate, (1, 0, 2))
    state = tracers
    for moment in range(STEPS):
        step_flux = flux_tiled[:, moment]
        step_mass = mass_tiled[:, moment]
        chosen_flux = step_flux[owner[moment], :, :, tile_ids]
        chosen_flux = jnp.transpose(chosen_flux, (1, 2, 0, 3, 4)).reshape(3, NZ, NX, NY)
        chosen_mass = step_mass[owner[moment], :, tile_ids]
        chosen_mass = jnp.transpose(chosen_mass, (1, 0, 2, 3)).reshape(NZ, NX, NY)
        state = lax.map(lambda single_tracer: advect_tracer(single_tracer, chosen_flux[0], chosen_flux[1],
                                                            chosen_flux[2], chosen_mass), state)
        flattened = state.reshape(TRACERS, NZ, N_TILE, CX * NY)
        columns = flattened[:, :, tile_rows, conv_cols]
        for substep in range(3):
            columns = jnp.where(conv_steps > substep, convect(columns, rates, -3), columns)
        state = flattened.at[:, :, tile_rows, conv_cols].set(columns).reshape(TRACERS, NZ, NX, NY)
    return state
```

```python
import functools

import jax
import jax.numpy as jnp
from jax import lax
from jax.experimental import pallas as pl
from jax.experimental.pallas import tpu as pltpu
from jax.sharding import PartitionSpec as P

FIELDS = 4
HALO = 3
SUBSTEPS = 3


def face_terms(flux, left_inverse, right_inverse):
    share = jnp.abs(flux) * jnp.where(flux > 0.0, left_inverse, right_inverse)
    half = 0.5 * flux * share
    bent = half * (3.0 - 2.0 * share)
    return flux - half - bent, half - bent


def edge_rise(before, here, after):
    raw = 0.5 * here + (1.0 / 12.0) * (before - after)
    return jnp.clip(raw, jnp.minimum(here, 0.0), jnp.maximum(here, 0.0))


def limited(up, down):
    up2 = up + up
    down2 = down + down
    right = jnp.clip(up, jnp.minimum(down2, 0.0), jnp.maximum(down2, 0.0))
    left = -jnp.clip(down, jnp.minimum(up2, 0.0), jnp.maximum(up2, 0.0))
    return right, left


def transport(flux, near, far, q0, right0, left0, q1, right1, left1):
    ahead = flux > 0.0
    return (
        flux * jnp.where(ahead, q0, q1)
        + near * jnp.where(ahead, right0, left1)
        + far * jnp.where(ahead, left0, right1)
    )


def kernel(
    dims,
    owner_ref, cols_ref, counts_ref, rate_ref, tracer_hbm, flux_hbm, mass_hbm,
    out_ref,
    own, inbox, relay, met, state, swept, halo_out, halo_in, rim_out, rim_in,
    cx, cy, cz, inverse_t, inverse_o, lift,
    own_sem, state_sem, chain_send, chain_recv, halo_send, halo_recv, rim_send, rim_recv,
):
    tiles, groups, steps, tracers, levels, cells, lats = dims
    rows = levels * cells
    tile = lax.axis_index("tile")
    me = lax.axis_index("trc")
    right = lax.rem(tile + 1, tiles)
    left = lax.rem(tile + tiles - 1, tiles)
    near = lax.div(2 * me, groups)
    far = 1 - near
    near_to = me + 1 - 2 * near
    far_to = me - 1 + 2 * near
    at_end = jnp.logical_or(me == 0, me == groups - 1)
    inner = jnp.logical_and(me > 0, me < groups - 1)
    chunk_total = steps * FIELDS

    load_state = pltpu.make_async_copy(tracer_hbm, state, state_sem)
    load_state.start()
    loads = []
    for s in range(steps):
        base = s * FIELDS * rows
        loads.append(pltpu.make_async_copy(
            mass_hbm.at[pl.ds(s * rows, rows)], own.at[pl.ds(base, rows)], own_sem.at[2 * s]))
        loads.append(pltpu.make_async_copy(
            flux_hbm.at[pl.ds(s * 3 * rows, 3 * rows)], own.at[pl.ds(base + rows, 3 * rows)],
            own_sem.at[2 * s + 1]))
    for load in loads:
        load.start()

    barrier = pltpu.get_barrier_semaphore()
    for neighbour in (left, right):
        pl.semaphore_signal(barrier, inc=1, device_id={"tile": neighbour}, device_id_type=pl.DeviceIdType.MESH)

    @pl.when(me > 0)
    def _():
        pl.semaphore_signal(barrier, inc=1, device_id={"trc": me - 1}, device_id_type=pl.DeviceIdType.MESH)

    @pl.when(me < groups - 1)
    def _():
        pl.semaphore_signal(barrier, inc=1, device_id={"trc": me + 1}, device_id_type=pl.DeviceIdType.MESH)

    def cell_rows(base, x):
        return pl.ds(base + x, levels, stride=cells)

    def block(i, size):
        return pl.ds(pl.multiple_of(i * size, size), size)

    cols = cols_ref[...]
    x_start = jnp.zeros_like(cols)
    for x in range(1, cells):
        x_start += jnp.where(cols >= x * lats, lats, 0)
    listed = cols.shape[1]
    at_x = x_start == lax.broadcasted_iota(jnp.int32, (cells, listed), 0) * lats
    at_y = ((cols - x_start) == lax.broadcasted_iota(jnp.int32, (lats, listed), 0)).astype(jnp.float32)
    spread = [jnp.where(at_x, counts_ref[...].astype(jnp.float32), 0.0)]
    for k in range(levels - 1):
        spread.append(jnp.where(at_x, rate_ref[pl.ds(k, 1), :], 0.0))
    dense = lax.dot_general(
        jnp.concatenate(spread, axis=0), at_y, (((1,), (1,)), ((), ())),
        precision=lax.Precision.HIGHEST, preferred_element_type=jnp.float32)
    count = dense[:cells]
    for n in range(SUBSTEPS):
        for k in range(levels - 1):
            lift[pl.ds((n * (levels - 1) + k) * cells, cells), :] = jnp.where(
                count > n + 0.5, dense[(k + 1) * cells:(k + 2) * cells], 0.0)

    def pack_halo(s, t, source, base):
        for i in range(HALO):
            at = (t * HALO + i) * levels
            halo_out[s, 0, pl.ds(at, levels), :] = source[cell_rows(base, cells - HALO + i), :]
            halo_out[s, 1, pl.ds(at, levels), :] = source[cell_rows(base, i), :]

    def halo_copy(s, side, t, how_many):
        size = HALO * levels
        at = pl.ds(pl.multiple_of(t * size, size), how_many * size)
        return pltpu.make_async_remote_copy(
            src_ref=halo_out.at[s, side, at], dst_ref=halo_in.at[s, side, at],
            send_sem=halo_send.at[s, side, t], recv_sem=halo_recv.at[s, side, t],
            device_id={"tile": left if side else right}, device_id_type=pl.DeviceIdType.MESH)

    load_state.wait()
    for t in range(tracers):
        pack_halo(0, t, state, t * rows)
    for load in loads:
        load.wait()

    expected = 2 + jnp.where(me > 0, 1, 0) + jnp.where(me < groups - 1, 1, 0)
    pl.semaphore_wait(barrier, expected)

    def raw(c):
        s, field = divmod(c, FIELDS)
        if field == 0:
            return mass_hbm.at[pl.ds(s * rows, rows)]
        return flux_hbm.at[pl.ds((s * 3 + field - 1) * rows, rows)]

    def chain_copy(c, way, to, source):
        at = pl.ds(c * rows, rows)
        return pltpu.make_async_remote_copy(
            src_ref=relay.at[way, at] if source is None else source, dst_ref=inbox.at[way, at],
            send_sem=chain_send.at[way, c], recv_sem=chain_recv.at[way, c],
            device_id={"trc": to}, device_id_type=pl.DeviceIdType.MESH)

    @pl.when(at_end)
    def _():
        for c in range(chunk_total):
            chain_copy(c, near, near_to, raw(c)).start()

    for side in (0, 1):
        halo_copy(0, side, 0, tracers).start()

    def owner_of(s):
        return jnp.full((rows, lats), owner_ref[s, 0], jnp.int32)

    def pass_on(c, way, to):
        at = pl.ds(c * rows, rows)
        relay[way, at, :] = jnp.where(owner_of(c // FIELDS) == me, own[at, :], inbox[way, at, :])
        chain_copy(c, way, to, None).start()

    def near_step(c):
        @pl.when(inner)
        def _():
            chain_copy(c, near, near_to, None).wait_recv()
            pass_on(c, near, near_to)

    def far_step(c):
        chain_copy(c, far, near_to, None).wait_recv()

        @pl.when(inner)
        def _():
            pass_on(c, far, far_to)

        at = pl.ds(c * rows, rows)
        holder = owner_of(c // FIELDS)
        met[at, :] = jnp.where(
            holder == me, own[at, :], jnp.where(holder < me, inbox[0, at, :], inbox[1, at, :]))

    def rim_copy(s, side):
        at = pl.ds(0, 2 * levels) if side == 0 else pl.ds(2 * levels, levels)
        return pltpu.make_async_remote_copy(
            src_ref=rim_out.at[s, at], dst_ref=rim_in.at[s, at],
            send_sem=rim_send.at[s, side], recv_sem=rim_recv.at[s, side],
            device_id={"tile": left if side else right}, device_id_type=pl.DeviceIdType.MESH)

    def start_rim(s):
        mass_at = s * FIELDS * rows
        rim_out[s, pl.ds(0, levels), :] = met[cell_rows(mass_at + rows, cells - 1), :]
        rim_out[s, pl.ds(levels, levels), :] = met[cell_rows(mass_at, cells - 1), :]
        rim_out[s, pl.ds(2 * levels, levels), :] = met[cell_rows(mass_at, 0), :]
        rim_copy(s, 0).start()
        rim_copy(s, 1).start()

    def x_terms(s):
        mass_at = s * FIELDS * rows
        inverses = [1.0 / rim_in[s, pl.ds(levels, levels), :]]
        fluxes = [rim_in[s, pl.ds(0, levels), :]]
        for x in range(cells):
            inverses.append(1.0 / met[cell_rows(mass_at, x), :])
            fluxes.append(met[cell_rows(mass_at + rows, x), :])
            inverse_t[pl.ds(x * levels, levels), :] = inverses[-1]
        inverses.append(1.0 / rim_in[s, pl.ds(2 * levels, levels), :])
        for x in range(cells + 1):
            at = pl.ds(x * levels, levels)
            cx[0, at, :] = fluxes[x]
            cx[1, at, :], cx[2, at, :] = face_terms(fluxes[x], inverses[x], inverses[x + 1])

    def y_terms(s):
        flux_at = (s * FIELDS + 2) * rows
        open_face = lax.broadcasted_iota(jnp.int32, (levels, lats), 1) < lats - 1
        for x in range(cells):
            at = pl.ds(x * levels, levels)
            flux = jnp.where(open_face, met[cell_rows(flux_at, x), :], 0.0)
            inverse = inverse_t[at, :]
            cy[0, at, :] = flux
            cy[1, at, :], cy[2, at, :] = face_terms(flux, inverse, pltpu.roll(inverse, lats - 1, 1))

    def z_terms(s):
        mass_at = s * FIELDS * rows
        flux_at = mass_at + 3 * rows
        inverses = []
        for k in range(levels):
            at = pl.ds(k * cells, cells)
            inverses.append(1.0 / met[pl.ds(mass_at + k * cells, cells), :])
            inverse_o[at, :] = inverses[-1]
        for k in range(levels - 1):
            at = pl.ds(k * cells, cells)
            flux = met[pl.ds(flux_at + k * cells, cells), :]
            cz[0, at, :] = flux
            cz[1, at, :], cz[2, at, :] = face_terms(flux, inverses[k], inverses[k + 1])

    def sweep_x(s, t):
        base = pl.multiple_of(t * rows, rows)
        q = []
        for i in range(HALO):
            q.append(halo_in[s, 0, block(t * HALO + i, levels), :])
        for x in range(cells):
            q.append(state[cell_rows(base, x), :])
        for i in range(HALO):
            q.append(halo_in[s, 1, block(t * HALO + i, levels), :])
        rise = [q[i + 1] - q[i] for i in range(cells + 5)]
        up = [edge_rise(rise[i], rise[i + 1], rise[i + 2]) for i in range(cells + 3)]
        shape = [limited(up[i + 1], rise[i + 1] - up[i]) for i in range(cells + 2)]
        moved = []
        for j in range(cells + 1):
            at = pl.ds(j * levels, levels)
            moved.append(transport(
                cx[0, at, :], cx[1, at, :], cx[2, at, :],
                q[j + 2], *shape[j], q[j + 3], *shape[j + 1]))
        return [
            q[x + 3] - (moved[x + 1] - moved[x]) * inverse_t[pl.ds(x * levels, levels), :]
            for x in range(cells)
        ]

    def sweep_y(x, q):
        at = pl.ds(x * levels, levels)
        inside = lax.broadcasted_iota(jnp.int32, (levels, lats), 1) < lats - 1

        def ahead(v):
            return pltpu.roll(v, lats - 1, 1)

        def behind(v):
            return pltpu.roll(v, 1, 1)

        q1 = ahead(q)
        rise = jnp.where(inside, q1 - q, 0.0)
        up = edge_rise(behind(rise), rise, ahead(rise))
        r, l = limited(up, behind(rise - up))
        moved = transport(cy[0, at, :], cy[1, at, :], cy[2, at, :], q, r, l, q1, ahead(r), ahead(l))
        return q - (moved - behind(moved)) * inverse_t[at, :]

    def sweep_xy(s, t):
        base = pl.multiple_of(t * rows, rows)
        after_x = sweep_x(s, t)
        for x in range(cells):
            swept[cell_rows(base, x), :] = sweep_y(x, after_x[x])

    def sweep_z(s, t):
        base = pl.multiple_of(t * rows, rows)
        q = [swept[pl.ds(base + k * cells, cells), :] for k in range(levels)]
        zero = jnp.zeros_like(q[0])
        rise = [zero] + [q[k + 1] - q[k] for k in range(levels - 1)] + [zero]
        up = [zero] + [edge_rise(rise[k], rise[k + 1], rise[k + 2]) for k in range(levels - 1)]
        shape = [(zero, zero)]
        for k in range(1, levels - 1):
            shape.append(limited(up[k + 1], rise[k] - up[k]))
        shape.append((zero, zero))
        moved = [zero]
        for k in range(levels - 1):
            at = pl.ds(k * cells, cells)
            moved.append(transport(
                cz[0, at, :], cz[1, at, :], cz[2, at, :], q[k], *shape[k], q[k + 1], *shape[k + 1]))
        moved.append(zero)
        q = [
            q[k] - (moved[k + 1] - moved[k]) * inverse_o[pl.ds(k * cells, cells), :]
            for k in range(levels)
        ]
        for n in range(SUBSTEPS):
            gain = [
                lift[pl.ds((n * (levels - 1) + k) * cells, cells), :] * q[k] for k in range(levels - 1)
            ]
            q = [
                (q[k] + gain[k - 1] if k else q[k]) - (gain[k] if k < levels - 1 else 0.0)
                for k in range(levels)
            ]
        target = out_ref if s == steps - 1 else state
        for k in range(levels):
            target[pl.ds(base + k * cells, cells), :] = q[k]

    def each_tracer(body):
        lax.fori_loop(0, tracers, lambda t, carry: (body(t), carry)[1], 0)

    def after_far(c):
        s, field = divmod(c, FIELDS)
        if field == 1:
            start_rim(s)
        if field == 2:
            rim_copy(s, 0).wait_recv()
            rim_copy(s, 1).wait_recv()
            x_terms(s)
            y_terms(s)
            if s == 0:
                for side in (0, 1):
                    halo_copy(0, side, 0, tracers).wait_recv()

            def xy(t):
                if s > 0:
                    for side in (0, 1):
                        halo_copy(s, side, t, 1).wait_recv()
                sweep_xy(s, t)

            each_tracer(xy)
        if field == 3:
            z_terms(s)

            def z(t):
                sweep_z(s, t)
                if s < steps - 1:
                    pack_halo(s + 1, t, state, pl.multiple_of(t * rows, rows))
                    for side in (0, 1):
                        halo_copy(s + 1, side, t, 1).start()

            each_tracer(z)

    near_step(0)
    for c in range(chunk_total):
        if c + 1 < chunk_total:
            near_step(c + 1)
        far_step(c)
        after_far(c)

    for side in (0, 1):
        halo_copy(0, side, 0, tracers).wait_send()
        for s in range(steps):
            rim_copy(s, side).wait_send()
    for s in range(1, steps):
        def left_device(t):
            for side in (0, 1):
                halo_copy(s, side, t, 1).wait_send()
        each_tracer(left_device)
    for c in range(chunk_total):
        chain_copy(c, near, near_to, None).wait_send()

    @pl.when(inner)
    def _():
        for c in range(chunk_total):
            chain_copy(c, far, far_to, None).wait_send()


def body(dims, tracers, flux_pool, mass_pool, owner, conv_cols, conv_steps, conv_rate):
    _, _, steps, count, levels, cells, lats = dims
    rows = levels * cells
    total = steps * FIELDS
    flat = (count * rows, lats)
    vmem = pl.BlockSpec(memory_space=pltpu.VMEM)
    hbm = pl.BlockSpec(memory_space=pl.ANY)
    f32 = jnp.float32
    out = pl.pallas_call(
        functools.partial(kernel, dims),
        out_shape=jax.ShapeDtypeStruct(flat, f32),
        in_specs=[pl.BlockSpec(memory_space=pltpu.SMEM), vmem, vmem, vmem, hbm, hbm, hbm],
        out_specs=vmem,
        scratch_shapes=[
            pltpu.VMEM((total * rows, lats), f32),
            pltpu.VMEM((2, total * rows, lats), f32),
            pltpu.VMEM((2, total * rows, lats), f32),
            pltpu.VMEM((total * rows, lats), f32),
            pltpu.VMEM(flat, f32),
            pltpu.VMEM(flat, f32),
            pltpu.VMEM((steps, 2, count * HALO * levels, lats), f32),
            pltpu.VMEM((steps, 2, count * HALO * levels, lats), f32),
            pltpu.VMEM((steps, 3 * levels, lats), f32),
            pltpu.VMEM((steps, 3 * levels, lats), f32),
            pltpu.VMEM((3, (cells + 1) * levels, lats), f32),
            pltpu.VMEM((3, rows, lats), f32),
            pltpu.VMEM((3, (levels - 1) * cells, lats), f32),
            pltpu.VMEM((rows, lats), f32),
            pltpu.VMEM((rows, lats), f32),
            pltpu.VMEM((SUBSTEPS * (levels - 1) * cells, lats), f32),
            pltpu.SemaphoreType.DMA((2 * steps,)),
            pltpu.SemaphoreType.DMA,
            pltpu.SemaphoreType.DMA((2, total)),
            pltpu.SemaphoreType.DMA((2, total)),
            pltpu.SemaphoreType.DMA((steps, 2, count)),
            pltpu.SemaphoreType.DMA((steps, 2, count)),
            pltpu.SemaphoreType.DMA((steps, 2)),
            pltpu.SemaphoreType.DMA((steps, 2)),
        ],
        compiler_params=pltpu.CompilerParams(collective_id=0, has_side_effects=True),
    )(
        owner, conv_cols, conv_steps, conv_rate[0], tracers.reshape(flat),
        flux_pool.reshape(steps * 3 * rows, lats), mass_pool.reshape(steps * rows, lats),
    )
    return out.reshape(tracers.shape)


def solution(mesh):
    def local(tracers, flux_pool, *rest):
        dims = (mesh.shape["tile"], mesh.shape["trc"], flux_pool.shape[1]) + tracers.shape
        return body(dims, tracers, flux_pool, *rest)

    in_specs = (
        P("trc", None, "tile", None),
        P("trc", None, None, None, "tile", None),
        P("trc", None, None, "tile", None),
        P(None, "tile"),
        P("tile", None),
        P("tile", None),
        P("tile", None, None),
    )
    out_specs = P("trc", None, "tile", None)
    return jax.shard_map(local, mesh=mesh, in_specs=in_specs, out_specs=out_specs, check_vma=False)
```

```python
import functools

import jax
import jax.numpy as jnp
from jax import lax
from jax.experimental import pallas as pl
from jax.experimental.pallas import tpu as pltpu
from jax.sharding import PartitionSpec as P

FIELDS = 4
HALO = 3
SUBSTEPS = 3
LEAD = 2


def face_terms(flux, left_inverse, right_inverse):
    share = jnp.abs(flux) * jnp.where(flux > 0.0, left_inverse, right_inverse)
    half = 0.5 * flux * share
    bent = half * (3.0 - 2.0 * share)
    return flux - half - bent, half - bent


def edge_rise(before, here, after):
    raw = 0.5 * here + (1.0 / 12.0) * (before - after)
    return jnp.clip(raw, jnp.minimum(here, 0.0), jnp.maximum(here, 0.0))


def limited(up, down):
    up2 = up + up
    down2 = down + down
    right = jnp.clip(up, jnp.minimum(down2, 0.0), jnp.maximum(down2, 0.0))
    left = -jnp.clip(down, jnp.minimum(up2, 0.0), jnp.maximum(up2, 0.0))
    return right, left


def transport(flux, near, far, q0, right0, left0, q1, right1, left1):
    ahead = flux > 0.0
    return (
        flux * jnp.where(ahead, q0, q1)
        + near * jnp.where(ahead, right0, left1)
        + far * jnp.where(ahead, left0, right1)
    )


def kernel(
    dims,
    owner_ref, cols_ref, counts_ref, rate_ref, tracer_hbm, flux_hbm, mass_hbm,
    out_ref,
    own, inbox, relay, met, state, swept, halo_out, halo_in, rim_out, rim_in,
    cx, cy, cz, inverse_t, inverse_o, lift,
    own_sem, state_sem, chain_send, chain_recv, halo_send, halo_recv, rim_send, rim_recv,
):
    tiles, groups, steps, tracers, levels, cells, lats = dims
    rows = levels * cells
    tile = lax.axis_index("tile")
    me = lax.axis_index("trc")
    right = lax.rem(tile + 1, tiles)
    left = lax.rem(tile + tiles - 1, tiles)
    near = lax.div(2 * me, groups)
    far = 1 - near
    near_to = me + 1 - 2 * near
    far_to = me - 1 + 2 * near
    at_end = jnp.logical_or(me == 0, me == groups - 1)
    inner = jnp.logical_and(me > 0, me < groups - 1)
    chunk_total = steps * FIELDS

    load_state = pltpu.make_async_copy(tracer_hbm, state, state_sem)
    load_state.start()
    loads = []
    for s in range(steps):
        base = s * FIELDS * rows
        loads.append(pltpu.make_async_copy(
            mass_hbm.at[pl.ds(s * rows, rows)], own.at[pl.ds(base, rows)], own_sem.at[2 * s]))
        loads.append(pltpu.make_async_copy(
            flux_hbm.at[pl.ds(s * 3 * rows, 3 * rows)], own.at[pl.ds(base + rows, 3 * rows)],
            own_sem.at[2 * s + 1]))
    for load in loads:
        load.start()

    barrier = pltpu.get_barrier_semaphore()
    for neighbour in (left, right):
        pl.semaphore_signal(barrier, inc=1, device_id={"tile": neighbour}, device_id_type=pl.DeviceIdType.MESH)

    @pl.when(me > 0)
    def _():
        pl.semaphore_signal(barrier, inc=1, device_id={"trc": me - 1}, device_id_type=pl.DeviceIdType.MESH)

    @pl.when(me < groups - 1)
    def _():
        pl.semaphore_signal(barrier, inc=1, device_id={"trc": me + 1}, device_id_type=pl.DeviceIdType.MESH)

    def cell_rows(base, x):
        return pl.ds(base + x, levels, stride=cells)

    def block(i, size):
        return pl.ds(pl.multiple_of(i * size, size), size)

    def pack_halo(s, t, source, base):
        for i in range(HALO):
            at = (t * HALO + i) * levels
            halo_out[s, 0, pl.ds(at, levels), :] = source[cell_rows(base, cells - HALO + i), :]
            halo_out[s, 1, pl.ds(at, levels), :] = source[cell_rows(base, i), :]

    def halo_copy(s, side, t, how_many):
        size = HALO * levels
        at = pl.ds(pl.multiple_of(t * size, size), how_many * size)
        return pltpu.make_async_remote_copy(
            src_ref=halo_out.at[s, side, at], dst_ref=halo_in.at[s, side, at],
            send_sem=halo_send.at[s, side, t], recv_sem=halo_recv.at[s, side, t],
            device_id={"tile": left if side else right}, device_id_type=pl.DeviceIdType.MESH)

    load_state.wait()
    for t in range(tracers):
        pack_halo(0, t, state, t * rows)

    expected = 2 + jnp.where(me > 0, 1, 0) + jnp.where(me < groups - 1, 1, 0)
    pl.semaphore_wait(barrier, expected)

    def raw(c):
        s, field = divmod(c, FIELDS)
        if field == 0:
            return mass_hbm.at[pl.ds(s * rows, rows)]
        return flux_hbm.at[pl.ds((s * 3 + field - 1) * rows, rows)]

    def chunk(c):
        return pl.ds(c * rows, rows) if isinstance(c, int) else block(c, rows)

    def chain_copy(c, way, to, source=None):
        at = chunk(c)
        return pltpu.make_async_remote_copy(
            src_ref=relay.at[way, at] if source is None else source, dst_ref=inbox.at[way, at],
            send_sem=chain_send.at[way, c], recv_sem=chain_recv.at[way, c],
            device_id={"trc": to}, device_id_type=pl.DeviceIdType.MESH)

    @pl.when(at_end)
    def _():
        for c in range(chunk_total):
            chain_copy(c, near, near_to, raw(c)).start()

    for side in (0, 1):
        halo_copy(0, side, 0, tracers).start()

    cols = cols_ref[...]
    x_start = jnp.zeros_like(cols)
    for x in range(1, cells):
        x_start += jnp.where(cols >= x * lats, lats, 0)
    listed = cols.shape[1]
    at_x = x_start == lax.broadcasted_iota(jnp.int32, (cells, listed), 0) * lats
    at_y = ((cols - x_start) == lax.broadcasted_iota(jnp.int32, (lats, listed), 0)).astype(jnp.float32)
    spread = [jnp.where(at_x, counts_ref[...].astype(jnp.float32), 0.0)]
    for k in range(levels - 1):
        spread.append(jnp.where(at_x, rate_ref[k], 0.0))
    dense = lax.dot_general(
        jnp.concatenate(spread, axis=0), at_y, (((1,), (1,)), ((), ())),
        precision=lax.Precision.HIGHEST, preferred_element_type=jnp.float32)
    count = dense[:cells]
    for n in range(SUBSTEPS):
        for k in range(levels - 1):
            lift[pl.ds((n * (levels - 1) + k) * cells, cells), :] = jnp.where(
                count > n + 0.5, dense[(k + 1) * cells:(k + 2) * cells], 0.0)

    for load in loads:
        load.wait()

    def owner_of(s):
        return jnp.full((rows, lats), owner_ref[0, s], jnp.int32)

    def pass_on(s, c, way, to):
        at = chunk(c)
        relay[way, at, :] = jnp.where(owner_of(s) == me, own[at, :], inbox[way, at, :])
        chain_copy(c, way, to).start()

    def near_step(s, c):
        @pl.when(inner)
        def _():
            chain_copy(c, near, near_to).wait_recv()
            pass_on(s, c, near, near_to)

    def far_arrives(s, c):
        chain_copy(c, far, near_to).wait_recv()

        @pl.when(inner)
        def _():
            pass_on(s, c, far, far_to)

    def choose(s, c):
        at = chunk(c)
        holder = owner_of(s)
        met[at, :] = jnp.where(
            holder == me, own[at, :], jnp.where(holder < me, inbox[0, at, :], inbox[1, at, :]))

    def far_step(s, c):
        far_arrives(s, c)
        choose(s, c)

    def rim_copy(s, side):
        at = pl.ds(0, 2 * levels) if side == 0 else pl.ds(2 * levels, levels)
        return pltpu.make_async_remote_copy(
            src_ref=rim_out.at[s, at], dst_ref=rim_in.at[s, at],
            send_sem=rim_send.at[s, side], recv_sem=rim_recv.at[s, side],
            device_id={"tile": left if side else right}, device_id_type=pl.DeviceIdType.MESH)

    def start_rim(s):
        mass_at = s * FIELDS * rows
        rim_out[s, pl.ds(0, levels), :] = met[cell_rows(mass_at + rows, cells - 1), :]
        rim_out[s, pl.ds(levels, levels), :] = met[cell_rows(mass_at, cells - 1), :]
        rim_out[s, pl.ds(2 * levels, levels), :] = met[cell_rows(mass_at, 0), :]
        rim_copy(s, 0).start()
        rim_copy(s, 1).start()

    def x_terms(s):
        mass_at = s * FIELDS * rows
        inverses = [1.0 / rim_in[s, pl.ds(levels, levels), :]]
        fluxes = [rim_in[s, pl.ds(0, levels), :]]
        for x in range(cells):
            inverses.append(1.0 / met[cell_rows(mass_at, x), :])
            fluxes.append(met[cell_rows(mass_at + rows, x), :])
            inverse_t[pl.ds(x * levels, levels), :] = inverses[-1]
        inverses.append(1.0 / rim_in[s, pl.ds(2 * levels, levels), :])
        for x in range(cells + 1):
            at = pl.ds(x * levels, levels)
            cx[0, at, :] = fluxes[x]
            cx[1, at, :], cx[2, at, :] = face_terms(fluxes[x], inverses[x], inverses[x + 1])

    def y_terms(s):
        flux_at = (s * FIELDS + 2) * rows
        open_face = lax.broadcasted_iota(jnp.int32, (levels, lats), 1) < lats - 1
        for x in range(cells):
            at = pl.ds(x * levels, levels)
            flux = jnp.where(open_face, met[cell_rows(flux_at, x), :], 0.0)
            inverse = inverse_t[at, :]
            cy[0, at, :] = flux
            cy[1, at, :], cy[2, at, :] = face_terms(flux, inverse, pltpu.roll(inverse, lats - 1, 1))

    def z_terms(s):
        mass_at = s * FIELDS * rows
        flux_at = mass_at + 3 * rows
        inverses = []
        for k in range(levels):
            at = pl.ds(k * cells, cells)
            inverses.append(1.0 / met[pl.ds(mass_at + k * cells, cells), :])
            inverse_o[at, :] = inverses[-1]
        for k in range(levels - 1):
            at = pl.ds(k * cells, cells)
            flux = met[pl.ds(flux_at + k * cells, cells), :]
            cz[0, at, :] = flux
            cz[1, at, :], cz[2, at, :] = face_terms(flux, inverses[k], inverses[k + 1])

    def sweep_x(s, t):
        base = pl.multiple_of(t * rows, rows)
        q = []
        for i in range(HALO):
            q.append(halo_in[s, 0, block(t * HALO + i, levels), :])
        for x in range(cells):
            q.append(state[cell_rows(base, x), :])
        for i in range(HALO):
            q.append(halo_in[s, 1, block(t * HALO + i, levels), :])
        rise = [q[i + 1] - q[i] for i in range(cells + 5)]
        up = [edge_rise(rise[i], rise[i + 1], rise[i + 2]) for i in range(cells + 3)]
        shape = [limited(up[i + 1], rise[i + 1] - up[i]) for i in range(cells + 2)]
        moved = []
        for j in range(cells + 1):
            at = pl.ds(j * levels, levels)
            moved.append(transport(
                cx[0, at, :], cx[1, at, :], cx[2, at, :],
                q[j + 2], *shape[j], q[j + 3], *shape[j + 1]))
        return [
            q[x + 3] - (moved[x + 1] - moved[x]) * inverse_t[pl.ds(x * levels, levels), :]
            for x in range(cells)
        ]

    def sweep_y(x, q):
        at = pl.ds(x * levels, levels)
        inside = lax.broadcasted_iota(jnp.int32, (levels, lats), 1) < lats - 1

        def ahead(v):
            return pltpu.roll(v, lats - 1, 1)

        def behind(v):
            return pltpu.roll(v, 1, 1)

        q1 = ahead(q)
        rise = jnp.where(inside, q1 - q, 0.0)
        up = edge_rise(behind(rise), rise, ahead(rise))
        r, l = limited(up, behind(rise - up))
        moved = transport(cy[0, at, :], cy[1, at, :], cy[2, at, :], q, r, l, q1, ahead(r), ahead(l))
        return q - (moved - behind(moved)) * inverse_t[at, :]

    def sweep_xy(s, some):
        after_x = [sweep_x(s, t) for t in some]
        for x in range(cells):
            for t, q in zip(some, after_x):
                swept[cell_rows(pl.multiple_of(t * rows, rows), x), :] = sweep_y(x, q[x])

    def sweep_z(s, t):
        base = pl.multiple_of(t * rows, rows)
        q = [swept[pl.ds(base + k * cells, cells), :] for k in range(levels)]
        zero = jnp.zeros_like(q[0])
        rise = [zero] + [q[k + 1] - q[k] for k in range(levels - 1)] + [zero]
        up = [zero] + [edge_rise(rise[k], rise[k + 1], rise[k + 2]) for k in range(levels - 1)]
        shape = [(zero, zero)]
        for k in range(1, levels - 1):
            shape.append(limited(up[k + 1], rise[k] - up[k]))
        shape.append((zero, zero))
        moved = [zero]
        for k in range(levels - 1):
            at = pl.ds(k * cells, cells)
            moved.append(transport(
                cz[0, at, :], cz[1, at, :], cz[2, at, :], q[k], *shape[k], q[k + 1], *shape[k + 1]))
        moved.append(zero)
        q = [
            q[k] - (moved[k + 1] - moved[k]) * inverse_o[pl.ds(k * cells, cells), :]
            for k in range(levels)
        ]
        for n in range(SUBSTEPS):
            gain = [
                lift[pl.ds((n * (levels - 1) + k) * cells, cells), :] * q[k] for k in range(levels - 1)
            ]
            q = [
                (q[k] + gain[k - 1] if k else q[k]) - (gain[k] if k < levels - 1 else 0.0)
                for k in range(levels)
            ]
        target = out_ref if s == steps - 1 else state
        for k in range(levels):
            target[pl.ds(base + k * cells, cells), :] = q[k]

    together = 2 if tracers % 2 == 0 else 1
    loops = tracers // together

    def each_group(body):
        def run(p, carry):
            body(p, [p * together + i for i in range(together)])
            return carry
        lax.fori_loop(0, loops, run, 0)

    def halo_arrives(s, some):
        for t in some:
            for side in (0, 1):
                halo_copy(s, side, t, 1).wait_recv()

    def rim_arrives(s):
        for side in (0, 1):
            rim_copy(s, side).wait_recv()

    def near_if(c):
        if c < chunk_total:
            near_step(c // FIELDS, c)

    for c in range(LEAD):
        near_if(c)
    far_done = 0
    for s in range(steps):
        first = s * FIELDS
        final = s == steps - 1
        for c in range(far_done, first + FIELDS - final):
            near_if(c + LEAD)
            far_step(s, c)
            if c == first + 1:
                start_rim(s)
        far_done = first + FIELDS
        if final:
            last = chunk_total - 1

            @pl.when(inner)
            def _():
                far_arrives(s, last)

        rim_arrives(s)
        x_terms(s)
        y_terms(s)
        if s == 0:
            for side in (0, 1):
                halo_copy(0, side, 0, tracers).wait_recv()
        if final:
            def do_xy(p, some):
                if s > 0:
                    halo_arrives(s, some)
                sweep_xy(s, some)
            each_group(do_xy)

            @pl.when(at_end)
            def _():
                far_arrives(s, last)

            choose(s, last)
            z_terms(s)
            each_group(lambda p, some: [sweep_z(s, t) for t in some])
        else:
            z_terms(s)
            slots = loops if loops <= FIELDS - LEAD else 0

            def do_all(p, some):
                if s > 0:
                    halo_arrives(s, some)
                sweep_xy(s, some)
                for t in some:
                    sweep_z(s, t)
                for t in some:
                    pack_halo(s + 1, t, state, pl.multiple_of(t * rows, rows))
                    for side in (0, 1):
                        halo_copy(s + 1, side, t, 1).start()
                if slots:
                    near_step(s + 1, far_done + LEAD + p)
                    far_step(s + 1, far_done + p)
            each_group(do_all)
            if slots > 1:
                start_rim(s + 1)
            far_done += slots

    for side in (0, 1):
        halo_copy(0, side, 0, tracers).wait_send()
        for s in range(steps):
            rim_copy(s, side).wait_send()
    for s in range(1, steps):
        for t in range(tracers):
            for side in (0, 1):
                halo_copy(s, side, t, 1).wait_send()
    for c in range(chunk_total):
        chain_copy(c, near, near_to).wait_send()

    @pl.when(inner)
    def _():
        for c in range(chunk_total):
            chain_copy(c, far, far_to).wait_send()


def body(dims, tracers, flux_pool, mass_pool, owner, conv_cols, conv_steps, conv_rate):
    _, _, steps, count, levels, cells, lats = dims
    rows = levels * cells
    total = steps * FIELDS
    flat = (count * rows, lats)
    vmem = pl.BlockSpec(memory_space=pltpu.VMEM)
    hbm = pl.BlockSpec(memory_space=pl.ANY)
    f32 = jnp.float32
    out = pl.pallas_call(
        functools.partial(kernel, dims),
        out_shape=jax.ShapeDtypeStruct(flat, f32),
        in_specs=[pl.BlockSpec(memory_space=pltpu.SMEM), vmem, vmem, vmem, hbm, hbm, hbm],
        out_specs=vmem,
        scratch_shapes=[
            pltpu.VMEM((total * rows, lats), f32),
            pltpu.VMEM((2, total * rows, lats), f32),
            pltpu.VMEM((2, total * rows, lats), f32),
            pltpu.VMEM((total * rows, lats), f32),
            pltpu.VMEM(flat, f32),
            pltpu.VMEM(flat, f32),
            pltpu.VMEM((steps, 2, count * HALO * levels, lats), f32),
            pltpu.VMEM((steps, 2, count * HALO * levels, lats), f32),
            pltpu.VMEM((steps, 3 * levels, lats), f32),
            pltpu.VMEM((steps, 3 * levels, lats), f32),
            pltpu.VMEM((3, (cells + 1) * levels, lats), f32),
            pltpu.VMEM((3, rows, lats), f32),
            pltpu.VMEM((3, (levels - 1) * cells, lats), f32),
            pltpu.VMEM((rows, lats), f32),
            pltpu.VMEM((rows, lats), f32),
            pltpu.VMEM((SUBSTEPS * (levels - 1) * cells, lats), f32),
            pltpu.SemaphoreType.DMA((2 * steps,)),
            pltpu.SemaphoreType.DMA,
            pltpu.SemaphoreType.DMA((2, total)),
            pltpu.SemaphoreType.DMA((2, total)),
            pltpu.SemaphoreType.DMA((steps, 2, count)),
            pltpu.SemaphoreType.DMA((steps, 2, count)),
            pltpu.SemaphoreType.DMA((steps, 2)),
            pltpu.SemaphoreType.DMA((steps, 2)),
        ],
        compiler_params=pltpu.CompilerParams(collective_id=0, has_side_effects=True),
    )(
        owner.T, conv_cols, conv_steps, jnp.transpose(conv_rate, (1, 0, 2)), tracers.reshape(flat),
        flux_pool.reshape(steps * 3 * rows, lats), mass_pool.reshape(steps * rows, lats),
    )
    return out.reshape(tracers.shape)


def solution(mesh):
    def local(tracers, flux_pool, *rest):
        dims = (mesh.shape["tile"], mesh.shape["trc"], flux_pool.shape[1]) + tracers.shape
        return body(dims, tracers, flux_pool, *rest)

    in_specs = (
        P("trc", None, "tile", None),
        P("trc", None, None, None, "tile", None),
        P("trc", None, None, "tile", None),
        P(None, "tile"),
        P("tile", None),
        P("tile", None),
        P("tile", None, None),
    )
    out_specs = P("trc", None, "tile", None)
    return jax.shard_map(local, mesh=mesh, in_specs=in_specs, out_specs=out_specs, check_vma=False)
```

```python
import functools

import jax
import jax.numpy as jnp
from jax import lax
from jax.experimental import pallas as pl
from jax.experimental.pallas import tpu as pltpu
from jax.sharding import PartitionSpec as P

FIELDS = 4
HALO = 3
SUBSTEPS = 3
LEAD = 2


def face_terms(flux, left_inverse, right_inverse):
    share = jnp.abs(flux) * jnp.where(flux > 0.0, left_inverse, right_inverse)
    half = 0.5 * flux * share
    bent = half * (3.0 - 2.0 * share)
    return flux - half - bent, half - bent


def edge_rise(before, here, after):
    raw = 0.5 * here + (1.0 / 12.0) * (before - after)
    return jnp.clip(raw, jnp.minimum(here, 0.0), jnp.maximum(here, 0.0))


def limited(up, down):
    up2 = up + up
    down2 = down + down
    right = jnp.clip(up, jnp.minimum(down2, 0.0), jnp.maximum(down2, 0.0))
    left = -jnp.clip(down, jnp.minimum(up2, 0.0), jnp.maximum(up2, 0.0))
    return right, left


def transport(flux, near, far, q0, right0, left0, q1, right1, left1):
    ahead = flux > 0.0
    return (
        flux * jnp.where(ahead, q0, q1)
        + near * jnp.where(ahead, right0, left1)
        + far * jnp.where(ahead, left0, right1)
    )


def kernel(
    dims,
    owner_ref, cols_ref, counts_ref, rate_ref, tracer_hbm, flux_hbm, mass_hbm,
    out_ref,
    own, inbox, relay, met, state, mid, swept, shapes, halo_out, halo_in, rim_out, rim_in,
    cx, cy, cz, inverse_t, inverse_o, lift,
    own_sem, state_sem, chain_send, chain_recv, halo_send, halo_recv, rim_send, rim_recv,
):
    tiles, groups, steps, tracers, levels, cells, lats = dims
    rows = levels * cells
    tile = lax.axis_index("tile")
    me = lax.axis_index("trc")
    right = lax.rem(tile + 1, tiles)
    left = lax.rem(tile + tiles - 1, tiles)
    near = lax.div(2 * me, groups)
    far = 1 - near
    near_to = me + 1 - 2 * near
    far_to = me - 1 + 2 * near
    at_end = jnp.logical_or(me == 0, me == groups - 1)
    inner = jnp.logical_and(me > 0, me < groups - 1)
    chunk_total = steps * FIELDS

    load_state = pltpu.make_async_copy(tracer_hbm, state, state_sem)
    load_state.start()
    loads = []
    for s in range(steps):
        base = s * FIELDS * rows
        loads.append(pltpu.make_async_copy(
            mass_hbm.at[pl.ds(s * rows, rows)], own.at[pl.ds(base, rows)], own_sem.at[2 * s]))
        loads.append(pltpu.make_async_copy(
            flux_hbm.at[pl.ds(s * 3 * rows, 3 * rows)], own.at[pl.ds(base + rows, 3 * rows)],
            own_sem.at[2 * s + 1]))
    for load in loads:
        load.start()

    barrier = pltpu.get_barrier_semaphore()
    for neighbour in (left, right):
        pl.semaphore_signal(barrier, inc=1, device_id={"tile": neighbour}, device_id_type=pl.DeviceIdType.MESH)

    @pl.when(me > 0)
    def _():
        pl.semaphore_signal(barrier, inc=1, device_id={"trc": me - 1}, device_id_type=pl.DeviceIdType.MESH)

    @pl.when(me < groups - 1)
    def _():
        pl.semaphore_signal(barrier, inc=1, device_id={"trc": me + 1}, device_id_type=pl.DeviceIdType.MESH)

    def cell_rows(base, x):
        return pl.ds(base + x, levels, stride=cells)

    def block(i, size):
        return pl.ds(pl.multiple_of(i * size, size), size)

    def pack_halo(s, t, source, base):
        for i in range(HALO):
            at = (t * HALO + i) * levels
            halo_out[s, 0, pl.ds(at, levels), :] = source[cell_rows(base, cells - HALO + i), :]
            halo_out[s, 1, pl.ds(at, levels), :] = source[cell_rows(base, i), :]

    def halo_copy(s, side, t, how_many):
        size = HALO * levels
        at = pl.ds(pl.multiple_of(t * size, size), how_many * size)
        return pltpu.make_async_remote_copy(
            src_ref=halo_out.at[s, side, at], dst_ref=halo_in.at[s, side, at],
            send_sem=halo_send.at[s, side, t], recv_sem=halo_recv.at[s, side, t],
            device_id={"tile": left if side else right}, device_id_type=pl.DeviceIdType.MESH)

    load_state.wait()
    for t in range(tracers):
        pack_halo(0, t, state, t * rows)

    expected = 2 + jnp.where(me > 0, 1, 0) + jnp.where(me < groups - 1, 1, 0)
    pl.semaphore_wait(barrier, expected)

    def raw(c):
        s, field = divmod(c, FIELDS)
        if field == 0:
            return mass_hbm.at[pl.ds(s * rows, rows)]
        return flux_hbm.at[pl.ds((s * 3 + field - 1) * rows, rows)]

    def chunk(c):
        return pl.ds(c * rows, rows) if isinstance(c, int) else block(c, rows)

    def chain_copy(c, way, to, source=None):
        at = chunk(c)
        return pltpu.make_async_remote_copy(
            src_ref=relay.at[way, at] if source is None else source, dst_ref=inbox.at[way, at],
            send_sem=chain_send.at[way, c], recv_sem=chain_recv.at[way, c],
            device_id={"trc": to}, device_id_type=pl.DeviceIdType.MESH)

    @pl.when(at_end)
    def _():
        for c in range(chunk_total):
            chain_copy(c, near, near_to, raw(c)).start()

    for side in (0, 1):
        halo_copy(0, side, 0, tracers).start()

    cols = cols_ref[...]
    x_start = jnp.zeros_like(cols)
    for x in range(1, cells):
        x_start += jnp.where(cols >= x * lats, lats, 0)
    listed = cols.shape[1]
    at_x = x_start == lax.broadcasted_iota(jnp.int32, (cells, listed), 0) * lats
    at_y = ((cols - x_start) == lax.broadcasted_iota(jnp.int32, (lats, listed), 0)).astype(jnp.float32)
    spread = [jnp.where(at_x, counts_ref[...].astype(jnp.float32), 0.0)]
    for k in range(levels - 1):
        spread.append(jnp.where(at_x, rate_ref[k], 0.0))
    dense = lax.dot_general(
        jnp.concatenate(spread, axis=0), at_y, (((1,), (1,)), ((), ())),
        precision=lax.Precision.HIGHEST, preferred_element_type=jnp.float32)
    count = dense[:cells]
    for n in range(SUBSTEPS):
        for k in range(levels - 1):
            lift[pl.ds((n * (levels - 1) + k) * cells, cells), :] = jnp.where(
                count > n + 0.5, dense[(k + 1) * cells:(k + 2) * cells], 0.0)

    for load in loads:
        load.wait()

    def owner_of(s):
        return jnp.full((rows, lats), owner_ref[0, s], jnp.int32)

    def pass_on(s, c, way, to):
        at = chunk(c)
        relay[way, at, :] = jnp.where(owner_of(s) == me, own[at, :], inbox[way, at, :])
        chain_copy(c, way, to).start()

    def near_step(s, c):
        @pl.when(inner)
        def _():
            chain_copy(c, near, near_to).wait_recv()
            pass_on(s, c, near, near_to)

    def far_arrives(s, c):
        chain_copy(c, far, near_to).wait_recv()

        @pl.when(inner)
        def _():
            pass_on(s, c, far, far_to)

    def choose(s, c):
        at = chunk(c)
        holder = owner_of(s)
        met[at, :] = jnp.where(
            holder == me, own[at, :], jnp.where(holder < me, inbox[0, at, :], inbox[1, at, :]))

    def far_step(s, c):
        far_arrives(s, c)
        choose(s, c)

    def rim_copy(s, side):
        at = pl.ds(0, 2 * levels) if side == 0 else pl.ds(2 * levels, levels)
        return pltpu.make_async_remote_copy(
            src_ref=rim_out.at[s, at], dst_ref=rim_in.at[s, at],
            send_sem=rim_send.at[s, side], recv_sem=rim_recv.at[s, side],
            device_id={"tile": left if side else right}, device_id_type=pl.DeviceIdType.MESH)

    def start_rim(s):
        mass_at = s * FIELDS * rows
        rim_out[s, pl.ds(0, levels), :] = met[cell_rows(mass_at + rows, cells - 1), :]
        rim_out[s, pl.ds(levels, levels), :] = met[cell_rows(mass_at, cells - 1), :]
        rim_out[s, pl.ds(2 * levels, levels), :] = met[cell_rows(mass_at, 0), :]
        rim_copy(s, 0).start()
        rim_copy(s, 1).start()

    def mass_terms(s):
        mass_at = s * FIELDS * rows
        for k in range(levels):
            at = pl.ds(k * cells, cells)
            inverse_o[at, :] = 1.0 / met[pl.ds(mass_at + k * cells, cells), :]
        for x in range(cells):
            inverse_t[pl.ds(x * levels, levels), :] = inverse_o[cell_rows(0, x), :]

    def x_terms(s):
        mass_at = s * FIELDS * rows
        inverses = [1.0 / rim_in[s, pl.ds(levels, levels), :]]
        fluxes = [rim_in[s, pl.ds(0, levels), :]]
        for x in range(cells):
            inverses.append(inverse_t[pl.ds(x * levels, levels), :])
            fluxes.append(met[cell_rows(mass_at + rows, x), :])
        inverses.append(1.0 / rim_in[s, pl.ds(2 * levels, levels), :])
        for x in range(cells + 1):
            at = pl.ds(x * levels, levels)
            cx[0, at, :] = fluxes[x]
            cx[1, at, :], cx[2, at, :] = face_terms(fluxes[x], inverses[x], inverses[x + 1])

    def y_terms(s):
        flux_at = (s * FIELDS + 2) * rows
        open_face = lax.broadcasted_iota(jnp.int32, (levels, lats), 1) < lats - 1
        for x in range(cells):
            at = pl.ds(x * levels, levels)
            flux = jnp.where(open_face, met[cell_rows(flux_at, x), :], 0.0)
            inverse = inverse_t[at, :]
            cy[0, at, :] = flux
            cy[1, at, :], cy[2, at, :] = face_terms(flux, inverse, pltpu.roll(inverse, lats - 1, 1))

    def z_terms(s):
        flux_at = (s * FIELDS + 3) * rows
        for k in range(levels - 1):
            at = pl.ds(k * cells, cells)
            flux = met[pl.ds(flux_at + k * cells, cells), :]
            cz[0, at, :] = flux
            cz[1, at, :], cz[2, at, :] = face_terms(
                flux, inverse_o[at, :], inverse_o[pl.ds((k + 1) * cells, cells), :])

    def padded_x(s, t):
        base = pl.multiple_of(t * rows, rows)
        q = [halo_in[s, 0, block(t * HALO + i, levels), :] for i in range(HALO)]
        q += [state[cell_rows(base, x), :] for x in range(cells)]
        return q + [halo_in[s, 1, block(t * HALO + i, levels), :] for i in range(HALO)]

    def shape_x(s, t):
        q = padded_x(s, t)
        rise = [q[i + 1] - q[i] for i in range(cells + 5)]
        up = [edge_rise(rise[i], rise[i + 1], rise[i + 2]) for i in range(cells + 3)]
        for i in range(cells + 2):
            at = block(t * (cells + 2) + i, levels)
            shapes[0, at, :], shapes[1, at, :] = limited(up[i + 1], rise[i + 1] - up[i])

    def sweep_x(s, t):
        q = padded_x(s, t)
        shape = []
        for i in range(cells + 2):
            at = block(t * (cells + 2) + i, levels)
            shape.append((shapes[0, at, :], shapes[1, at, :]))
        moved = []
        for j in range(cells + 1):
            at = pl.ds(j * levels, levels)
            moved.append(transport(
                cx[0, at, :], cx[1, at, :], cx[2, at, :],
                q[j + 2], *shape[j], q[j + 3], *shape[j + 1]))
        for x in range(cells):
            mid[block(t * cells + x, levels), :] = (
                q[x + 3] - (moved[x + 1] - moved[x]) * inverse_t[pl.ds(x * levels, levels), :])

    def sweep_y(x, q):
        at = pl.ds(x * levels, levels)
        inside = lax.broadcasted_iota(jnp.int32, (levels, lats), 1) < lats - 1

        def ahead(v):
            return pltpu.roll(v, lats - 1, 1)

        def behind(v):
            return pltpu.roll(v, 1, 1)

        q1 = ahead(q)
        rise = jnp.where(inside, q1 - q, 0.0)
        up = edge_rise(behind(rise), rise, ahead(rise))
        r, l = limited(up, behind(rise - up))
        moved = transport(cy[0, at, :], cy[1, at, :], cy[2, at, :], q, r, l, q1, ahead(r), ahead(l))
        return q - (moved - behind(moved)) * inverse_t[at, :]

    def sweep_ys(some):
        for x in range(cells):
            for t in some:
                swept[cell_rows(pl.multiple_of(t * rows, rows), x), :] = sweep_y(
                    x, mid[block(t * cells + x, levels), :])

    def sweep_z(s, t):
        base = pl.multiple_of(t * rows, rows)
        q = [swept[pl.ds(base + k * cells, cells), :] for k in range(levels)]
        zero = jnp.zeros_like(q[0])
        rise = [zero] + [q[k + 1] - q[k] for k in range(levels - 1)] + [zero]
        up = [zero] + [edge_rise(rise[k], rise[k + 1], rise[k + 2]) for k in range(levels - 1)]
        shape = [(zero, zero)]
        for k in range(1, levels - 1):
            shape.append(limited(up[k + 1], rise[k] - up[k]))
        shape.append((zero, zero))
        moved = [zero]
        for k in range(levels - 1):
            at = pl.ds(k * cells, cells)
            moved.append(transport(
                cz[0, at, :], cz[1, at, :], cz[2, at, :], q[k], *shape[k], q[k + 1], *shape[k + 1]))
        moved.append(zero)
        q = [
            q[k] - (moved[k + 1] - moved[k]) * inverse_o[pl.ds(k * cells, cells), :]
            for k in range(levels)
        ]
        for n in range(SUBSTEPS):
            gain = [
                lift[pl.ds((n * (levels - 1) + k) * cells, cells), :] * q[k] for k in range(levels - 1)
            ]
            q = [
                (q[k] + gain[k - 1] if k else q[k]) - (gain[k] if k < levels - 1 else 0.0)
                for k in range(levels)
            ]
        target = out_ref if s == steps - 1 else state
        for k in range(levels):
            target[pl.ds(base + k * cells, cells), :] = q[k]

    together = 2 if tracers % 2 == 0 else 1
    loops = tracers // together

    def each_group(body):
        def run(p, carry):
            body(p, [p * together + i for i in range(together)])
            return carry
        lax.fori_loop(0, loops, run, 0)

    def halo_arrives(s, some):
        for t in some:
            for side in (0, 1):
                halo_copy(s, side, t, 1).wait_recv()

    def rim_arrives(s):
        for side in (0, 1):
            rim_copy(s, side).wait_recv()

    def near_if(c):
        if c < chunk_total:
            near_step(c // FIELDS, c)

    def shape_xs(s):
        each_group(lambda p, some: [shape_x(s, t) for t in some])

    def sweep_xs(s):
        each_group(lambda p, some: [sweep_x(s, t) for t in some])

    def sweep_zs(s):
        def run(p, some):
            for t in some:
                sweep_z(s, t)
            if s < steps - 1:
                for t in some:
                    pack_halo(s + 1, t, state, pl.multiple_of(t * rows, rows))
                    for side in (0, 1):
                        halo_copy(s + 1, side, t, 1).start()
        each_group(run)

    def link(c):
        s, field = divmod(c, FIELDS)
        near_if(c + LEAD)
        far_step(s, c)
        if field == 0 and s == 0:
            mass_terms(s)
        if field == 1:
            start_rim(s)

    def links(start, stop):
        for c in range(start, min(stop, chunk_total)):
            link(c)

    for side in (0, 1):
        halo_copy(0, side, 0, tracers).wait_recv()
    near_if(0)
    shape_xs(0)
    for c in range(1, LEAD):
        near_if(c)
    links(0, FIELDS - (steps == 1))
    for s in range(steps):
        follow = (s + 1) * FIELDS
        last = chunk_total - 1
        final = s == steps - 1
        if s > 0:
            links(follow - 2, follow - final)
            mass_terms(s)
        if final:
            @pl.when(inner)
            def _():
                far_arrives(s, last)
        if s > 0:
            each_group(lambda p, some: halo_arrives(s, some))
            shape_xs(s)
        rim_arrives(s)
        x_terms(s)
        sweep_xs(s)
        y_terms(s)
        each_group(lambda p, some: sweep_ys(some))
        if final:
            @pl.when(at_end)
            def _():
                far_arrives(s, last)

            choose(s, last)
        else:
            links(follow, follow + 1)
        z_terms(s)
        sweep_zs(s)
        if not final:
            links(follow + 1, follow + 2)

    for side in (0, 1):
        halo_copy(0, side, 0, tracers).wait_send()
        for s in range(steps):
            rim_copy(s, side).wait_send()
    for s in range(1, steps):
        for t in range(tracers):
            for side in (0, 1):
                halo_copy(s, side, t, 1).wait_send()
    for c in range(chunk_total):
        chain_copy(c, near, near_to).wait_send()

    @pl.when(inner)
    def _():
        for c in range(chunk_total):
            chain_copy(c, far, far_to).wait_send()


def body(dims, tracers, flux_pool, mass_pool, owner, conv_cols, conv_steps, conv_rate):
    _, _, steps, count, levels, cells, lats = dims
    rows = levels * cells
    total = steps * FIELDS
    flat = (count * rows, lats)
    vmem = pl.BlockSpec(memory_space=pltpu.VMEM)
    hbm = pl.BlockSpec(memory_space=pl.ANY)
    f32 = jnp.float32
    out = pl.pallas_call(
        functools.partial(kernel, dims),
        out_shape=jax.ShapeDtypeStruct(flat, f32),
        in_specs=[pl.BlockSpec(memory_space=pltpu.SMEM), vmem, vmem, vmem, hbm, hbm, hbm],
        out_specs=vmem,
        scratch_shapes=[
            pltpu.VMEM((total * rows, lats), f32),
            pltpu.VMEM((2, total * rows, lats), f32),
            pltpu.VMEM((2, total * rows, lats), f32),
            pltpu.VMEM((total * rows, lats), f32),
            pltpu.VMEM(flat, f32),
            pltpu.VMEM(flat, f32),
            pltpu.VMEM(flat, f32),
            pltpu.VMEM((2, count * (cells + 2) * levels, lats), f32),
            pltpu.VMEM((steps, 2, count * HALO * levels, lats), f32),
            pltpu.VMEM((steps, 2, count * HALO * levels, lats), f32),
            pltpu.VMEM((steps, 3 * levels, lats), f32),
            pltpu.VMEM((steps, 3 * levels, lats), f32),
            pltpu.VMEM((3, (cells + 1) * levels, lats), f32),
            pltpu.VMEM((3, rows, lats), f32),
            pltpu.VMEM((3, (levels - 1) * cells, lats), f32),
            pltpu.VMEM((rows, lats), f32),
            pltpu.VMEM((rows, lats), f32),
            pltpu.VMEM((SUBSTEPS * (levels - 1) * cells, lats), f32),
            pltpu.SemaphoreType.DMA((2 * steps,)),
            pltpu.SemaphoreType.DMA,
            pltpu.SemaphoreType.DMA((2, total)),
            pltpu.SemaphoreType.DMA((2, total)),
            pltpu.SemaphoreType.DMA((steps, 2, count)),
            pltpu.SemaphoreType.DMA((steps, 2, count)),
            pltpu.SemaphoreType.DMA((steps, 2)),
            pltpu.SemaphoreType.DMA((steps, 2)),
        ],
        compiler_params=pltpu.CompilerParams(collective_id=0, has_side_effects=True),
    )(
        owner.T, conv_cols, conv_steps, jnp.transpose(conv_rate, (1, 0, 2)), tracers.reshape(flat),
        flux_pool.reshape(steps * 3 * rows, lats), mass_pool.reshape(steps * rows, lats),
    )
    return out.reshape(tracers.shape)


def solution(mesh):
    def local(tracers, flux_pool, *rest):
        dims = (mesh.shape["tile"], mesh.shape["trc"], flux_pool.shape[1]) + tracers.shape
        return body(dims, tracers, flux_pool, *rest)

    in_specs = (
        P("trc", None, "tile", None),
        P("trc", None, None, None, "tile", None),
        P("trc", None, None, "tile", None),
        P(None, "tile"),
        P("tile", None),
        P("tile", None),
        P("tile", None, None),
    )
    out_specs = P("trc", None, "tile", None)
    return jax.shard_map(local, mesh=mesh, in_specs=in_specs, out_specs=out_specs, check_vma=False)
```

```python
import functools

import jax
import jax.numpy as jnp
from jax import lax
from jax.experimental import pallas as pl
from jax.experimental.pallas import tpu as pltpu
from jax.sharding import PartitionSpec as P

FIELDS = 4
HALO = 3
SUBSTEPS = 3
WINDOW = 2
LEAD = 2


def face_terms(flux, left_inverse, right_inverse):
    share = jnp.abs(flux) * jnp.where(flux > 0.0, left_inverse, right_inverse)
    half = 0.5 * flux * share
    bent = half * (3.0 - 2.0 * share)
    return flux - half - bent, half - bent


def edge_rise(before, here, after):
    raw = 0.5 * here + (1.0 / 12.0) * (before - after)
    return jnp.clip(raw, jnp.minimum(here, 0.0), jnp.maximum(here, 0.0))


def limited(up, down):
    up2 = up + up
    down2 = down + down
    right = jnp.clip(up, jnp.minimum(down2, 0.0), jnp.maximum(down2, 0.0))
    left = -jnp.clip(down, jnp.minimum(up2, 0.0), jnp.maximum(up2, 0.0))
    return right, left


def transport(flux, near, far, q0, right0, left0, q1, right1, left1):
    ahead = flux > 0.0
    return (
        flux * jnp.where(ahead, q0, q1)
        + near * jnp.where(ahead, right0, left1)
        + far * jnp.where(ahead, left0, right1)
    )


def kernel(
    dims,
    owner_hbm, cols_hbm, counts_hbm, rate_hbm, tracer_hbm, flux_hbm, mass_hbm,
    out_hbm,
    owner_ref, cols_ref, counts_ref, rate_ref, out_ref,
    own, inbox, relay, met, state, mid, swept, shapes, halo_out, halo_in, rim_out, rim_in,
    cx, cy, cz, inverse_t, inverse_o, lift,
    own_sem, state_sem, small_sem, out_sem, chain_send, chain_recv, halo_send, halo_recv, rim_send, rim_recv,
):
    tiles, groups, steps, tracers, levels, cells, lats = dims
    rows = levels * cells
    tile = lax.axis_index("tile")
    me = lax.axis_index("trc")
    right = lax.rem(tile + 1, tiles)
    left = lax.rem(tile + tiles - 1, tiles)
    near = lax.div(2 * me, groups)
    far = 1 - near
    near_to = me + 1 - 2 * near
    far_to = me - 1 + 2 * near
    at_end = jnp.logical_or(me == 0, me == groups - 1)
    inner = jnp.logical_and(me > 0, me < groups - 1)
    chunk_total = steps * FIELDS

    load_state = pltpu.make_async_copy(tracer_hbm, state, state_sem)
    load_state.start()
    loads = []
    for s in range(steps):
        base = s * FIELDS * rows
        loads.append(pltpu.make_async_copy(
            mass_hbm.at[pl.ds(s * rows, rows)], own.at[pl.ds(base, rows)], own_sem.at[2 * s]))
        loads.append(pltpu.make_async_copy(
            flux_hbm.at[pl.ds(s * 3 * rows, 3 * rows)], own.at[pl.ds(base + rows, 3 * rows)],
            own_sem.at[2 * s + 1]))
    for load in loads:
        load.start()
    smalls = [
        pltpu.make_async_copy(source, target, small_sem.at[i])
        for i, (source, target) in enumerate((
            (owner_hbm, owner_ref), (cols_hbm, cols_ref), (counts_hbm, counts_ref), (rate_hbm, rate_ref)))
    ]
    for small in smalls:
        small.start()

    barrier = pltpu.get_barrier_semaphore()
    for neighbour in (left, right):
        pl.semaphore_signal(barrier, inc=1, device_id={"tile": neighbour}, device_id_type=pl.DeviceIdType.MESH)

    @pl.when(me > 0)
    def _():
        pl.semaphore_signal(barrier, inc=1, device_id={"trc": me - 1}, device_id_type=pl.DeviceIdType.MESH)

    @pl.when(me < groups - 1)
    def _():
        pl.semaphore_signal(barrier, inc=1, device_id={"trc": me + 1}, device_id_type=pl.DeviceIdType.MESH)

    def cell_rows(base, x):
        return pl.ds(base + x, levels, stride=cells)

    def block(i, size):
        return pl.ds(pl.multiple_of(i * size, size), size)

    def pack_halo(s, t, source, base):
        for i in range(HALO):
            at = (t * HALO + i) * levels
            halo_out[s, 0, pl.ds(at, levels), :] = source[cell_rows(base, cells - HALO + i), :]
            halo_out[s, 1, pl.ds(at, levels), :] = source[cell_rows(base, i), :]

    def halo_copy(s, side, t, how_many):
        size = HALO * levels
        at = pl.ds(pl.multiple_of(t * size, size), how_many * size)
        return pltpu.make_async_remote_copy(
            src_ref=halo_out.at[s, side, at], dst_ref=halo_in.at[s, side, at],
            send_sem=halo_send.at[s, side, t], recv_sem=halo_recv.at[s, side, t],
            device_id={"tile": left if side else right}, device_id_type=pl.DeviceIdType.MESH)

    load_state.wait()
    for t in range(tracers):
        pack_halo(0, t, state, t * rows)

    expected = 2 + jnp.where(me > 0, 1, 0) + jnp.where(me < groups - 1, 1, 0)
    pl.semaphore_wait(barrier, expected)

    def raw(c):
        s, field = divmod(c, FIELDS)
        if field == 0:
            return mass_hbm.at[pl.ds(s * rows, rows)]
        return flux_hbm.at[pl.ds((s * 3 + field - 1) * rows, rows)]

    def chunk(c):
        return pl.ds(c * rows, rows) if isinstance(c, int) else block(c, rows)

    def chain_copy(c, way, to, source=None):
        at = chunk(c)
        return pltpu.make_async_remote_copy(
            src_ref=relay.at[way, at] if source is None else source, dst_ref=inbox.at[way, at],
            send_sem=chain_send.at[way, c], recv_sem=chain_recv.at[way, c],
            device_id={"trc": to}, device_id_type=pl.DeviceIdType.MESH)

    def pump(start, stop):
        @pl.when(at_end)
        def _():
            for c in range(start, stop):
                if c >= WINDOW:
                    chain_copy(c - WINDOW, near, near_to, raw(c - WINDOW)).wait_send()
                chain_copy(c, near, near_to, raw(c)).start()

    pump(0, min(WINDOW, chunk_total))

    for side in (0, 1):
        halo_copy(0, side, 0, tracers).start()

    for small in smalls:
        small.wait()
    cols = cols_ref[...]
    x_start = jnp.zeros_like(cols)
    for x in range(1, cells):
        x_start += jnp.where(cols >= x * lats, lats, 0)
    listed = cols.shape[1]
    at_x = x_start == lax.broadcasted_iota(jnp.int32, (cells, listed), 0) * lats
    at_y = ((cols - x_start) == lax.broadcasted_iota(jnp.int32, (lats, listed), 0)).astype(jnp.float32)
    spread = [jnp.where(at_x, counts_ref[...].astype(jnp.float32), 0.0)]
    for k in range(levels - 1):
        spread.append(jnp.where(at_x, rate_ref[k], 0.0))
    dense = lax.dot_general(
        jnp.concatenate(spread, axis=0), at_y, (((1,), (1,)), ((), ())),
        precision=lax.Precision.HIGHEST, preferred_element_type=jnp.float32)
    count = dense[:cells]
    for n in range(SUBSTEPS):
        for k in range(levels - 1):
            lift[pl.ds((n * (levels - 1) + k) * cells, cells), :] = jnp.where(
                count > n + 0.5, dense[(k + 1) * cells:(k + 2) * cells], 0.0)

    for load in loads:
        load.wait()

    def owner_of(s):
        return jnp.full((rows, lats), owner_ref[0, s], jnp.int32)

    def pass_on(s, c, way, to):
        at = chunk(c)
        relay[way, at, :] = jnp.where(owner_of(s) == me, own[at, :], inbox[way, at, :])
        chain_copy(c, way, to).start()

    def near_step(s, c):
        @pl.when(inner)
        def _():
            chain_copy(c, near, near_to).wait_recv()
            pass_on(s, c, near, near_to)

    def far_arrives(s, c):
        chain_copy(c, far, near_to).wait_recv()

        @pl.when(inner)
        def _():
            pass_on(s, c, far, far_to)

    def choose(s, c):
        at = chunk(c)
        holder = owner_of(s)
        met[at, :] = jnp.where(
            holder == me, own[at, :], jnp.where(holder < me, inbox[0, at, :], inbox[1, at, :]))

    def far_step(s, c):
        far_arrives(s, c)
        choose(s, c)

    def rim_copy(s, side):
        at = pl.ds(0, 2 * levels) if side == 0 else pl.ds(2 * levels, levels)
        return pltpu.make_async_remote_copy(
            src_ref=rim_out.at[s, at], dst_ref=rim_in.at[s, at],
            send_sem=rim_send.at[s, side], recv_sem=rim_recv.at[s, side],
            device_id={"tile": left if side else right}, device_id_type=pl.DeviceIdType.MESH)

    def start_rim(s):
        mass_at = s * FIELDS * rows
        rim_out[s, pl.ds(0, levels), :] = met[cell_rows(mass_at + rows, cells - 1), :]
        rim_out[s, pl.ds(levels, levels), :] = met[cell_rows(mass_at, cells - 1), :]
        rim_out[s, pl.ds(2 * levels, levels), :] = met[cell_rows(mass_at, 0), :]
        rim_copy(s, 0).start()
        rim_copy(s, 1).start()

    def mass_terms(s):
        mass_at = s * FIELDS * rows
        for k in range(levels):
            at = pl.ds(k * cells, cells)
            inverse_o[at, :] = 1.0 / met[pl.ds(mass_at + k * cells, cells), :]
        for x in range(cells):
            inverse_t[pl.ds(x * levels, levels), :] = inverse_o[cell_rows(0, x), :]

    def x_terms(s):
        mass_at = s * FIELDS * rows
        inverses = [1.0 / rim_in[s, pl.ds(levels, levels), :]]
        fluxes = [rim_in[s, pl.ds(0, levels), :]]
        for x in range(cells):
            inverses.append(inverse_t[pl.ds(x * levels, levels), :])
            fluxes.append(met[cell_rows(mass_at + rows, x), :])
        inverses.append(1.0 / rim_in[s, pl.ds(2 * levels, levels), :])
        for x in range(cells + 1):
            at = pl.ds(x * levels, levels)
            cx[0, at, :] = fluxes[x]
            cx[1, at, :], cx[2, at, :] = face_terms(fluxes[x], inverses[x], inverses[x + 1])

    def y_terms(s):
        flux_at = (s * FIELDS + 2) * rows
        open_face = lax.broadcasted_iota(jnp.int32, (levels, lats), 1) < lats - 1
        for x in range(cells):
            at = pl.ds(x * levels, levels)
            flux = jnp.where(open_face, met[cell_rows(flux_at, x), :], 0.0)
            inverse = inverse_t[at, :]
            cy[0, at, :] = flux
            cy[1, at, :], cy[2, at, :] = face_terms(flux, inverse, pltpu.roll(inverse, lats - 1, 1))

    def z_terms(s):
        flux_at = (s * FIELDS + 3) * rows
        for k in range(levels - 1):
            at = pl.ds(k * cells, cells)
            flux = met[pl.ds(flux_at + k * cells, cells), :]
            cz[0, at, :] = flux
            cz[1, at, :], cz[2, at, :] = face_terms(
                flux, inverse_o[at, :], inverse_o[pl.ds((k + 1) * cells, cells), :])

    def padded_x(s, t):
        base = pl.multiple_of(t * rows, rows)
        q = [halo_in[s, 0, block(t * HALO + i, levels), :] for i in range(HALO)]
        q += [state[cell_rows(base, x), :] for x in range(cells)]
        return q + [halo_in[s, 1, block(t * HALO + i, levels), :] for i in range(HALO)]

    def shape_x(s, t):
        q = padded_x(s, t)
        rise = [q[i + 1] - q[i] for i in range(cells + 5)]
        up = [edge_rise(rise[i], rise[i + 1], rise[i + 2]) for i in range(cells + 3)]
        for i in range(cells + 2):
            at = block(t * (cells + 2) + i, levels)
            shapes[0, at, :], shapes[1, at, :] = limited(up[i + 1], rise[i + 1] - up[i])

    def sweep_x(s, t):
        q = padded_x(s, t)
        shape = []
        for i in range(cells + 2):
            at = block(t * (cells + 2) + i, levels)
            shape.append((shapes[0, at, :], shapes[1, at, :]))
        moved = []
        for j in range(cells + 1):
            at = pl.ds(j * levels, levels)
            moved.append(transport(
                cx[0, at, :], cx[1, at, :], cx[2, at, :],
                q[j + 2], *shape[j], q[j + 3], *shape[j + 1]))
        for x in range(cells):
            mid[block(t * cells + x, levels), :] = (
                q[x + 3] - (moved[x + 1] - moved[x]) * inverse_t[pl.ds(x * levels, levels), :])

    def sweep_y(x, q):
        at = pl.ds(x * levels, levels)
        inside = lax.broadcasted_iota(jnp.int32, (levels, lats), 1) < lats - 1

        def ahead(v):
            return pltpu.roll(v, lats - 1, 1)

        def behind(v):
            return pltpu.roll(v, 1, 1)

        q1 = ahead(q)
        rise = jnp.where(inside, q1 - q, 0.0)
        up = edge_rise(behind(rise), rise, ahead(rise))
        r, l = limited(up, behind(rise - up))
        moved = transport(cy[0, at, :], cy[1, at, :], cy[2, at, :], q, r, l, q1, ahead(r), ahead(l))
        return q - (moved - behind(moved)) * inverse_t[at, :]

    def sweep_ys(some):
        for x in range(cells):
            for t in some:
                swept[cell_rows(pl.multiple_of(t * rows, rows), x), :] = sweep_y(
                    x, mid[block(t * cells + x, levels), :])

    def sweep_z(s, t):
        base = pl.multiple_of(t * rows, rows)
        q = [swept[pl.ds(base + k * cells, cells), :] for k in range(levels)]
        zero = jnp.zeros_like(q[0])
        rise = [zero] + [q[k + 1] - q[k] for k in range(levels - 1)] + [zero]
        up = [zero] + [edge_rise(rise[k], rise[k + 1], rise[k + 2]) for k in range(levels - 1)]
        shape = [(zero, zero)]
        for k in range(1, levels - 1):
            shape.append(limited(up[k + 1], rise[k] - up[k]))
        shape.append((zero, zero))
        moved = [zero]
        for k in range(levels - 1):
            at = pl.ds(k * cells, cells)
            moved.append(transport(
                cz[0, at, :], cz[1, at, :], cz[2, at, :], q[k], *shape[k], q[k + 1], *shape[k + 1]))
        moved.append(zero)
        q = [
            q[k] - (moved[k + 1] - moved[k]) * inverse_o[pl.ds(k * cells, cells), :]
            for k in range(levels)
        ]
        for n in range(SUBSTEPS):
            gain = [
                lift[pl.ds((n * (levels - 1) + k) * cells, cells), :] * q[k] for k in range(levels - 1)
            ]
            q = [
                (q[k] + gain[k - 1] if k else q[k]) - (gain[k] if k < levels - 1 else 0.0)
                for k in range(levels)
            ]
        target = out_ref if s == steps - 1 else state
        for k in range(levels):
            target[pl.ds(base + k * cells, cells), :] = q[k]

    together = 2 if tracers % 2 == 0 else 1
    loops = tracers // together

    def each_group(body):
        def run(p, carry):
            body(p, [p * together + i for i in range(together)])
            return carry
        lax.fori_loop(0, loops, run, 0)

    def halo_arrives(s, some):
        for t in some:
            for side in (0, 1):
                halo_copy(s, side, t, 1).wait_recv()

    def rim_arrives(s):
        for side in (0, 1):
            rim_copy(s, side).wait_recv()

    def near_if(c):
        if c < chunk_total:
            near_step(c // FIELDS, c)

    def shape_xs(s):
        each_group(lambda p, some: [shape_x(s, t) for t in some])

    def sweep_xs(s):
        each_group(lambda p, some: [sweep_x(s, t) for t in some])

    def out_copy(t):
        at = block(t, rows)
        return pltpu.make_async_copy(out_ref.at[at], out_hbm.at[at], out_sem.at[t])

    def sweep_zs(s):
        def run(p, some):
            for t in some:
                sweep_z(s, t)
            if s == steps - 1:
                for t in some:
                    out_copy(t).start()
            else:
                for t in some:
                    pack_halo(s + 1, t, state, pl.multiple_of(t * rows, rows))
                    for side in (0, 1):
                        halo_copy(s + 1, side, t, 1).start()
        each_group(run)

    def link(c):
        s, field = divmod(c, FIELDS)
        near_if(c + LEAD)
        far_step(s, c)
        if field == 0 and s == 0:
            mass_terms(s)
        if field == 1:
            start_rim(s)

    def links(start, stop):
        for c in range(start, min(stop, chunk_total)):
            link(c)

    for side in (0, 1):
        halo_copy(0, side, 0, tracers).wait_recv()
    near_if(0)
    pump(WINDOW, min(WINDOW + 2, chunk_total))
    shape_xs(0)
    pump(WINDOW + 2, chunk_total)
    for c in range(1, LEAD):
        near_if(c)
    links(0, FIELDS - (steps == 1))
    for s in range(steps):
        follow = (s + 1) * FIELDS
        last = chunk_total - 1
        final = s == steps - 1
        if s > 0:
            links(follow - 2, follow - final)
            mass_terms(s)
        if final:
            @pl.when(inner)
            def _():
                far_arrives(s, last)
        if s > 0:
            each_group(lambda p, some: halo_arrives(s, some))
            shape_xs(s)
        rim_arrives(s)
        x_terms(s)
        sweep_xs(s)
        y_terms(s)
        each_group(lambda p, some: sweep_ys(some))
        if final:
            @pl.when(at_end)
            def _():
                far_arrives(s, last)

            choose(s, last)
        else:
            links(follow, follow + 1)
        z_terms(s)
        sweep_zs(s)
        if not final:
            links(follow + 1, follow + 2)

    for side in (0, 1):
        halo_copy(0, side, 0, tracers).wait_send()
        for s in range(steps):
            rim_copy(s, side).wait_send()
    for s in range(1, steps):
        for t in range(tracers):
            for side in (0, 1):
                halo_copy(s, side, t, 1).wait_send()
    for c in range(max(chunk_total - WINDOW, 0), chunk_total):
        chain_copy(c, near, near_to).wait_send()

    @pl.when(inner)
    def _():
        for c in range(chunk_total):
            if c < chunk_total - WINDOW:
                chain_copy(c, near, near_to).wait_send()
            chain_copy(c, far, far_to).wait_send()

    for t in range(tracers):
        out_copy(t).wait()


def body(dims, tracers, flux_pool, mass_pool, owner, conv_cols, conv_steps, conv_rate):
    _, _, steps, count, levels, cells, lats = dims
    rows = levels * cells
    total = steps * FIELDS
    flat = (count * rows, lats)
    hbm = pl.BlockSpec(memory_space=pl.ANY)
    f32 = jnp.float32
    out = pl.pallas_call(
        functools.partial(kernel, dims),
        out_shape=jax.ShapeDtypeStruct(flat, f32),
        in_specs=[hbm] * 7,
        out_specs=hbm,
        scratch_shapes=[
            pltpu.SMEM((1, steps), jnp.int32),
            pltpu.VMEM(conv_cols.shape, jnp.int32),
            pltpu.VMEM(conv_steps.shape, jnp.int32),
            pltpu.VMEM((levels - 1, 1, conv_cols.shape[1]), f32),
            pltpu.VMEM(flat, f32),
            pltpu.VMEM((total * rows, lats), f32),
            pltpu.VMEM((2, total * rows, lats), f32),
            pltpu.VMEM((2, total * rows, lats), f32),
            pltpu.VMEM((total * rows, lats), f32),
            pltpu.VMEM(flat, f32),
            pltpu.VMEM(flat, f32),
            pltpu.VMEM(flat, f32),
            pltpu.VMEM((2, count * (cells + 2) * levels, lats), f32),
            pltpu.VMEM((steps, 2, count * HALO * levels, lats), f32),
            pltpu.VMEM((steps, 2, count * HALO * levels, lats), f32),
            pltpu.VMEM((steps, 3 * levels, lats), f32),
            pltpu.VMEM((steps, 3 * levels, lats), f32),
            pltpu.VMEM((3, (cells + 1) * levels, lats), f32),
            pltpu.VMEM((3, rows, lats), f32),
            pltpu.VMEM((3, (levels - 1) * cells, lats), f32),
            pltpu.VMEM((rows, lats), f32),
            pltpu.VMEM((rows, lats), f32),
            pltpu.VMEM((SUBSTEPS * (levels - 1) * cells, lats), f32),
            pltpu.SemaphoreType.DMA((2 * steps,)),
            pltpu.SemaphoreType.DMA,
            pltpu.SemaphoreType.DMA((4,)),
            pltpu.SemaphoreType.DMA((count,)),
            pltpu.SemaphoreType.DMA((2, total)),
            pltpu.SemaphoreType.DMA((2, total)),
            pltpu.SemaphoreType.DMA((steps, 2, count)),
            pltpu.SemaphoreType.DMA((steps, 2, count)),
            pltpu.SemaphoreType.DMA((steps, 2)),
            pltpu.SemaphoreType.DMA((steps, 2)),
        ],
        compiler_params=pltpu.CompilerParams(collective_id=0, has_side_effects=True),
    )(
        owner.T, conv_cols, conv_steps, jnp.transpose(conv_rate, (1, 0, 2)), tracers.reshape(flat),
        flux_pool.reshape(steps * 3 * rows, lats), mass_pool.reshape(steps * rows, lats),
    )
    return out.reshape(tracers.shape)


def solution(mesh):
    def local(tracers, flux_pool, *rest):
        dims = (mesh.shape["tile"], mesh.shape["trc"], flux_pool.shape[1]) + tracers.shape
        return body(dims, tracers, flux_pool, *rest)

    in_specs = (
        P("trc", None, "tile", None),
        P("trc", None, None, None, "tile", None),
        P("trc", None, None, "tile", None),
        P(None, "tile"),
        P("tile", None),
        P("tile", None),
        P("tile", None, None),
    )
    out_specs = P("trc", None, "tile", None)
    return jax.shard_map(local, mesh=mesh, in_specs=in_specs, out_specs=out_specs, check_vma=False)
```

```python
import functools

import jax
import jax.numpy as jnp
from jax import lax
from jax.experimental import pallas as pl
from jax.experimental.pallas import tpu as pltpu
from jax.sharding import PartitionSpec as P

FIELDS = 4
HALO = 3
SUBSTEPS = 3
SPLIT = 2
WINDOW = 4
LEAD = 3 * SPLIT


def face_terms(flux, left_inverse, right_inverse):
    share = jnp.abs(flux) * jnp.where(flux > 0.0, left_inverse, right_inverse)
    half = 0.5 * flux * share
    bent = half * (3.0 - 2.0 * share)
    return flux - half - bent, half - bent


def edge_rise(before, here, after):
    raw = 0.5 * here + (1.0 / 12.0) * (before - after)
    return jnp.clip(raw, jnp.minimum(here, 0.0), jnp.maximum(here, 0.0))


def limited(up, down):
    up2 = up + up
    down2 = down + down
    right = jnp.clip(up, jnp.minimum(down2, 0.0), jnp.maximum(down2, 0.0))
    left = -jnp.clip(down, jnp.minimum(up2, 0.0), jnp.maximum(up2, 0.0))
    return right, left


def transport(flux, near, far, q0, right0, left0, q1, right1, left1):
    ahead = flux > 0.0
    return (
        flux * jnp.where(ahead, q0, q1)
        + near * jnp.where(ahead, right0, left1)
        + far * jnp.where(ahead, left0, right1)
    )


def kernel(
    dims,
    owner_hbm, cols_hbm, counts_hbm, rate_hbm, tracer_hbm, flux_hbm, mass_hbm,
    out_hbm,
    owner_ref, cols_ref, counts_ref, rate_ref, out_ref,
    own, inbox, relay, met, state, mid, swept, shapes, halo_out, halo_in, rim_out, rim_in,
    cx, cy, cz, inverse_t, inverse_o, lift,
    own_sem, state_sem, small_sem, out_sem, chain_send, chain_recv, halo_send, halo_recv, rim_send, rim_recv,
):
    tiles, groups, steps, tracers, levels, cells, lats = dims
    rows = levels * cells
    tile = lax.axis_index("tile")
    me = lax.axis_index("trc")
    right = lax.rem(tile + 1, tiles)
    left = lax.rem(tile + tiles - 1, tiles)
    near = lax.div(2 * me, groups)
    far = 1 - near
    near_to = me + 1 - 2 * near
    far_to = me - 1 + 2 * near
    at_end = jnp.logical_or(me == 0, me == groups - 1)
    inner = jnp.logical_and(me > 0, me < groups - 1)
    split = SPLIT if levels % SPLIT == 0 else 1
    part = rows // split
    chunk_total = steps * FIELDS * split

    load_state = pltpu.make_async_copy(tracer_hbm, state, state_sem)
    load_state.start()
    loads = []
    for s in range(steps):
        base = s * FIELDS * rows
        loads.append(pltpu.make_async_copy(
            mass_hbm.at[pl.ds(s * rows, rows)], own.at[pl.ds(base, rows)], own_sem.at[2 * s]))
        loads.append(pltpu.make_async_copy(
            flux_hbm.at[pl.ds(s * 3 * rows, 3 * rows)], own.at[pl.ds(base + rows, 3 * rows)],
            own_sem.at[2 * s + 1]))
    for load in loads:
        load.start()
    smalls = [
        pltpu.make_async_copy(source, target, small_sem.at[i])
        for i, (source, target) in enumerate((
            (owner_hbm, owner_ref), (cols_hbm, cols_ref), (counts_hbm, counts_ref), (rate_hbm, rate_ref)))
    ]
    for small in smalls:
        small.start()

    barrier = pltpu.get_barrier_semaphore()
    for neighbour in (left, right):
        pl.semaphore_signal(barrier, inc=1, device_id={"tile": neighbour}, device_id_type=pl.DeviceIdType.MESH)

    @pl.when(me > 0)
    def _():
        pl.semaphore_signal(barrier, inc=1, device_id={"trc": me - 1}, device_id_type=pl.DeviceIdType.MESH)

    @pl.when(me < groups - 1)
    def _():
        pl.semaphore_signal(barrier, inc=1, device_id={"trc": me + 1}, device_id_type=pl.DeviceIdType.MESH)

    def cell_rows(base, x):
        return pl.ds(base + x, levels, stride=cells)

    def block(i, size):
        return pl.ds(pl.multiple_of(i * size, size), size)

    def pack_halo(s, t, source, base):
        for i in range(HALO):
            at = (t * HALO + i) * levels
            halo_out[s, 0, pl.ds(at, levels), :] = source[cell_rows(base, cells - HALO + i), :]
            halo_out[s, 1, pl.ds(at, levels), :] = source[cell_rows(base, i), :]

    def halo_copy(s, side, t, how_many):
        size = HALO * levels
        at = pl.ds(pl.multiple_of(t * size, size), how_many * size)
        return pltpu.make_async_remote_copy(
            src_ref=halo_out.at[s, side, at], dst_ref=halo_in.at[s, side, at],
            send_sem=halo_send.at[s, side, t], recv_sem=halo_recv.at[s, side, t],
            device_id={"tile": left if side else right}, device_id_type=pl.DeviceIdType.MESH)

    load_state.wait()
    for t in range(tracers):
        pack_halo(0, t, state, t * rows)

    expected = 2 + jnp.where(me > 0, 1, 0) + jnp.where(me < groups - 1, 1, 0)
    pl.semaphore_wait(barrier, expected)

    def raw(c):
        s, field = divmod(c // split, FIELDS)
        start = c % split * part
        if field == 0:
            return mass_hbm.at[pl.ds(s * rows + start, part)]
        return flux_hbm.at[pl.ds((s * 3 + field - 1) * rows + start, part)]

    def chunk(c):
        return pl.ds(c * part, part)

    def chain_copy(c, way, to, source=None):
        at = chunk(c)
        return pltpu.make_async_remote_copy(
            src_ref=relay.at[way, at] if source is None else source, dst_ref=inbox.at[way, at],
            send_sem=chain_send.at[way, c], recv_sem=chain_recv.at[way, c],
            device_id={"trc": to}, device_id_type=pl.DeviceIdType.MESH)

    def pump(start, stop):
        @pl.when(at_end)
        def _():
            for c in range(start, stop):
                if c >= WINDOW:
                    chain_copy(c - WINDOW, near, near_to, raw(c - WINDOW)).wait_send()
                chain_copy(c, near, near_to, raw(c)).start()

    pump(0, min(WINDOW, chunk_total))

    for side in (0, 1):
        halo_copy(0, side, 0, tracers).start()

    for small in smalls:
        small.wait()
    cols = cols_ref[...]
    x_start = jnp.zeros_like(cols)
    for x in range(1, cells):
        x_start += jnp.where(cols >= x * lats, lats, 0)
    listed = cols.shape[1]
    at_x = x_start == lax.broadcasted_iota(jnp.int32, (cells, listed), 0) * lats
    at_y = ((cols - x_start) == lax.broadcasted_iota(jnp.int32, (lats, listed), 0)).astype(jnp.float32)
    spread = [jnp.where(at_x, counts_ref[...].astype(jnp.float32), 0.0)]
    for k in range(levels - 1):
        spread.append(jnp.where(at_x, rate_ref[k], 0.0))
    dense = lax.dot_general(
        jnp.concatenate(spread, axis=0), at_y, (((1,), (1,)), ((), ())),
        precision=lax.Precision.HIGHEST, preferred_element_type=jnp.float32)
    count = dense[:cells]
    for n in range(SUBSTEPS):
        for k in range(levels - 1):
            lift[pl.ds((n * (levels - 1) + k) * cells, cells), :] = jnp.where(
                count > n + 0.5, dense[(k + 1) * cells:(k + 2) * cells], 0.0)

    for load in loads:
        load.wait()

    def owner_of(s):
        return jnp.full((part, lats), owner_ref[0, s], jnp.int32)

    def pass_on(s, c, way, to):
        at = chunk(c)
        relay[way, at, :] = jnp.where(owner_of(s) == me, own[at, :], inbox[way, at, :])
        chain_copy(c, way, to).start()

    def near_step(s, c):
        @pl.when(inner)
        def _():
            chain_copy(c, near, near_to).wait_recv()
            pass_on(s, c, near, near_to)

    def far_arrives(s, c):
        chain_copy(c, far, near_to).wait_recv()

        @pl.when(inner)
        def _():
            pass_on(s, c, far, far_to)

    def choose(s, c):
        at = chunk(c)
        holder = owner_of(s)
        met[at, :] = jnp.where(
            holder == me, own[at, :], jnp.where(holder < me, inbox[0, at, :], inbox[1, at, :]))

    def far_step(s, c):
        far_arrives(s, c)
        choose(s, c)

    def rim_copy(s, side):
        at = pl.ds(0, 2 * levels) if side == 0 else pl.ds(2 * levels, levels)
        return pltpu.make_async_remote_copy(
            src_ref=rim_out.at[s, at], dst_ref=rim_in.at[s, at],
            send_sem=rim_send.at[s, side], recv_sem=rim_recv.at[s, side],
            device_id={"tile": left if side else right}, device_id_type=pl.DeviceIdType.MESH)

    def start_rim(s):
        mass_at = s * FIELDS * rows
        rim_out[s, pl.ds(0, levels), :] = met[cell_rows(mass_at + rows, cells - 1), :]
        rim_out[s, pl.ds(levels, levels), :] = met[cell_rows(mass_at, cells - 1), :]
        rim_out[s, pl.ds(2 * levels, levels), :] = met[cell_rows(mass_at, 0), :]
        rim_copy(s, 0).start()
        rim_copy(s, 1).start()

    def mass_terms(s):
        mass_at = s * FIELDS * rows
        for k in range(levels):
            at = pl.ds(k * cells, cells)
            inverse_o[at, :] = 1.0 / met[pl.ds(mass_at + k * cells, cells), :]
        for x in range(cells):
            inverse_t[pl.ds(x * levels, levels), :] = inverse_o[cell_rows(0, x), :]

    def x_terms(s):
        mass_at = s * FIELDS * rows
        inverses = [1.0 / rim_in[s, pl.ds(levels, levels), :]]
        fluxes = [rim_in[s, pl.ds(0, levels), :]]
        for x in range(cells):
            inverses.append(inverse_t[pl.ds(x * levels, levels), :])
            fluxes.append(met[cell_rows(mass_at + rows, x), :])
        inverses.append(1.0 / rim_in[s, pl.ds(2 * levels, levels), :])
        for x in range(cells + 1):
            at = pl.ds(x * levels, levels)
            cx[0, at, :] = fluxes[x]
            cx[1, at, :], cx[2, at, :] = face_terms(fluxes[x], inverses[x], inverses[x + 1])

    def y_terms(s):
        flux_at = (s * FIELDS + 2) * rows
        open_face = lax.broadcasted_iota(jnp.int32, (levels, lats), 1) < lats - 1
        for x in range(cells):
            at = pl.ds(x * levels, levels)
            flux = jnp.where(open_face, met[cell_rows(flux_at, x), :], 0.0)
            inverse = inverse_t[at, :]
            cy[0, at, :] = flux
            cy[1, at, :], cy[2, at, :] = face_terms(flux, inverse, pltpu.roll(inverse, lats - 1, 1))

    def z_terms(s):
        flux_at = (s * FIELDS + 3) * rows
        for k in range(levels - 1):
            at = pl.ds(k * cells, cells)
            flux = met[pl.ds(flux_at + k * cells, cells), :]
            cz[0, at, :] = flux
            cz[1, at, :], cz[2, at, :] = face_terms(
                flux, inverse_o[at, :], inverse_o[pl.ds((k + 1) * cells, cells), :])

    def padded_x(s, t):
        base = pl.multiple_of(t * rows, rows)
        q = [halo_in[s, 0, block(t * HALO + i, levels), :] for i in range(HALO)]
        q += [state[cell_rows(base, x), :] for x in range(cells)]
        return q + [halo_in[s, 1, block(t * HALO + i, levels), :] for i in range(HALO)]

    def shape_x(s, t):
        q = padded_x(s, t)
        rise = [q[i + 1] - q[i] for i in range(cells + 5)]
        up = [edge_rise(rise[i], rise[i + 1], rise[i + 2]) for i in range(cells + 3)]
        for i in range(cells + 2):
            at = block(t * (cells + 2) + i, levels)
            shapes[0, at, :], shapes[1, at, :] = limited(up[i + 1], rise[i + 1] - up[i])

    def sweep_x(s, t):
        q = padded_x(s, t)
        shape = []
        for i in range(cells + 2):
            at = block(t * (cells + 2) + i, levels)
            shape.append((shapes[0, at, :], shapes[1, at, :]))
        moved = []
        for j in range(cells + 1):
            at = pl.ds(j * levels, levels)
            moved.append(transport(
                cx[0, at, :], cx[1, at, :], cx[2, at, :],
                q[j + 2], *shape[j], q[j + 3], *shape[j + 1]))
        for x in range(cells):
            mid[block(t * cells + x, levels), :] = (
                q[x + 3] - (moved[x + 1] - moved[x]) * inverse_t[pl.ds(x * levels, levels), :])

    def sweep_y(x, q):
        at = pl.ds(x * levels, levels)
        inside = lax.broadcasted_iota(jnp.int32, (levels, lats), 1) < lats - 1

        def ahead(v):
            return pltpu.roll(v, lats - 1, 1)

        def behind(v):
            return pltpu.roll(v, 1, 1)

        q1 = ahead(q)
        rise = jnp.where(inside, q1 - q, 0.0)
        up = edge_rise(behind(rise), rise, ahead(rise))
        r, l = limited(up, behind(rise - up))
        moved = transport(cy[0, at, :], cy[1, at, :], cy[2, at, :], q, r, l, q1, ahead(r), ahead(l))
        return q - (moved - behind(moved)) * inverse_t[at, :]

    def sweep_ys(some):
        for x in range(cells):
            for t in some:
                swept[cell_rows(pl.multiple_of(t * rows, rows), x), :] = sweep_y(
                    x, mid[block(t * cells + x, levels), :])

    def sweep_z(s, t):
        base = pl.multiple_of(t * rows, rows)
        q = [swept[pl.ds(base + k * cells, cells), :] for k in range(levels)]
        zero = jnp.zeros_like(q[0])
        rise = [zero] + [q[k + 1] - q[k] for k in range(levels - 1)] + [zero]
        up = [zero] + [edge_rise(rise[k], rise[k + 1], rise[k + 2]) for k in range(levels - 1)]
        shape = [(zero, zero)]
        for k in range(1, levels - 1):
            shape.append(limited(up[k + 1], rise[k] - up[k]))
        shape.append((zero, zero))
        moved = [zero]
        for k in range(levels - 1):
            at = pl.ds(k * cells, cells)
            moved.append(transport(
                cz[0, at, :], cz[1, at, :], cz[2, at, :], q[k], *shape[k], q[k + 1], *shape[k + 1]))
        moved.append(zero)
        q = [
            q[k] - (moved[k + 1] - moved[k]) * inverse_o[pl.ds(k * cells, cells), :]
            for k in range(levels)
        ]
        for n in range(SUBSTEPS):
            gain = [
                lift[pl.ds((n * (levels - 1) + k) * cells, cells), :] * q[k] for k in range(levels - 1)
            ]
            q = [
                (q[k] + gain[k - 1] if k else q[k]) - (gain[k] if k < levels - 1 else 0.0)
                for k in range(levels)
            ]
        target = out_ref if s == steps - 1 else state
        for k in range(levels):
            target[pl.ds(base + k * cells, cells), :] = q[k]

    together = 2 if tracers % 2 == 0 else 1
    loops = tracers // together

    def each_group(body):
        def run(p, carry):
            body(p, [p * together + i for i in range(together)])
            return carry
        lax.fori_loop(0, loops, run, 0)

    def halo_arrives(s, some):
        for t in some:
            for side in (0, 1):
                halo_copy(s, side, t, 1).wait_recv()

    def rim_arrives(s):
        for side in (0, 1):
            rim_copy(s, side).wait_recv()

    def near_if(c):
        if c < chunk_total:
            near_step(c // (FIELDS * split), c)

    def shape_xs(s):
        each_group(lambda p, some: [shape_x(s, t) for t in some])

    def sweep_xs(s):
        each_group(lambda p, some: [sweep_x(s, t) for t in some])

    def out_copy(t):
        at = block(t, rows)
        return pltpu.make_async_copy(out_ref.at[at], out_hbm.at[at], out_sem.at[t])

    def sweep_zs(s):
        def run(p, some):
            for t in some:
                sweep_z(s, t)
            if s == steps - 1:
                for t in some:
                    out_copy(t).start()
            else:
                for t in some:
                    pack_halo(s + 1, t, state, pl.multiple_of(t * rows, rows))
                    for side in (0, 1):
                        halo_copy(s + 1, side, t, 1).start()
        each_group(run)

    def link(f):
        s, field = divmod(f, FIELDS)
        for c in range(f * split, (f + 1) * split):
            near_if(c + LEAD)
            far_step(s, c)
        if field == 0 and s == 0:
            mass_terms(s)
        if field == 1:
            start_rim(s)

    def links(start, stop):
        for f in range(start, min(stop, steps * FIELDS)):
            link(f)

    for side in (0, 1):
        halo_copy(0, side, 0, tracers).wait_recv()
    near_if(0)
    pump(WINDOW, min(WINDOW + 2, chunk_total))
    shape_xs(0)
    pump(WINDOW + 2, chunk_total)
    for c in range(1, LEAD):
        near_if(c)
    links(0, FIELDS - (steps == 1))
    for s in range(steps):
        follow = (s + 1) * FIELDS
        last = range(chunk_total - split, chunk_total)
        final = s == steps - 1
        if s > 0:
            links(follow - 2, follow - final)
            mass_terms(s)
        if final:
            @pl.when(inner)
            def _():
                for c in last:
                    far_arrives(s, c)
        if s > 0:
            each_group(lambda p, some: halo_arrives(s, some))
            shape_xs(s)
        rim_arrives(s)
        x_terms(s)
        sweep_xs(s)
        y_terms(s)
        each_group(lambda p, some: sweep_ys(some))
        if final:
            @pl.when(at_end)
            def _():
                for c in last:
                    far_arrives(s, c)

            for c in last:
                choose(s, c)
        else:
            links(follow, follow + 1)
        z_terms(s)
        sweep_zs(s)
        if not final:
            links(follow + 1, follow + 2)

    for side in (0, 1):
        halo_copy(0, side, 0, tracers).wait_send()
        for s in range(steps):
            rim_copy(s, side).wait_send()
    for s in range(1, steps):
        for t in range(tracers):
            for side in (0, 1):
                halo_copy(s, side, t, 1).wait_send()
    for c in range(max(chunk_total - WINDOW, 0), chunk_total):
        chain_copy(c, near, near_to).wait_send()

    @pl.when(inner)
    def _():
        for c in range(chunk_total):
            if c < chunk_total - WINDOW:
                chain_copy(c, near, near_to).wait_send()
            chain_copy(c, far, far_to).wait_send()

    for t in range(tracers):
        out_copy(t).wait()


def body(dims, tracers, flux_pool, mass_pool, owner, conv_cols, conv_steps, conv_rate):
    _, _, steps, count, levels, cells, lats = dims
    rows = levels * cells
    total = steps * FIELDS
    chunks = total * SPLIT
    flat = (count * rows, lats)
    hbm = pl.BlockSpec(memory_space=pl.ANY)
    f32 = jnp.float32
    out = pl.pallas_call(
        functools.partial(kernel, dims),
        out_shape=jax.ShapeDtypeStruct(flat, f32),
        in_specs=[hbm] * 7,
        out_specs=hbm,
        scratch_shapes=[
            pltpu.SMEM((1, steps), jnp.int32),
            pltpu.VMEM(conv_cols.shape, jnp.int32),
            pltpu.VMEM(conv_steps.shape, jnp.int32),
            pltpu.VMEM((levels - 1, 1, conv_cols.shape[1]), f32),
            pltpu.VMEM(flat, f32),
            pltpu.VMEM((total * rows, lats), f32),
            pltpu.VMEM((2, total * rows, lats), f32),
            pltpu.VMEM((2, total * rows, lats), f32),
            pltpu.VMEM((total * rows, lats), f32),
            pltpu.VMEM(flat, f32),
            pltpu.VMEM(flat, f32),
            pltpu.VMEM(flat, f32),
            pltpu.VMEM((2, count * (cells + 2) * levels, lats), f32),
            pltpu.VMEM((steps, 2, count * HALO * levels, lats), f32),
            pltpu.VMEM((steps, 2, count * HALO * levels, lats), f32),
            pltpu.VMEM((steps, 3 * levels, lats), f32),
            pltpu.VMEM((steps, 3 * levels, lats), f32),
            pltpu.VMEM((3, (cells + 1) * levels, lats), f32),
            pltpu.VMEM((3, rows, lats), f32),
            pltpu.VMEM((3, (levels - 1) * cells, lats), f32),
            pltpu.VMEM((rows, lats), f32),
            pltpu.VMEM((rows, lats), f32),
            pltpu.VMEM((SUBSTEPS * (levels - 1) * cells, lats), f32),
            pltpu.SemaphoreType.DMA((2 * steps,)),
            pltpu.SemaphoreType.DMA,
            pltpu.SemaphoreType.DMA((4,)),
            pltpu.SemaphoreType.DMA((count,)),
            pltpu.SemaphoreType.DMA((2, chunks)),
            pltpu.SemaphoreType.DMA((2, chunks)),
            pltpu.SemaphoreType.DMA((steps, 2, count)),
            pltpu.SemaphoreType.DMA((steps, 2, count)),
            pltpu.SemaphoreType.DMA((steps, 2)),
            pltpu.SemaphoreType.DMA((steps, 2)),
        ],
        compiler_params=pltpu.CompilerParams(collective_id=0, has_side_effects=True),
    )(
        owner.T, conv_cols, conv_steps, jnp.transpose(conv_rate, (1, 0, 2)), tracers.reshape(flat),
        flux_pool.reshape(steps * 3 * rows, lats), mass_pool.reshape(steps * rows, lats),
    )
    return out.reshape(tracers.shape)


def solution(mesh):
    def local(tracers, flux_pool, *rest):
        dims = (mesh.shape["tile"], mesh.shape["trc"], flux_pool.shape[1]) + tracers.shape
        return body(dims, tracers, flux_pool, *rest)

    in_specs = (
        P("trc", None, "tile", None),
        P("trc", None, None, None, "tile", None),
        P("trc", None, None, "tile", None),
        P(None, "tile"),
        P("tile", None),
        P("tile", None),
        P("tile", None, None),
    )
    out_specs = P("trc", None, "tile", None)
    return jax.shard_map(local, mesh=mesh, in_specs=in_specs, out_specs=out_specs, check_vma=False)
```

```python
import functools

import jax
import jax.numpy as jnp
from jax import lax
from jax.experimental import pallas as pl
from jax.experimental.pallas import tpu as pltpu
from jax.sharding import PartitionSpec as P

FIELDS = 4
HALO = 3
SUBSTEPS = 3
SPLIT = 1
LEAD = 3 * SPLIT


def face_terms(flux, left_inverse, right_inverse):
    share = jnp.abs(flux) * jnp.where(flux > 0.0, left_inverse, right_inverse)
    half = 0.5 * flux * share
    bent = half * (3.0 - 2.0 * share)
    return flux - half - bent, half - bent


def edge_rise(before, here, after):
    raw = 0.5 * here + (1.0 / 12.0) * (before - after)
    return jnp.clip(raw, jnp.minimum(here, 0.0), jnp.maximum(here, 0.0))


def limited(up, down):
    up2 = up + up
    down2 = down + down
    right = jnp.clip(up, jnp.minimum(down2, 0.0), jnp.maximum(down2, 0.0))
    left = -jnp.clip(down, jnp.minimum(up2, 0.0), jnp.maximum(up2, 0.0))
    return right, left


def transport(flux, near, far, q0, right0, left0, q1, right1, left1):
    ahead = flux > 0.0
    return (
        flux * jnp.where(ahead, q0, q1)
        + near * jnp.where(ahead, right0, left1)
        + far * jnp.where(ahead, left0, right1)
    )


def kernel(
    dims,
    owner_hbm, cols_hbm, counts_hbm, rate_hbm, tracer_hbm, flux_hbm, mass_hbm,
    out_hbm,
    owner_ref, cols_ref, counts_ref, rate_ref, out_ref,
    own, inbox, relay, met, state, mid, swept, shapes, halo_out, halo_in, rim_out, rim_in,
    cx, cy, cz, inverse_t, inverse_o, lift,
    own_sem, state_sem, small_sem, out_sem, chain_send, chain_recv, halo_send, halo_recv, rim_send, rim_recv,
):
    tiles, groups, steps, tracers, levels, cells, lats = dims
    rows = levels * cells
    tile = lax.axis_index("tile")
    me = lax.axis_index("trc")
    right = lax.rem(tile + 1, tiles)
    left = lax.rem(tile + tiles - 1, tiles)
    near = lax.div(2 * me, groups)
    far = 1 - near
    near_to = me + 1 - 2 * near
    far_to = me - 1 + 2 * near
    at_end = jnp.logical_or(me == 0, me == groups - 1)
    inner = jnp.logical_and(me > 0, me < groups - 1)
    split = SPLIT if levels % SPLIT == 0 else 1
    part = rows // split
    chunk_total = steps * FIELDS * split

    barrier = pltpu.get_barrier_semaphore()
    for neighbour in (left, right):
        pl.semaphore_signal(barrier, inc=1, device_id={"tile": neighbour}, device_id_type=pl.DeviceIdType.MESH)

    @pl.when(me > 0)
    def _():
        pl.semaphore_signal(barrier, inc=1, device_id={"trc": me - 1}, device_id_type=pl.DeviceIdType.MESH)

    @pl.when(me < groups - 1)
    def _():
        pl.semaphore_signal(barrier, inc=1, device_id={"trc": me + 1}, device_id_type=pl.DeviceIdType.MESH)

    load_state = pltpu.make_async_copy(tracer_hbm, state, state_sem)
    load_state.start()
    loads = []
    for s in range(steps):
        base = s * FIELDS * rows
        loads.append(pltpu.make_async_copy(
            mass_hbm.at[pl.ds(s * rows, rows)], own.at[pl.ds(base, rows)], own_sem.at[2 * s]))
        loads.append(pltpu.make_async_copy(
            flux_hbm.at[pl.ds(s * 3 * rows, 3 * rows)], own.at[pl.ds(base + rows, 3 * rows)],
            own_sem.at[2 * s + 1]))
    for load in loads:
        load.start()
    smalls = [
        pltpu.make_async_copy(source, target, small_sem.at[i])
        for i, (source, target) in enumerate((
            (owner_hbm, owner_ref), (cols_hbm, cols_ref), (counts_hbm, counts_ref), (rate_hbm, rate_ref)))
    ]
    for small in smalls:
        small.start()

    def cell_rows(base, x):
        return pl.ds(base + x, levels, stride=cells)

    def block(i, size):
        return pl.ds(pl.multiple_of(i * size, size), size)

    def pack_halo(s, t, source, base):
        for i in range(HALO):
            at = (t * HALO + i) * levels
            halo_out[s, 0, pl.ds(at, levels), :] = source[cell_rows(base, cells - HALO + i), :]
            halo_out[s, 1, pl.ds(at, levels), :] = source[cell_rows(base, i), :]

    def halo_copy(s, side, t, how_many):
        size = HALO * levels
        at = pl.ds(pl.multiple_of(t * size, size), how_many * size)
        return pltpu.make_async_remote_copy(
            src_ref=halo_out.at[s, side, at], dst_ref=halo_in.at[s, side, at],
            send_sem=halo_send.at[s, side, t], recv_sem=halo_recv.at[s, side, t],
            device_id={"tile": left if side else right}, device_id_type=pl.DeviceIdType.MESH)

    expected = 2 + jnp.where(me > 0, 1, 0) + jnp.where(me < groups - 1, 1, 0)
    pl.semaphore_wait(barrier, expected)

    def raw(c):
        s, field = divmod(c // split, FIELDS)
        start = c % split * part
        if field == 0:
            return mass_hbm.at[pl.ds(s * rows + start, part)]
        return flux_hbm.at[pl.ds((s * 3 + field - 1) * rows + start, part)]

    def chunk(c):
        return pl.ds(c * part, part)

    def chain_copy(c, way, to, source=None):
        at = chunk(c)
        return pltpu.make_async_remote_copy(
            src_ref=relay.at[way, at] if source is None else source, dst_ref=inbox.at[way, at],
            send_sem=chain_send.at[way, c], recv_sem=chain_recv.at[way, c],
            device_id={"trc": to}, device_id_type=pl.DeviceIdType.MESH)

    @pl.when(at_end)
    def _():
        for c in range(chunk_total):
            chain_copy(c, near, near_to, raw(c)).start()

    load_state.wait()
    for t in range(tracers):
        pack_halo(0, t, state, t * rows)
    for side in (0, 1):
        halo_copy(0, side, 0, tracers).start()

    for small in smalls:
        small.wait()
    cols = cols_ref[...]
    x_start = jnp.zeros_like(cols)
    for x in range(1, cells):
        x_start += jnp.where(cols >= x * lats, lats, 0)
    listed = cols.shape[1]
    at_x = x_start == lax.broadcasted_iota(jnp.int32, (cells, listed), 0) * lats
    at_y = ((cols - x_start) == lax.broadcasted_iota(jnp.int32, (lats, listed), 0)).astype(jnp.float32)
    spread = [jnp.where(at_x, counts_ref[...].astype(jnp.float32), 0.0)]
    for k in range(levels - 1):
        spread.append(jnp.where(at_x, rate_ref[k], 0.0))
    dense = lax.dot_general(
        jnp.concatenate(spread, axis=0), at_y, (((1,), (1,)), ((), ())),
        precision=lax.Precision.HIGHEST, preferred_element_type=jnp.float32)
    count = dense[:cells]
    for n in range(SUBSTEPS):
        for k in range(levels - 1):
            lift[pl.ds((n * (levels - 1) + k) * cells, cells), :] = jnp.where(
                count > n + 0.5, dense[(k + 1) * cells:(k + 2) * cells], 0.0)

    for load in loads:
        load.wait()

    def owner_of(s):
        return jnp.full((part, lats), owner_ref[0, s], jnp.int32)

    def pass_on(s, c, way, to):
        at = chunk(c)
        relay[way, at, :] = jnp.where(owner_of(s) == me, own[at, :], inbox[way, at, :])
        chain_copy(c, way, to).start()

    def near_step(s, c):
        @pl.when(inner)
        def _():
            chain_copy(c, near, near_to).wait_recv()
            pass_on(s, c, near, near_to)

    def far_arrives(s, c):
        chain_copy(c, far, near_to).wait_recv()

        @pl.when(inner)
        def _():
            pass_on(s, c, far, far_to)

    def choose(s, c):
        at = chunk(c)
        holder = owner_of(s)
        met[at, :] = jnp.where(
            holder == me, own[at, :], jnp.where(holder < me, inbox[0, at, :], inbox[1, at, :]))

    def far_step(s, c):
        far_arrives(s, c)
        choose(s, c)

    def rim_copy(s, side):
        at = pl.ds(0, 2 * levels) if side == 0 else pl.ds(2 * levels, levels)
        return pltpu.make_async_remote_copy(
            src_ref=rim_out.at[s, at], dst_ref=rim_in.at[s, at],
            send_sem=rim_send.at[s, side], recv_sem=rim_recv.at[s, side],
            device_id={"tile": left if side else right}, device_id_type=pl.DeviceIdType.MESH)

    def start_rim(s):
        mass_at = s * FIELDS * rows
        rim_out[s, pl.ds(0, levels), :] = met[cell_rows(mass_at + rows, cells - 1), :]
        rim_out[s, pl.ds(levels, levels), :] = met[cell_rows(mass_at, cells - 1), :]
        rim_out[s, pl.ds(2 * levels, levels), :] = met[cell_rows(mass_at, 0), :]
        rim_copy(s, 0).start()
        rim_copy(s, 1).start()

    def mass_terms(s):
        mass_at = s * FIELDS * rows
        for k in range(levels):
            at = pl.ds(k * cells, cells)
            inverse_o[at, :] = 1.0 / met[pl.ds(mass_at + k * cells, cells), :]
        for x in range(cells):
            inverse_t[pl.ds(x * levels, levels), :] = inverse_o[cell_rows(0, x), :]

    def x_terms(s):
        mass_at = s * FIELDS * rows
        inverses = [1.0 / rim_in[s, pl.ds(levels, levels), :]]
        fluxes = [rim_in[s, pl.ds(0, levels), :]]
        for x in range(cells):
            inverses.append(inverse_t[pl.ds(x * levels, levels), :])
            fluxes.append(met[cell_rows(mass_at + rows, x), :])
        inverses.append(1.0 / rim_in[s, pl.ds(2 * levels, levels), :])
        for x in range(cells + 1):
            at = pl.ds(x * levels, levels)
            cx[0, at, :] = fluxes[x]
            cx[1, at, :], cx[2, at, :] = face_terms(fluxes[x], inverses[x], inverses[x + 1])

    def y_terms(s):
        flux_at = (s * FIELDS + 2) * rows
        open_face = lax.broadcasted_iota(jnp.int32, (levels, lats), 1) < lats - 1
        for x in range(cells):
            at = pl.ds(x * levels, levels)
            flux = jnp.where(open_face, met[cell_rows(flux_at, x), :], 0.0)
            inverse = inverse_t[at, :]
            cy[0, at, :] = flux
            cy[1, at, :], cy[2, at, :] = face_terms(flux, inverse, pltpu.roll(inverse, lats - 1, 1))

    def z_terms(s):
        flux_at = (s * FIELDS + 3) * rows
        for k in range(levels - 1):
            at = pl.ds(k * cells, cells)
            flux = met[pl.ds(flux_at + k * cells, cells), :]
            cz[0, at, :] = flux
            cz[1, at, :], cz[2, at, :] = face_terms(
                flux, inverse_o[at, :], inverse_o[pl.ds((k + 1) * cells, cells), :])

    def padded_x(s, t):
        base = pl.multiple_of(t * rows, rows)
        q = [halo_in[s, 0, block(t * HALO + i, levels), :] for i in range(HALO)]
        q += [state[cell_rows(base, x), :] for x in range(cells)]
        return q + [halo_in[s, 1, block(t * HALO + i, levels), :] for i in range(HALO)]

    def shape_x(s, t):
        q = padded_x(s, t)
        rise = [q[i + 1] - q[i] for i in range(cells + 5)]
        up = [edge_rise(rise[i], rise[i + 1], rise[i + 2]) for i in range(cells + 3)]
        for i in range(cells + 2):
            at = block(t * (cells + 2) + i, levels)
            shapes[0, at, :], shapes[1, at, :] = limited(up[i + 1], rise[i + 1] - up[i])

    def sweep_x(s, t):
        q = padded_x(s, t)
        shape = []
        for i in range(cells + 2):
            at = block(t * (cells + 2) + i, levels)
            shape.append((shapes[0, at, :], shapes[1, at, :]))
        moved = []
        for j in range(cells + 1):
            at = pl.ds(j * levels, levels)
            moved.append(transport(
                cx[0, at, :], cx[1, at, :], cx[2, at, :],
                q[j + 2], *shape[j], q[j + 3], *shape[j + 1]))
        for x in range(cells):
            mid[block(t * cells + x, levels), :] = (
                q[x + 3] - (moved[x + 1] - moved[x]) * inverse_t[pl.ds(x * levels, levels), :])

    def sweep_y(x, q):
        at = pl.ds(x * levels, levels)
        inside = lax.broadcasted_iota(jnp.int32, (levels, lats), 1) < lats - 1

        def ahead(v):
            return pltpu.roll(v, lats - 1, 1)

        def behind(v):
            return pltpu.roll(v, 1, 1)

        q1 = ahead(q)
        rise = jnp.where(inside, q1 - q, 0.0)
        up = edge_rise(behind(rise), rise, ahead(rise))
        r, l = limited(up, behind(rise - up))
        moved = transport(cy[0, at, :], cy[1, at, :], cy[2, at, :], q, r, l, q1, ahead(r), ahead(l))
        return q - (moved - behind(moved)) * inverse_t[at, :]

    def sweep_ys(some):
        for x in range(cells):
            for t in some:
                swept[cell_rows(pl.multiple_of(t * rows, rows), x), :] = sweep_y(
                    x, mid[block(t * cells + x, levels), :])

    def sweep_z(s, t):
        base = pl.multiple_of(t * rows, rows)
        q = [swept[pl.ds(base + k * cells, cells), :] for k in range(levels)]
        zero = jnp.zeros_like(q[0])
        rise = [zero] + [q[k + 1] - q[k] for k in range(levels - 1)] + [zero]
        up = [zero] + [edge_rise(rise[k], rise[k + 1], rise[k + 2]) for k in range(levels - 1)]
        shape = [(zero, zero)]
        for k in range(1, levels - 1):
            shape.append(limited(up[k + 1], rise[k] - up[k]))
        shape.append((zero, zero))
        moved = [zero]
        for k in range(levels - 1):
            at = pl.ds(k * cells, cells)
            moved.append(transport(
                cz[0, at, :], cz[1, at, :], cz[2, at, :], q[k], *shape[k], q[k + 1], *shape[k + 1]))
        moved.append(zero)
        q = [
            q[k] - (moved[k + 1] - moved[k]) * inverse_o[pl.ds(k * cells, cells), :]
            for k in range(levels)
        ]
        for n in range(SUBSTEPS):
            gain = [
                lift[pl.ds((n * (levels - 1) + k) * cells, cells), :] * q[k] for k in range(levels - 1)
            ]
            q = [
                (q[k] + gain[k - 1] if k else q[k]) - (gain[k] if k < levels - 1 else 0.0)
                for k in range(levels)
            ]
        target = out_ref if s == steps - 1 else state
        for k in range(levels):
            target[pl.ds(base + k * cells, cells), :] = q[k]

    together = 2 if tracers % 2 == 0 else 1
    loops = tracers // together

    def each_group(body):
        def run(p, carry):
            body(p, [p * together + i for i in range(together)])
            return carry
        lax.fori_loop(0, loops, run, 0)

    def halo_arrives(s, some):
        for t in some:
            for side in (0, 1):
                halo_copy(s, side, t, 1).wait_recv()

    def rim_arrives(s):
        for side in (0, 1):
            rim_copy(s, side).wait_recv()

    def near_if(c):
        if c < chunk_total:
            near_step(c // (FIELDS * split), c)

    def shape_xs(s):
        each_group(lambda p, some: [shape_x(s, t) for t in some])

    def sweep_xs(s):
        each_group(lambda p, some: [sweep_x(s, t) for t in some])

    def out_copy(t):
        at = block(t, rows)
        return pltpu.make_async_copy(out_ref.at[at], out_hbm.at[at], out_sem.at[t])

    def sweep_zs(s):
        def run(p, some):
            for t in some:
                sweep_z(s, t)
            if s == steps - 1:
                for t in some:
                    out_copy(t).start()
            else:
                for t in some:
                    pack_halo(s + 1, t, state, pl.multiple_of(t * rows, rows))
                    for side in (0, 1):
                        halo_copy(s + 1, side, t, 1).start()
        each_group(run)

    def link(f):
        s, field = divmod(f, FIELDS)
        for c in range(f * split, (f + 1) * split):
            near_if(c + LEAD)
            far_step(s, c)
        if field == 0 and s == 0:
            mass_terms(s)
        if field == 1:
            start_rim(s)

    def links(start, stop):
        for f in range(start, min(stop, steps * FIELDS)):
            link(f)

    for side in (0, 1):
        halo_copy(0, side, 0, tracers).wait_recv()
    near_if(0)
    shape_xs(0)
    for c in range(1, LEAD):
        near_if(c)
    links(0, FIELDS - (steps == 1))
    for s in range(steps):
        follow = (s + 1) * FIELDS
        last = range(chunk_total - split, chunk_total)
        final = s == steps - 1
        if s > 0:
            links(follow - 2, follow - final)
            mass_terms(s)
        if final:
            @pl.when(inner)
            def _():
                for c in last:
                    far_arrives(s, c)
        if s > 0:
            each_group(lambda p, some: halo_arrives(s, some))
            shape_xs(s)
        rim_arrives(s)
        x_terms(s)
        sweep_xs(s)
        y_terms(s)
        each_group(lambda p, some: sweep_ys(some))
        if final:
            @pl.when(at_end)
            def _():
                for c in last:
                    far_arrives(s, c)

            for c in last:
                choose(s, c)
        else:
            links(follow, follow + 1)
        z_terms(s)
        sweep_zs(s)
        if not final:
            links(follow + 1, follow + 2)

    for side in (0, 1):
        halo_copy(0, side, 0, tracers).wait_send()
        for s in range(steps):
            rim_copy(s, side).wait_send()
    for s in range(1, steps):
        for t in range(tracers):
            for side in (0, 1):
                halo_copy(s, side, t, 1).wait_send()
    for c in range(chunk_total):
        chain_copy(c, near, near_to).wait_send()

    @pl.when(inner)
    def _():
        for c in range(chunk_total):
            chain_copy(c, far, far_to).wait_send()

    for t in range(tracers):
        out_copy(t).wait()


def body(dims, tracers, flux_pool, mass_pool, owner, conv_cols, conv_steps, conv_rate):
    _, _, steps, count, levels, cells, lats = dims
    rows = levels * cells
    total = steps * FIELDS
    chunks = total * SPLIT
    flat = (count * rows, lats)
    hbm = pl.BlockSpec(memory_space=pl.ANY)
    f32 = jnp.float32
    out = pl.pallas_call(
        functools.partial(kernel, dims),
        out_shape=jax.ShapeDtypeStruct(flat, f32),
        in_specs=[hbm] * 7,
        out_specs=pl.BlockSpec(memory_space=pl.ANY),
        scratch_shapes=[
            pltpu.SMEM((1, steps), jnp.int32),
            pltpu.VMEM(conv_cols.shape, jnp.int32),
            pltpu.VMEM(conv_steps.shape, jnp.int32),
            pltpu.VMEM((levels - 1, 1, conv_cols.shape[1]), f32),
            pltpu.VMEM(flat, f32),
            pltpu.VMEM((total * rows, lats), f32),
            pltpu.VMEM((2, total * rows, lats), f32),
            pltpu.VMEM((2, total * rows, lats), f32),
            pltpu.VMEM((total * rows, lats), f32),
            pltpu.VMEM(flat, f32),
            pltpu.VMEM(flat, f32),
            pltpu.VMEM(flat, f32),
            pltpu.VMEM((2, count * (cells + 2) * levels, lats), f32),
            pltpu.VMEM((steps, 2, count * HALO * levels, lats), f32),
            pltpu.VMEM((steps, 2, count * HALO * levels, lats), f32),
            pltpu.VMEM((steps, 3 * levels, lats), f32),
            pltpu.VMEM((steps, 3 * levels, lats), f32),
            pltpu.VMEM((3, (cells + 1) * levels, lats), f32),
            pltpu.VMEM((3, rows, lats), f32),
            pltpu.VMEM((3, (levels - 1) * cells, lats), f32),
            pltpu.VMEM((rows, lats), f32),
            pltpu.VMEM((rows, lats), f32),
            pltpu.VMEM((SUBSTEPS * (levels - 1) * cells, lats), f32),
            pltpu.SemaphoreType.DMA((2 * steps,)),
            pltpu.SemaphoreType.DMA,
            pltpu.SemaphoreType.DMA((4,)),
            pltpu.SemaphoreType.DMA((count,)),
            pltpu.SemaphoreType.DMA((2, chunks)),
            pltpu.SemaphoreType.DMA((2, chunks)),
            pltpu.SemaphoreType.DMA((steps, 2, count)),
            pltpu.SemaphoreType.DMA((steps, 2, count)),
            pltpu.SemaphoreType.DMA((steps, 2)),
            pltpu.SemaphoreType.DMA((steps, 2)),
        ],
        compiler_params=pltpu.CompilerParams(collective_id=0, has_side_effects=True),
    )(
        owner.T, conv_cols, conv_steps, jnp.transpose(conv_rate, (1, 0, 2)), tracers.reshape(flat),
        flux_pool.reshape(steps * 3 * rows, lats), mass_pool.reshape(steps * rows, lats),
    )
    return out.reshape(tracers.shape)


def solution(mesh):
    def local(tracers, flux_pool, *rest):
        dims = (mesh.shape["tile"], mesh.shape["trc"], flux_pool.shape[1]) + tracers.shape
        return body(dims, tracers, flux_pool, *rest)

    in_specs = (
        P("trc", None, "tile", None),
        P("trc", None, None, None, "tile", None),
        P("trc", None, None, "tile", None),
        P(None, "tile"),
        P("tile", None),
        P("tile", None),
        P("tile", None, None),
    )
    out_specs = P("trc", None, "tile", None)
    return jax.shard_map(local, mesh=mesh, in_specs=in_specs, out_specs=out_specs, check_vma=False)
```

```python
import functools

import jax
import jax.numpy as jnp
from jax import lax
from jax.experimental import pallas as pl
from jax.experimental.pallas import tpu as pltpu
from jax.sharding import PartitionSpec as P

FIELDS = 4
HALO = 3
SUBSTEPS = 3
SPLIT = 1
WINDOW = 3
LEAD = 3 * SPLIT


def face_terms(flux, left_inverse, right_inverse):
    share = jnp.abs(flux) * jnp.where(flux > 0.0, left_inverse, right_inverse)
    half = 0.5 * flux * share
    bent = half * (3.0 - 2.0 * share)
    return flux - half - bent, half - bent


def edge_rise(before, here, after):
    raw = 0.5 * here + (1.0 / 12.0) * (before - after)
    return jnp.clip(raw, jnp.minimum(here, 0.0), jnp.maximum(here, 0.0))


def limited(up, down):
    up2 = up + up
    down2 = down + down
    right = jnp.clip(up, jnp.minimum(down2, 0.0), jnp.maximum(down2, 0.0))
    left = -jnp.clip(down, jnp.minimum(up2, 0.0), jnp.maximum(up2, 0.0))
    return right, left


def transport(flux, near, far, q0, right0, left0, q1, right1, left1):
    ahead = flux > 0.0
    return (
        flux * jnp.where(ahead, q0, q1)
        + near * jnp.where(ahead, right0, left1)
        + far * jnp.where(ahead, left0, right1)
    )


def kernel(
    dims,
    owner_hbm, cols_hbm, counts_hbm, rate_hbm, tracer_hbm, flux_hbm, mass_hbm,
    out_hbm,
    owner_ref, cols_ref, counts_ref, rate_ref, out_ref,
    own, inbox, relay, met, state, mid, swept, shapes, halo_out, halo_in, rim_out, rim_in,
    cx, cy, cz, inverse_t, inverse_o, lift,
    own_sem, state_sem, small_sem, out_sem, chain_send, chain_recv, halo_send, halo_recv, rim_send, rim_recv,
):
    tiles, groups, steps, tracers, levels, cells, lats = dims
    rows = levels * cells
    tile = lax.axis_index("tile")
    me = lax.axis_index("trc")
    right = lax.rem(tile + 1, tiles)
    left = lax.rem(tile + tiles - 1, tiles)
    near = lax.div(2 * me, groups)
    far = 1 - near
    near_to = me + 1 - 2 * near
    far_to = me - 1 + 2 * near
    at_end = jnp.logical_or(me == 0, me == groups - 1)
    inner = jnp.logical_and(me > 0, me < groups - 1)
    split = SPLIT if levels % SPLIT == 0 else 1
    part = rows // split
    chunk_total = steps * FIELDS * split

    barrier = pltpu.get_barrier_semaphore()
    for neighbour in (left, right):
        pl.semaphore_signal(barrier, inc=1, device_id={"tile": neighbour}, device_id_type=pl.DeviceIdType.MESH)

    @pl.when(me > 0)
    def _():
        pl.semaphore_signal(barrier, inc=1, device_id={"trc": me - 1}, device_id_type=pl.DeviceIdType.MESH)

    @pl.when(me < groups - 1)
    def _():
        pl.semaphore_signal(barrier, inc=1, device_id={"trc": me + 1}, device_id_type=pl.DeviceIdType.MESH)

    load_state = pltpu.make_async_copy(tracer_hbm, state, state_sem)
    load_state.start()
    loads = []
    for s in range(steps):
        base = s * FIELDS * rows
        loads.append(pltpu.make_async_copy(
            mass_hbm.at[pl.ds(s * rows, rows)], own.at[pl.ds(base, rows)], own_sem.at[2 * s]))
        loads.append(pltpu.make_async_copy(
            flux_hbm.at[pl.ds(s * 3 * rows, 3 * rows)], own.at[pl.ds(base + rows, 3 * rows)],
            own_sem.at[2 * s + 1]))
    for load in loads:
        load.start()
    smalls = [
        pltpu.make_async_copy(source, target, small_sem.at[i])
        for i, (source, target) in enumerate((
            (owner_hbm, owner_ref), (cols_hbm, cols_ref), (counts_hbm, counts_ref), (rate_hbm, rate_ref)))
    ]
    for small in smalls:
        small.start()

    def cell_rows(base, x):
        return pl.ds(base + x, levels, stride=cells)

    def block(i, size):
        return pl.ds(pl.multiple_of(i * size, size), size)

    def pack_halo(s, t, source, base):
        for i in range(HALO):
            at = (t * HALO + i) * levels
            halo_out[s, 0, pl.ds(at, levels), :] = source[cell_rows(base, cells - HALO + i), :]
            halo_out[s, 1, pl.ds(at, levels), :] = source[cell_rows(base, i), :]

    def halo_copy(s, side, t, how_many):
        size = HALO * levels
        at = pl.ds(pl.multiple_of(t * size, size), how_many * size)
        return pltpu.make_async_remote_copy(
            src_ref=halo_out.at[s, side, at], dst_ref=halo_in.at[s, side, at],
            send_sem=halo_send.at[s, side, t], recv_sem=halo_recv.at[s, side, t],
            device_id={"tile": left if side else right}, device_id_type=pl.DeviceIdType.MESH)

    expected = 2 + jnp.where(me > 0, 1, 0) + jnp.where(me < groups - 1, 1, 0)
    pl.semaphore_wait(barrier, expected)

    def raw(c):
        s, field = divmod(c // split, FIELDS)
        start = c % split * part
        if field == 0:
            return mass_hbm.at[pl.ds(s * rows + start, part)]
        return flux_hbm.at[pl.ds((s * 3 + field - 1) * rows + start, part)]

    def chunk(c):
        return pl.ds(c * part, part)

    def chain_copy(c, way, to, source=None):
        at = chunk(c)
        return pltpu.make_async_remote_copy(
            src_ref=relay.at[way, at] if source is None else source, dst_ref=inbox.at[way, at],
            send_sem=chain_send.at[way, c], recv_sem=chain_recv.at[way, c],
            device_id={"trc": to}, device_id_type=pl.DeviceIdType.MESH)

    def pump(start, stop):
        @pl.when(at_end)
        def _():
            for c in range(min(start, chunk_total), min(stop, chunk_total)):
                if c >= WINDOW:
                    chain_copy(c - WINDOW, near, near_to, raw(c - WINDOW)).wait_send()
                chain_copy(c, near, near_to, raw(c)).start()

    pump(0, WINDOW)
    load_state.wait()
    for t in range(tracers):
        pack_halo(0, t, state, t * rows)
    for side in (0, 1):
        halo_copy(0, side, 0, tracers).start()

    pump(WINDOW, WINDOW + 1)
    for small in smalls:
        small.wait()
    cols = cols_ref[...]
    x_start = jnp.zeros_like(cols)
    for x in range(1, cells):
        x_start += jnp.where(cols >= x * lats, lats, 0)
    listed = cols.shape[1]
    at_x = x_start == lax.broadcasted_iota(jnp.int32, (cells, listed), 0) * lats
    at_y = ((cols - x_start) == lax.broadcasted_iota(jnp.int32, (lats, listed), 0)).astype(jnp.float32)
    spread = [jnp.where(at_x, counts_ref[...].astype(jnp.float32), 0.0)]
    for k in range(levels - 1):
        spread.append(jnp.where(at_x, rate_ref[k], 0.0))
    dense = lax.dot_general(
        jnp.concatenate(spread, axis=0), at_y, (((1,), (1,)), ((), ())),
        precision=lax.Precision.HIGHEST, preferred_element_type=jnp.float32)
    count = dense[:cells]
    for n in range(SUBSTEPS):
        for k in range(levels - 1):
            lift[pl.ds((n * (levels - 1) + k) * cells, cells), :] = jnp.where(
                count > n + 0.5, dense[(k + 1) * cells:(k + 2) * cells], 0.0)

    pump(WINDOW + 1, WINDOW + 3)
    for load in loads:
        load.wait()

    def owner_of(s):
        return jnp.full((part, lats), owner_ref[0, s], jnp.int32)

    def pass_on(s, c, way, to):
        at = chunk(c)
        relay[way, at, :] = jnp.where(owner_of(s) == me, own[at, :], inbox[way, at, :])
        chain_copy(c, way, to).start()

    def near_step(s, c):
        @pl.when(inner)
        def _():
            chain_copy(c, near, near_to).wait_recv()
            pass_on(s, c, near, near_to)

    def far_arrives(s, c):
        chain_copy(c, far, near_to).wait_recv()

        @pl.when(inner)
        def _():
            pass_on(s, c, far, far_to)

    def choose(s, c):
        at = chunk(c)
        holder = owner_of(s)
        met[at, :] = jnp.where(
            holder == me, own[at, :], jnp.where(holder < me, inbox[0, at, :], inbox[1, at, :]))

    def far_step(s, c):
        far_arrives(s, c)
        choose(s, c)

    def rim_copy(s, side):
        at = pl.ds(0, 2 * levels) if side == 0 else pl.ds(2 * levels, levels)
        return pltpu.make_async_remote_copy(
            src_ref=rim_out.at[s, at], dst_ref=rim_in.at[s, at],
            send_sem=rim_send.at[s, side], recv_sem=rim_recv.at[s, side],
            device_id={"tile": left if side else right}, device_id_type=pl.DeviceIdType.MESH)

    def start_rim(s):
        mass_at = s * FIELDS * rows
        rim_out[s, pl.ds(0, levels), :] = met[cell_rows(mass_at + rows, cells - 1), :]
        rim_out[s, pl.ds(levels, levels), :] = met[cell_rows(mass_at, cells - 1), :]
        rim_out[s, pl.ds(2 * levels, levels), :] = met[cell_rows(mass_at, 0), :]
        rim_copy(s, 0).start()
        rim_copy(s, 1).start()

    def mass_terms(s):
        mass_at = s * FIELDS * rows
        for k in range(levels):
            at = pl.ds(k * cells, cells)
            inverse_o[at, :] = 1.0 / met[pl.ds(mass_at + k * cells, cells), :]
        for x in range(cells):
            inverse_t[pl.ds(x * levels, levels), :] = inverse_o[cell_rows(0, x), :]

    def x_terms(s):
        mass_at = s * FIELDS * rows
        inverses = [1.0 / rim_in[s, pl.ds(levels, levels), :]]
        fluxes = [rim_in[s, pl.ds(0, levels), :]]
        for x in range(cells):
            inverses.append(inverse_t[pl.ds(x * levels, levels), :])
            fluxes.append(met[cell_rows(mass_at + rows, x), :])
        inverses.append(1.0 / rim_in[s, pl.ds(2 * levels, levels), :])
        for x in range(cells + 1):
            at = pl.ds(x * levels, levels)
            cx[0, at, :] = fluxes[x]
            cx[1, at, :], cx[2, at, :] = face_terms(fluxes[x], inverses[x], inverses[x + 1])

    def y_terms(s):
        flux_at = (s * FIELDS + 2) * rows
        open_face = lax.broadcasted_iota(jnp.int32, (levels, lats), 1) < lats - 1
        for x in range(cells):
            at = pl.ds(x * levels, levels)
            flux = jnp.where(open_face, met[cell_rows(flux_at, x), :], 0.0)
            inverse = inverse_t[at, :]
            cy[0, at, :] = flux
            cy[1, at, :], cy[2, at, :] = face_terms(flux, inverse, pltpu.roll(inverse, lats - 1, 1))

    def z_terms(s):
        flux_at = (s * FIELDS + 3) * rows
        for k in range(levels - 1):
            at = pl.ds(k * cells, cells)
            flux = met[pl.ds(flux_at + k * cells, cells), :]
            cz[0, at, :] = flux
            cz[1, at, :], cz[2, at, :] = face_terms(
                flux, inverse_o[at, :], inverse_o[pl.ds((k + 1) * cells, cells), :])

    def padded_x(s, t):
        base = pl.multiple_of(t * rows, rows)
        q = [halo_in[s, 0, block(t * HALO + i, levels), :] for i in range(HALO)]
        q += [state[cell_rows(base, x), :] for x in range(cells)]
        return q + [halo_in[s, 1, block(t * HALO + i, levels), :] for i in range(HALO)]

    def shape_x(s, t):
        q = padded_x(s, t)
        rise = [q[i + 1] - q[i] for i in range(cells + 5)]
        up = [edge_rise(rise[i], rise[i + 1], rise[i + 2]) for i in range(cells + 3)]
        for i in range(cells + 2):
            at = block(t * (cells + 2) + i, levels)
            shapes[0, at, :], shapes[1, at, :] = limited(up[i + 1], rise[i + 1] - up[i])

    def sweep_x(s, t):
        q = padded_x(s, t)
        shape = []
        for i in range(cells + 2):
            at = block(t * (cells + 2) + i, levels)
            shape.append((shapes[0, at, :], shapes[1, at, :]))
        moved = []
        for j in range(cells + 1):
            at = pl.ds(j * levels, levels)
            moved.append(transport(
                cx[0, at, :], cx[1, at, :], cx[2, at, :],
                q[j + 2], *shape[j], q[j + 3], *shape[j + 1]))
        for x in range(cells):
            mid[block(t * cells + x, levels), :] = (
                q[x + 3] - (moved[x + 1] - moved[x]) * inverse_t[pl.ds(x * levels, levels), :])

    def sweep_y(x, q):
        at = pl.ds(x * levels, levels)
        inside = lax.broadcasted_iota(jnp.int32, (levels, lats), 1) < lats - 1

        def ahead(v):
            return pltpu.roll(v, lats - 1, 1)

        def behind(v):
            return pltpu.roll(v, 1, 1)

        q1 = ahead(q)
        rise = jnp.where(inside, q1 - q, 0.0)
        up = edge_rise(behind(rise), rise, ahead(rise))
        r, l = limited(up, behind(rise - up))
        moved = transport(cy[0, at, :], cy[1, at, :], cy[2, at, :], q, r, l, q1, ahead(r), ahead(l))
        return q - (moved - behind(moved)) * inverse_t[at, :]

    def sweep_ys(some):
        for x in range(cells):
            for t in some:
                swept[cell_rows(pl.multiple_of(t * rows, rows), x), :] = sweep_y(
                    x, mid[block(t * cells + x, levels), :])

    def sweep_z(s, t):
        base = pl.multiple_of(t * rows, rows)
        q = [swept[pl.ds(base + k * cells, cells), :] for k in range(levels)]
        zero = jnp.zeros_like(q[0])
        rise = [zero] + [q[k + 1] - q[k] for k in range(levels - 1)] + [zero]
        up = [zero] + [edge_rise(rise[k], rise[k + 1], rise[k + 2]) for k in range(levels - 1)]
        shape = [(zero, zero)]
        for k in range(1, levels - 1):
            shape.append(limited(up[k + 1], rise[k] - up[k]))
        shape.append((zero, zero))
        moved = [zero]
        for k in range(levels - 1):
            at = pl.ds(k * cells, cells)
            moved.append(transport(
                cz[0, at, :], cz[1, at, :], cz[2, at, :], q[k], *shape[k], q[k + 1], *shape[k + 1]))
        moved.append(zero)
        q = [
            q[k] - (moved[k + 1] - moved[k]) * inverse_o[pl.ds(k * cells, cells), :]
            for k in range(levels)
        ]
        for n in range(SUBSTEPS):
            gain = [
                lift[pl.ds((n * (levels - 1) + k) * cells, cells), :] * q[k] for k in range(levels - 1)
            ]
            q = [
                (q[k] + gain[k - 1] if k else q[k]) - (gain[k] if k < levels - 1 else 0.0)
                for k in range(levels)
            ]
        target = out_ref if s == steps - 1 else state
        for k in range(levels):
            target[pl.ds(base + k * cells, cells), :] = q[k]

    together = 2 if tracers % 2 == 0 else 1
    loops = tracers // together

    def each_group(body):
        def run(p, carry):
            body(p, [p * together + i for i in range(together)])
            return carry
        lax.fori_loop(0, loops, run, 0)

    def halo_arrives(s, some):
        for t in some:
            for side in (0, 1):
                halo_copy(s, side, t, 1).wait_recv()

    def rim_arrives(s):
        for side in (0, 1):
            rim_copy(s, side).wait_recv()

    def near_if(c):
        if c < chunk_total:
            near_step(c // (FIELDS * split), c)

    def shape_xs(s):
        each_group(lambda p, some: [shape_x(s, t) for t in some])

    def sweep_xs(s):
        each_group(lambda p, some: [sweep_x(s, t) for t in some])

    def out_copy(t):
        at = block(t, rows)
        return pltpu.make_async_copy(out_ref.at[at], out_hbm.at[at], out_sem.at[t])

    def sweep_zs(s):
        def run(p, some):
            for t in some:
                sweep_z(s, t)
            if s == steps - 1:
                for t in some:
                    out_copy(t).start()
            else:
                for t in some:
                    pack_halo(s + 1, t, state, pl.multiple_of(t * rows, rows))
                    for side in (0, 1):
                        halo_copy(s + 1, side, t, 1).start()
        each_group(run)

    def link(f):
        s, field = divmod(f, FIELDS)
        for c in range(f * split, (f + 1) * split):
            near_if(c + LEAD)
            far_step(s, c)
        if field == 0 and s == 0:
            mass_terms(s)
        if field == 1:
            start_rim(s)

    def links(start, stop):
        for f in range(start, min(stop, steps * FIELDS)):
            link(f)

    for side in (0, 1):
        halo_copy(0, side, 0, tracers).wait_recv()
    near_if(0)
    shape_xs(0)
    pump(WINDOW + 3, chunk_total)
    for c in range(1, LEAD):
        near_if(c)
    links(0, FIELDS - (steps == 1))
    for s in range(steps):
        follow = (s + 1) * FIELDS
        last = range(chunk_total - split, chunk_total)
        final = s == steps - 1
        if s > 0:
            links(follow - 2, follow - final)
            mass_terms(s)
        if final:
            @pl.when(inner)
            def _():
                for c in last:
                    far_arrives(s, c)
        if s > 0:
            each_group(lambda p, some: halo_arrives(s, some))
            shape_xs(s)
        rim_arrives(s)
        x_terms(s)
        sweep_xs(s)
        y_terms(s)
        each_group(lambda p, some: sweep_ys(some))
        if final:
            @pl.when(at_end)
            def _():
                for c in last:
                    far_arrives(s, c)

            for c in last:
                choose(s, c)
        else:
            links(follow, follow + 1)
        z_terms(s)
        sweep_zs(s)
        if not final:
            links(follow + 1, follow + 2)

    for side in (0, 1):
        halo_copy(0, side, 0, tracers).wait_send()
        for s in range(steps):
            rim_copy(s, side).wait_send()
    for s in range(1, steps):
        for t in range(tracers):
            for side in (0, 1):
                halo_copy(s, side, t, 1).wait_send()
    for c in range(max(chunk_total - WINDOW, 0), chunk_total):
        chain_copy(c, near, near_to).wait_send()

    @pl.when(inner)
    def _():
        for c in range(chunk_total):
            if c < chunk_total - WINDOW:
                chain_copy(c, near, near_to).wait_send()
            chain_copy(c, far, far_to).wait_send()

    for t in range(tracers):
        out_copy(t).wait()


def body(dims, tracers, flux_pool, mass_pool, owner, conv_cols, conv_steps, conv_rate):
    _, _, steps, count, levels, cells, lats = dims
    rows = levels * cells
    total = steps * FIELDS
    chunks = total * SPLIT
    flat = (count * rows, lats)
    hbm = pl.BlockSpec(memory_space=pl.ANY)
    f32 = jnp.float32
    out = pl.pallas_call(
        functools.partial(kernel, dims),
        out_shape=jax.ShapeDtypeStruct(flat, f32),
        in_specs=[hbm] * 7,
        out_specs=pl.BlockSpec(memory_space=pl.ANY),
        scratch_shapes=[
            pltpu.SMEM((1, steps), jnp.int32),
            pltpu.VMEM(conv_cols.shape, jnp.int32),
            pltpu.VMEM(conv_steps.shape, jnp.int32),
            pltpu.VMEM((levels - 1, 1, conv_cols.shape[1]), f32),
            pltpu.VMEM(flat, f32),
            pltpu.VMEM((total * rows, lats), f32),
            pltpu.VMEM((2, total * rows, lats), f32),
            pltpu.VMEM((2, total * rows, lats), f32),
            pltpu.VMEM((total * rows, lats), f32),
            pltpu.VMEM(flat, f32),
            pltpu.VMEM(flat, f32),
            pltpu.VMEM(flat, f32),
            pltpu.VMEM((2, count * (cells + 2) * levels, lats), f32),
            pltpu.VMEM((steps, 2, count * HALO * levels, lats), f32),
            pltpu.VMEM((steps, 2, count * HALO * levels, lats), f32),
            pltpu.VMEM((steps, 3 * levels, lats), f32),
            pltpu.VMEM((steps, 3 * levels, lats), f32),
            pltpu.VMEM((3, (cells + 1) * levels, lats), f32),
            pltpu.VMEM((3, rows, lats), f32),
            pltpu.VMEM((3, (levels - 1) * cells, lats), f32),
            pltpu.VMEM((rows, lats), f32),
            pltpu.VMEM((rows, lats), f32),
            pltpu.VMEM((SUBSTEPS * (levels - 1) * cells, lats), f32),
            pltpu.SemaphoreType.DMA((2 * steps,)),
            pltpu.SemaphoreType.DMA,
            pltpu.SemaphoreType.DMA((4,)),
            pltpu.SemaphoreType.DMA((count,)),
            pltpu.SemaphoreType.DMA((2, chunks)),
            pltpu.SemaphoreType.DMA((2, chunks)),
            pltpu.SemaphoreType.DMA((steps, 2, count)),
            pltpu.SemaphoreType.DMA((steps, 2, count)),
            pltpu.SemaphoreType.DMA((steps, 2)),
            pltpu.SemaphoreType.DMA((steps, 2)),
        ],
        compiler_params=pltpu.CompilerParams(collective_id=0, has_side_effects=True),
    )(
        owner.T, conv_cols, conv_steps, jnp.transpose(conv_rate, (1, 0, 2)), tracers.reshape(flat),
        flux_pool.reshape(steps * 3 * rows, lats), mass_pool.reshape(steps * rows, lats),
    )
    return out.reshape(tracers.shape)


def solution(mesh):
    def local(tracers, flux_pool, *rest):
        dims = (mesh.shape["tile"], mesh.shape["trc"], flux_pool.shape[1]) + tracers.shape
        return body(dims, tracers, flux_pool, *rest)

    in_specs = (
        P("trc", None, "tile", None),
        P("trc", None, None, None, "tile", None),
        P("trc", None, None, "tile", None),
        P(None, "tile"),
        P("tile", None),
        P("tile", None),
        P("tile", None, None),
    )
    out_specs = P("trc", None, "tile", None)
    return jax.shard_map(local, mesh=mesh, in_specs=in_specs, out_specs=out_specs, check_vma=False)
```

```python
import functools

import jax
import jax.numpy as jnp
from jax import lax
from jax.experimental import pallas as pl
from jax.experimental.pallas import tpu as pltpu
from jax.sharding import PartitionSpec as P

FIELDS = 4
HALO = 3
SUBSTEPS = 3
VMEM_BYTES = 16 * 1024 * 1024
SPLIT = 1
WINDOW = 3
LEAD = 3 * SPLIT


def face_terms(flux, left_inverse, right_inverse):
    share = jnp.abs(flux) * jnp.where(flux > 0.0, left_inverse, right_inverse)
    half = 0.5 * flux * share
    bent = half * (3.0 - 2.0 * share)
    return flux - half - bent, half - bent


def edge_rise(before, here, after):
    raw = 0.5 * here + (1.0 / 12.0) * (before - after)
    return jnp.clip(raw, jnp.minimum(here, 0.0), jnp.maximum(here, 0.0))


def limited(up, down):
    up2 = up + up
    down2 = down + down
    right = jnp.clip(up, jnp.minimum(down2, 0.0), jnp.maximum(down2, 0.0))
    left = -jnp.clip(down, jnp.minimum(up2, 0.0), jnp.maximum(up2, 0.0))
    return right, left


def transport(flux, near, far, q0, right0, left0, q1, right1, left1):
    ahead = flux > 0.0
    return (
        flux * jnp.where(ahead, q0, q1)
        + near * jnp.where(ahead, right0, left1)
        + far * jnp.where(ahead, left0, right1)
    )


def kernel(
    dims,
    owner_hbm, cols_hbm, counts_hbm, rate_hbm, tracer_hbm, flux_hbm, mass_hbm,
    out_ref,
    owner_ref, cols_ref, counts_ref, rate_ref,
    own, inbox, relay, met, state, mid, swept, shapes, halo_out, halo_in, rim_out, rim_in,
    cx, cy, cz, inverse_t, inverse_o, lift,
    own_sem, state_sem, small_sem, chain_send, chain_recv, halo_send, halo_recv, rim_send, rim_recv,
):
    tiles, groups, steps, tracers, levels, cells, lats = dims
    rows = levels * cells
    tile = lax.axis_index("tile")
    me = lax.axis_index("trc")
    right = lax.rem(tile + 1, tiles)
    left = lax.rem(tile + tiles - 1, tiles)
    near = lax.div(2 * me, groups)
    far = 1 - near
    near_to = me + 1 - 2 * near
    far_to = me - 1 + 2 * near
    at_end = jnp.logical_or(me == 0, me == groups - 1)
    inner = jnp.logical_and(me > 0, me < groups - 1)
    split = SPLIT if levels % SPLIT == 0 else 1
    part = rows // split
    chunk_total = steps * FIELDS * split

    barrier = pltpu.get_barrier_semaphore()
    for neighbour in (left, right):
        pl.semaphore_signal(barrier, inc=1, device_id={"tile": neighbour}, device_id_type=pl.DeviceIdType.MESH)

    @pl.when(me > 0)
    def _():
        pl.semaphore_signal(barrier, inc=1, device_id={"trc": me - 1}, device_id_type=pl.DeviceIdType.MESH)

    @pl.when(me < groups - 1)
    def _():
        pl.semaphore_signal(barrier, inc=1, device_id={"trc": me + 1}, device_id_type=pl.DeviceIdType.MESH)

    load_state = pltpu.make_async_copy(tracer_hbm, state, state_sem)
    load_state.start()
    loads = []
    for s in range(steps):
        base = s * FIELDS * rows
        loads.append(pltpu.make_async_copy(
            mass_hbm.at[pl.ds(s * rows, rows)], own.at[pl.ds(base, rows)], own_sem.at[2 * s]))
        loads.append(pltpu.make_async_copy(
            flux_hbm.at[pl.ds(s * 3 * rows, 3 * rows)], own.at[pl.ds(base + rows, 3 * rows)],
            own_sem.at[2 * s + 1]))
    for load in loads:
        load.start()
    smalls = [
        pltpu.make_async_copy(source, target, small_sem.at[i])
        for i, (source, target) in enumerate((
            (owner_hbm, owner_ref), (cols_hbm, cols_ref), (counts_hbm, counts_ref), (rate_hbm, rate_ref)))
    ]
    for small in smalls:
        small.start()

    def cell_rows(base, x):
        return pl.ds(base + x, levels, stride=cells)

    def block(i, size):
        return pl.ds(pl.multiple_of(i * size, size), size)

    def pack_halo(s, t, source, base):
        for i in range(HALO):
            at = (t * HALO + i) * levels
            halo_out[s, 0, pl.ds(at, levels), :] = source[cell_rows(base, cells - HALO + i), :]
            halo_out[s, 1, pl.ds(at, levels), :] = source[cell_rows(base, i), :]

    def halo_copy(s, side, t, how_many):
        size = HALO * levels
        at = pl.ds(pl.multiple_of(t * size, size), how_many * size)
        return pltpu.make_async_remote_copy(
            src_ref=halo_out.at[s, side, at], dst_ref=halo_in.at[s, side, at],
            send_sem=halo_send.at[s, side, t], recv_sem=halo_recv.at[s, side, t],
            device_id={"tile": left if side else right}, device_id_type=pl.DeviceIdType.MESH)

    expected = 2 + jnp.where(me > 0, 1, 0) + jnp.where(me < groups - 1, 1, 0)
    pl.semaphore_wait(barrier, expected)

    def raw(c):
        s, field = divmod(c // split, FIELDS)
        start = c % split * part
        if field == 0:
            return mass_hbm.at[pl.ds(s * rows + start, part)]
        return flux_hbm.at[pl.ds((s * 3 + field - 1) * rows + start, part)]

    def chunk(c):
        return pl.ds(c * part, part)

    def chain_copy(c, way, to, source=None):
        at = chunk(c)
        return pltpu.make_async_remote_copy(
            src_ref=relay.at[way, at] if source is None else source, dst_ref=inbox.at[way, at],
            send_sem=chain_send.at[way, c], recv_sem=chain_recv.at[way, c],
            device_id={"trc": to}, device_id_type=pl.DeviceIdType.MESH)

    def pump(start, stop):
        @pl.when(at_end)
        def _():
            for c in range(min(start, chunk_total), min(stop, chunk_total)):
                if c >= WINDOW:
                    chain_copy(c - WINDOW, near, near_to, raw(c - WINDOW)).wait_send()
                chain_copy(c, near, near_to, raw(c)).start()

    pump(0, WINDOW)
    load_state.wait()
    for t in range(tracers):
        pack_halo(0, t, state, t * rows)
    for side in (0, 1):
        halo_copy(0, side, 0, tracers).start()

    pump(WINDOW, WINDOW + 1)
    for small in smalls:
        small.wait()
    cols = cols_ref[...]
    x_start = jnp.zeros_like(cols)
    for x in range(1, cells):
        x_start += jnp.where(cols >= x * lats, lats, 0)
    listed = cols.shape[1]
    at_x = x_start == lax.broadcasted_iota(jnp.int32, (cells, listed), 0) * lats
    at_y = ((cols - x_start) == lax.broadcasted_iota(jnp.int32, (lats, listed), 0)).astype(jnp.float32)
    spread = [jnp.where(at_x, counts_ref[...].astype(jnp.float32), 0.0)]
    for k in range(levels - 1):
        spread.append(jnp.where(at_x, rate_ref[k], 0.0))
    dense = lax.dot_general(
        jnp.concatenate(spread, axis=0), at_y, (((1,), (1,)), ((), ())),
        precision=lax.Precision.HIGHEST, preferred_element_type=jnp.float32)
    count = dense[:cells]
    for n in range(SUBSTEPS):
        for k in range(levels - 1):
            lift[pl.ds((n * (levels - 1) + k) * cells, cells), :] = jnp.where(
                count > n + 0.5, dense[(k + 1) * cells:(k + 2) * cells], 0.0)

    pump(WINDOW + 1, WINDOW + 3)
    for load in loads:
        load.wait()

    def owner_of(s):
        return jnp.full((part, lats), owner_ref[0, s], jnp.int32)

    def pass_on(s, c, way, to):
        at = chunk(c)
        relay[way, at, :] = jnp.where(owner_of(s) == me, own[at, :], inbox[way, at, :])
        chain_copy(c, way, to).start()

    def near_step(s, c):
        @pl.when(inner)
        def _():
            chain_copy(c, near, near_to).wait_recv()
            pass_on(s, c, near, near_to)

    def far_arrives(s, c):
        chain_copy(c, far, near_to).wait_recv()

        @pl.when(inner)
        def _():
            pass_on(s, c, far, far_to)

    def choose(s, c):
        at = chunk(c)
        holder = owner_of(s)
        met[at, :] = jnp.where(
            holder == me, own[at, :], jnp.where(holder < me, inbox[0, at, :], inbox[1, at, :]))

    def far_step(s, c):
        far_arrives(s, c)
        choose(s, c)

    def rim_copy(s, side):
        at = pl.ds(0, 2 * levels) if side == 0 else pl.ds(2 * levels, levels)
        return pltpu.make_async_remote_copy(
            src_ref=rim_out.at[s, at], dst_ref=rim_in.at[s, at],
            send_sem=rim_send.at[s, side], recv_sem=rim_recv.at[s, side],
            device_id={"tile": left if side else right}, device_id_type=pl.DeviceIdType.MESH)

    def start_rim(s):
        mass_at = s * FIELDS * rows
        rim_out[s, pl.ds(0, levels), :] = met[cell_rows(mass_at + rows, cells - 1), :]
        rim_out[s, pl.ds(levels, levels), :] = met[cell_rows(mass_at, cells - 1), :]
        rim_out[s, pl.ds(2 * levels, levels), :] = met[cell_rows(mass_at, 0), :]
        rim_copy(s, 0).start()
        rim_copy(s, 1).start()

    def mass_terms(s):
        mass_at = s * FIELDS * rows
        for k in range(levels):
            at = pl.ds(k * cells, cells)
            inverse_o[at, :] = 1.0 / met[pl.ds(mass_at + k * cells, cells), :]
        for x in range(cells):
            inverse_t[pl.ds(x * levels, levels), :] = inverse_o[cell_rows(0, x), :]

    def x_terms(s):
        mass_at = s * FIELDS * rows
        inverses = [1.0 / rim_in[s, pl.ds(levels, levels), :]]
        fluxes = [rim_in[s, pl.ds(0, levels), :]]
        for x in range(cells):
            inverses.append(inverse_t[pl.ds(x * levels, levels), :])
            fluxes.append(met[cell_rows(mass_at + rows, x), :])
        inverses.append(1.0 / rim_in[s, pl.ds(2 * levels, levels), :])
        for x in range(cells + 1):
            at = pl.ds(x * levels, levels)
            cx[0, at, :] = fluxes[x]
            cx[1, at, :], cx[2, at, :] = face_terms(fluxes[x], inverses[x], inverses[x + 1])

    def y_terms(s):
        flux_at = (s * FIELDS + 2) * rows
        open_face = lax.broadcasted_iota(jnp.int32, (levels, lats), 1) < lats - 1
        for x in range(cells):
            at = pl.ds(x * levels, levels)
            flux = jnp.where(open_face, met[cell_rows(flux_at, x), :], 0.0)
            inverse = inverse_t[at, :]
            cy[0, at, :] = flux
            cy[1, at, :], cy[2, at, :] = face_terms(flux, inverse, pltpu.roll(inverse, lats - 1, 1))

    def z_terms(s):
        flux_at = (s * FIELDS + 3) * rows
        for k in range(levels - 1):
            at = pl.ds(k * cells, cells)
            flux = met[pl.ds(flux_at + k * cells, cells), :]
            cz[0, at, :] = flux
            cz[1, at, :], cz[2, at, :] = face_terms(
                flux, inverse_o[at, :], inverse_o[pl.ds((k + 1) * cells, cells), :])

    def padded_x(s, t):
        base = pl.multiple_of(t * rows, rows)
        q = [halo_in[s, 0, block(t * HALO + i, levels), :] for i in range(HALO)]
        q += [state[cell_rows(base, x), :] for x in range(cells)]
        return q + [halo_in[s, 1, block(t * HALO + i, levels), :] for i in range(HALO)]

    def shape_x(s, t):
        q = padded_x(s, t)
        rise = [q[i + 1] - q[i] for i in range(cells + 5)]
        up = [edge_rise(rise[i], rise[i + 1], rise[i + 2]) for i in range(cells + 3)]
        for i in range(cells + 2):
            at = block(t * (cells + 2) + i, levels)
            shapes[0, at, :], shapes[1, at, :] = limited(up[i + 1], rise[i + 1] - up[i])

    def sweep_x(s, t):
        q = padded_x(s, t)
        shape = []
        for i in range(cells + 2):
            at = block(t * (cells + 2) + i, levels)
            shape.append((shapes[0, at, :], shapes[1, at, :]))
        moved = []
        for j in range(cells + 1):
            at = pl.ds(j * levels, levels)
            moved.append(transport(
                cx[0, at, :], cx[1, at, :], cx[2, at, :],
                q[j + 2], *shape[j], q[j + 3], *shape[j + 1]))
        for x in range(cells):
            mid[block(t * cells + x, levels), :] = (
                q[x + 3] - (moved[x + 1] - moved[x]) * inverse_t[pl.ds(x * levels, levels), :])

    def sweep_y(x, q):
        at = pl.ds(x * levels, levels)
        inside = lax.broadcasted_iota(jnp.int32, (levels, lats), 1) < lats - 1

        def ahead(v):
            return pltpu.roll(v, lats - 1, 1)

        def behind(v):
            return pltpu.roll(v, 1, 1)

        q1 = ahead(q)
        rise = jnp.where(inside, q1 - q, 0.0)
        up = edge_rise(behind(rise), rise, ahead(rise))
        r, l = limited(up, behind(rise - up))
        moved = transport(cy[0, at, :], cy[1, at, :], cy[2, at, :], q, r, l, q1, ahead(r), ahead(l))
        return q - (moved - behind(moved)) * inverse_t[at, :]

    def sweep_ys(some):
        for x in range(cells):
            for t in some:
                swept[cell_rows(pl.multiple_of(t * rows, rows), x), :] = sweep_y(
                    x, mid[block(t * cells + x, levels), :])

    def sweep_z(s, t):
        base = pl.multiple_of(t * rows, rows)
        q = [swept[pl.ds(base + k * cells, cells), :] for k in range(levels)]
        zero = jnp.zeros_like(q[0])
        rise = [zero] + [q[k + 1] - q[k] for k in range(levels - 1)] + [zero]
        up = [zero] + [edge_rise(rise[k], rise[k + 1], rise[k + 2]) for k in range(levels - 1)]
        shape = [(zero, zero)]
        for k in range(1, levels - 1):
            shape.append(limited(up[k + 1], rise[k] - up[k]))
        shape.append((zero, zero))
        moved = [zero]
        for k in range(levels - 1):
            at = pl.ds(k * cells, cells)
            moved.append(transport(
                cz[0, at, :], cz[1, at, :], cz[2, at, :], q[k], *shape[k], q[k + 1], *shape[k + 1]))
        moved.append(zero)
        q = [
            q[k] - (moved[k + 1] - moved[k]) * inverse_o[pl.ds(k * cells, cells), :]
            for k in range(levels)
        ]
        for n in range(SUBSTEPS):
            gain = [
                lift[pl.ds((n * (levels - 1) + k) * cells, cells), :] * q[k] for k in range(levels - 1)
            ]
            q = [
                (q[k] + gain[k - 1] if k else q[k]) - (gain[k] if k < levels - 1 else 0.0)
                for k in range(levels)
            ]
        target = out_ref if s == steps - 1 else state
        for k in range(levels):
            target[pl.ds(base + k * cells, cells), :] = q[k]

    together = 2 if tracers % 2 == 0 else 1
    loops = tracers // together

    def each_group(body):
        def run(p, carry):
            body(p, [p * together + i for i in range(together)])
            return carry
        lax.fori_loop(0, loops, run, 0)

    def halo_arrives(s, some):
        for t in some:
            for side in (0, 1):
                halo_copy(s, side, t, 1).wait_recv()

    def rim_arrives(s):
        for side in (0, 1):
            rim_copy(s, side).wait_recv()

    def near_if(c):
        if c < chunk_total:
            near_step(c // (FIELDS * split), c)

    def shape_xs(s):
        each_group(lambda p, some: [shape_x(s, t) for t in some])

    def sweep_xs(s):
        each_group(lambda p, some: [sweep_x(s, t) for t in some])

    def sweep_zs(s):
        def run(p, some):
            for t in some:
                sweep_z(s, t)
            if s < steps - 1:
                for t in some:
                    pack_halo(s + 1, t, state, pl.multiple_of(t * rows, rows))
                    for side in (0, 1):
                        halo_copy(s + 1, side, t, 1).start()
        each_group(run)

    def link(f):
        s, field = divmod(f, FIELDS)
        for c in range(f * split, (f + 1) * split):
            near_if(c + LEAD)
            far_step(s, c)
        if field == 0 and s == 0:
            mass_terms(s)
        if field == 1:
            start_rim(s)

    def links(start, stop):
        for f in range(start, min(stop, steps * FIELDS)):
            link(f)

    for side in (0, 1):
        halo_copy(0, side, 0, tracers).wait_recv()
    near_if(0)
    shape_xs(0)
    pump(WINDOW + 3, chunk_total)
    for c in range(1, LEAD):
        near_if(c)
    links(0, FIELDS - (steps == 1))
    for s in range(steps):
        follow = (s + 1) * FIELDS
        last = range(chunk_total - split, chunk_total)
        final = s == steps - 1
        if s > 0:
            links(follow - 2, follow - final)
            mass_terms(s)
        if final:
            @pl.when(inner)
            def _():
                for c in last:
                    far_arrives(s, c)
        if s > 0:
            each_group(lambda p, some: halo_arrives(s, some))
            shape_xs(s)
        rim_arrives(s)
        x_terms(s)
        sweep_xs(s)
        y_terms(s)
        each_group(lambda p, some: sweep_ys(some))
        if final:
            @pl.when(at_end)
            def _():
                for c in last:
                    far_arrives(s, c)

            for c in last:
                choose(s, c)
        else:
            links(follow, follow + 1)
        z_terms(s)
        sweep_zs(s)
        if not final:
            links(follow + 1, follow + 2)

    for side in (0, 1):
        halo_copy(0, side, 0, tracers).wait_send()
        for s in range(steps):
            rim_copy(s, side).wait_send()
    for s in range(1, steps):
        for t in range(tracers):
            for side in (0, 1):
                halo_copy(s, side, t, 1).wait_send()
    for c in range(max(chunk_total - WINDOW, 0), chunk_total):
        chain_copy(c, near, near_to).wait_send()

    @pl.when(inner)
    def _():
        for c in range(chunk_total):
            if c < chunk_total - WINDOW:
                chain_copy(c, near, near_to).wait_send()
            chain_copy(c, far, far_to).wait_send()


def body(dims, tracers, flux_pool, mass_pool, owner, conv_cols, conv_steps, conv_rate):
    _, _, steps, count, levels, cells, lats = dims
    rows = levels * cells
    total = steps * FIELDS
    chunks = total * SPLIT
    flat = (count * rows, lats)
    hbm = pl.BlockSpec(memory_space=pl.ANY)
    f32 = jnp.float32
    operands = (
        owner.T, conv_cols, conv_steps, jnp.transpose(conv_rate, (1, 0, 2)), tracers.reshape(flat),
        flux_pool.reshape(steps * 3 * rows, lats), mass_pool.reshape(steps * rows, lats),
    )
    out = pl.pallas_call(
        functools.partial(kernel, dims),
        out_shape=pltpu.VMEM(flat, f32),
        in_specs=[hbm] * 7,
        out_specs=pl.BlockSpec(memory_space=pltpu.VMEM),
        scratch_shapes=[
            pltpu.SMEM((1, steps), jnp.int32),
            pltpu.VMEM(conv_cols.shape, jnp.int32),
            pltpu.VMEM(conv_steps.shape, jnp.int32),
            pltpu.VMEM((levels - 1, 1, conv_cols.shape[1]), f32),
            pltpu.VMEM((total * rows, lats), f32),
            pltpu.VMEM((2, total * rows, lats), f32),
            pltpu.VMEM((2, total * rows, lats), f32),
            pltpu.VMEM((total * rows, lats), f32),
            pltpu.VMEM(flat, f32),
            pltpu.VMEM(flat, f32),
            pltpu.VMEM(flat, f32),
            pltpu.VMEM((2, count * (cells + 2) * levels, lats), f32),
            pltpu.VMEM((steps, 2, count * HALO * levels, lats), f32),
            pltpu.VMEM((steps, 2, count * HALO * levels, lats), f32),
            pltpu.VMEM((steps, 3 * levels, lats), f32),
            pltpu.VMEM((steps, 3 * levels, lats), f32),
            pltpu.VMEM((3, (cells + 1) * levels, lats), f32),
            pltpu.VMEM((3, rows, lats), f32),
            pltpu.VMEM((3, (levels - 1) * cells, lats), f32),
            pltpu.VMEM((rows, lats), f32),
            pltpu.VMEM((rows, lats), f32),
            pltpu.VMEM((SUBSTEPS * (levels - 1) * cells, lats), f32),
            pltpu.SemaphoreType.DMA((2 * steps,)),
            pltpu.SemaphoreType.DMA,
            pltpu.SemaphoreType.DMA((4,)),
            pltpu.SemaphoreType.DMA((2, chunks)),
            pltpu.SemaphoreType.DMA((2, chunks)),
            pltpu.SemaphoreType.DMA((steps, 2, count)),
            pltpu.SemaphoreType.DMA((steps, 2, count)),
            pltpu.SemaphoreType.DMA((steps, 2)),
            pltpu.SemaphoreType.DMA((steps, 2)),
        ],
        compiler_params=pltpu.CompilerParams(collective_id=0, has_side_effects=True, vmem_limit_bytes=VMEM_BYTES),
    )(*(pltpu.with_memory_space_constraint(x, pltpu.HBM) for x in operands))
    return out.reshape(tracers.shape)


def solution(mesh):
    def local(tracers, flux_pool, *rest):
        dims = (mesh.shape["tile"], mesh.shape["trc"], flux_pool.shape[1]) + tracers.shape
        return body(dims, tracers, flux_pool, *rest)

    in_specs = (
        P("trc", None, "tile", None),
        P("trc", None, None, None, "tile", None),
        P("trc", None, None, "tile", None),
        P(None, "tile"),
        P("tile", None),
        P("tile", None),
        P("tile", None, None),
    )
    out_specs = P("trc", None, "tile", None)
    return jax.shard_map(local, mesh=mesh, in_specs=in_specs, out_specs=out_specs, check_vma=False)
```

```python
import functools

import jax
import jax.numpy as jnp
from jax import lax
from jax.experimental import pallas as pl
from jax.experimental.pallas import tpu as pltpu
from jax.sharding import PartitionSpec as P

FIELDS = 4
HALO = 3
SUBSTEPS = 3
VMEM_BYTES = 16 * 1024 * 1024
SPLIT = 2
WINDOW = 64
LEAD = 3 * SPLIT


def face_terms(flux, left_inverse, right_inverse):
    share = jnp.abs(flux) * jnp.where(flux > 0.0, left_inverse, right_inverse)
    half = 0.5 * flux * share
    bent = half * (3.0 - 2.0 * share)
    return flux - half - bent, half - bent


def edge_rise(before, here, after):
    raw = 0.5 * here + (1.0 / 12.0) * (before - after)
    return jnp.clip(raw, jnp.minimum(here, 0.0), jnp.maximum(here, 0.0))


def limited(up, down):
    up2 = up + up
    down2 = down + down
    right = jnp.clip(up, jnp.minimum(down2, 0.0), jnp.maximum(down2, 0.0))
    left = -jnp.clip(down, jnp.minimum(up2, 0.0), jnp.maximum(up2, 0.0))
    return right, left


def transport(flux, near, far, q0, right0, left0, q1, right1, left1):
    ahead = flux > 0.0
    return (
        flux * jnp.where(ahead, q0, q1)
        + near * jnp.where(ahead, right0, left1)
        + far * jnp.where(ahead, left0, right1)
    )


def kernel(
    dims,
    owner_hbm, cols_hbm, counts_hbm, rate_hbm, tracer_hbm, flux_hbm, mass_hbm,
    out_ref,
    owner_ref, cols_ref, counts_ref, rate_ref,
    own, inbox, relay, met, state, mid, swept, shapes, halo_out, halo_in, rim_out, rim_in,
    cx, cy, cz, inverse_t, inverse_o, lift,
    own_sem, state_sem, small_sem, chain_send, chain_recv, halo_send, halo_recv, rim_send, rim_recv,
):
    tiles, groups, steps, tracers, levels, cells, lats = dims
    rows = levels * cells
    tile = lax.axis_index("tile")
    me = lax.axis_index("trc")
    right = lax.rem(tile + 1, tiles)
    left = lax.rem(tile + tiles - 1, tiles)
    near = lax.div(2 * me, groups)
    far = 1 - near
    near_to = me + 1 - 2 * near
    far_to = me - 1 + 2 * near
    at_end = jnp.logical_or(me == 0, me == groups - 1)
    inner = jnp.logical_and(me > 0, me < groups - 1)
    split = SPLIT if levels % SPLIT == 0 else 1
    part = rows // split
    chunk_total = steps * FIELDS * split

    barrier = pltpu.get_barrier_semaphore()
    for neighbour in (left, right):
        pl.semaphore_signal(barrier, inc=1, device_id={"tile": neighbour}, device_id_type=pl.DeviceIdType.MESH)

    @pl.when(me > 0)
    def _():
        pl.semaphore_signal(barrier, inc=1, device_id={"trc": me - 1}, device_id_type=pl.DeviceIdType.MESH)

    @pl.when(me < groups - 1)
    def _():
        pl.semaphore_signal(barrier, inc=1, device_id={"trc": me + 1}, device_id_type=pl.DeviceIdType.MESH)

    load_state = pltpu.make_async_copy(tracer_hbm, state, state_sem)
    load_state.start()
    loads = []
    for s in range(steps):
        base = s * FIELDS * rows
        loads.append(pltpu.make_async_copy(
            mass_hbm.at[pl.ds(s * rows, rows)], own.at[pl.ds(base, rows)], own_sem.at[2 * s]))
        loads.append(pltpu.make_async_copy(
            flux_hbm.at[pl.ds(s * 3 * rows, 3 * rows)], own.at[pl.ds(base + rows, 3 * rows)],
            own_sem.at[2 * s + 1]))
    for load in loads:
        load.start()
    smalls = [
        pltpu.make_async_copy(source, target, small_sem.at[i])
        for i, (source, target) in enumerate((
            (owner_hbm, owner_ref), (cols_hbm, cols_ref), (counts_hbm, counts_ref), (rate_hbm, rate_ref)))
    ]
    for small in smalls:
        small.start()

    def cell_rows(base, x):
        return pl.ds(base + x, levels, stride=cells)

    def block(i, size):
        return pl.ds(pl.multiple_of(i * size, size), size)

    def pack_halo(s, t, source, base):
        for i in range(HALO):
            at = (t * HALO + i) * levels
            halo_out[s, 0, pl.ds(at, levels), :] = source[cell_rows(base, cells - HALO + i), :]
            halo_out[s, 1, pl.ds(at, levels), :] = source[cell_rows(base, i), :]

    def halo_copy(s, side, t, how_many):
        size = HALO * levels
        at = pl.ds(pl.multiple_of(t * size, size), how_many * size)
        return pltpu.make_async_remote_copy(
            src_ref=halo_out.at[s, side, at], dst_ref=halo_in.at[s, side, at],
            send_sem=halo_send.at[s, side, t], recv_sem=halo_recv.at[s, side, t],
            device_id={"tile": left if side else right}, device_id_type=pl.DeviceIdType.MESH)

    expected = 2 + jnp.where(me > 0, 1, 0) + jnp.where(me < groups - 1, 1, 0)
    pl.semaphore_wait(barrier, expected)

    def raw(c):
        s, field = divmod(c // split, FIELDS)
        start = c % split * part
        if field == 0:
            return mass_hbm.at[pl.ds(s * rows + start, part)]
        return flux_hbm.at[pl.ds((s * 3 + field - 1) * rows + start, part)]

    def chunk(c):
        return pl.ds(c * part, part)

    def chain_copy(c, way, to, source=None):
        at = chunk(c)
        return pltpu.make_async_remote_copy(
            src_ref=relay.at[way, at] if source is None else source, dst_ref=inbox.at[way, at],
            send_sem=chain_send.at[way, c], recv_sem=chain_recv.at[way, c],
            device_id={"trc": to}, device_id_type=pl.DeviceIdType.MESH)

    def pump(start, stop):
        @pl.when(at_end)
        def _():
            for c in range(min(start, chunk_total), min(stop, chunk_total)):
                if c >= WINDOW:
                    chain_copy(c - WINDOW, near, near_to, raw(c - WINDOW)).wait_send()
                chain_copy(c, near, near_to, raw(c)).start()

    pump(0, WINDOW)
    load_state.wait()
    for t in range(tracers):
        pack_halo(0, t, state, t * rows)
    for side in (0, 1):
        halo_copy(0, side, 0, tracers).start()

    pump(WINDOW, WINDOW + 1)
    for small in smalls:
        small.wait()
    cols = cols_ref[...]
    x_start = jnp.zeros_like(cols)
    for x in range(1, cells):
        x_start += jnp.where(cols >= x * lats, lats, 0)
    listed = cols.shape[1]
    at_x = x_start == lax.broadcasted_iota(jnp.int32, (cells, listed), 0) * lats
    at_y = ((cols - x_start) == lax.broadcasted_iota(jnp.int32, (lats, listed), 0)).astype(jnp.float32)
    spread = [jnp.where(at_x, counts_ref[...].astype(jnp.float32), 0.0)]
    for k in range(levels - 1):
        spread.append(jnp.where(at_x, rate_ref[k], 0.0))
    dense = lax.dot_general(
        jnp.concatenate(spread, axis=0), at_y, (((1,), (1,)), ((), ())),
        precision=lax.Precision.HIGHEST, preferred_element_type=jnp.float32)
    count = dense[:cells]
    for n in range(SUBSTEPS):
        for k in range(levels - 1):
            lift[pl.ds((n * (levels - 1) + k) * cells, cells), :] = jnp.where(
                count > n + 0.5, dense[(k + 1) * cells:(k + 2) * cells], 0.0)

    pump(WINDOW + 1, WINDOW + 3)
    for load in loads:
        load.wait()

    def owner_of(s):
        return jnp.full((part, lats), owner_ref[0, s], jnp.int32)

    def pass_on(s, c, way, to):
        at = chunk(c)
        relay[way, at, :] = jnp.where(owner_of(s) == me, own[at, :], inbox[way, at, :])
        chain_copy(c, way, to).start()

    def near_step(s, c):
        @pl.when(inner)
        def _():
            chain_copy(c, near, near_to).wait_recv()
            pass_on(s, c, near, near_to)

    def far_arrives(s, c):
        chain_copy(c, far, near_to).wait_recv()

        @pl.when(inner)
        def _():
            pass_on(s, c, far, far_to)

    def choose(s, c):
        at = chunk(c)
        holder = owner_of(s)
        met[at, :] = jnp.where(
            holder == me, own[at, :], jnp.where(holder < me, inbox[0, at, :], inbox[1, at, :]))

    def far_step(s, c):
        far_arrives(s, c)
        choose(s, c)

    def rim_copy(s, side):
        at = pl.ds(0, 2 * levels) if side == 0 else pl.ds(2 * levels, levels)
        return pltpu.make_async_remote_copy(
            src_ref=rim_out.at[s, at], dst_ref=rim_in.at[s, at],
            send_sem=rim_send.at[s, side], recv_sem=rim_recv.at[s, side],
            device_id={"tile": left if side else right}, device_id_type=pl.DeviceIdType.MESH)

    def start_rim(s):
        mass_at = s * FIELDS * rows
        rim_out[s, pl.ds(0, levels), :] = met[cell_rows(mass_at + rows, cells - 1), :]
        rim_out[s, pl.ds(levels, levels), :] = met[cell_rows(mass_at, cells - 1), :]
        rim_out[s, pl.ds(2 * levels, levels), :] = met[cell_rows(mass_at, 0), :]
        rim_copy(s, 0).start()
        rim_copy(s, 1).start()

    def mass_terms(s):
        mass_at = s * FIELDS * rows
        for k in range(levels):
            at = pl.ds(k * cells, cells)
            inverse_o[at, :] = 1.0 / met[pl.ds(mass_at + k * cells, cells), :]
        for x in range(cells):
            inverse_t[pl.ds(x * levels, levels), :] = inverse_o[cell_rows(0, x), :]

    def x_terms(s):
        mass_at = s * FIELDS * rows
        inverses = [1.0 / rim_in[s, pl.ds(levels, levels), :]]
        fluxes = [rim_in[s, pl.ds(0, levels), :]]
        for x in range(cells):
            inverses.append(inverse_t[pl.ds(x * levels, levels), :])
            fluxes.append(met[cell_rows(mass_at + rows, x), :])
        inverses.append(1.0 / rim_in[s, pl.ds(2 * levels, levels), :])
        for x in range(cells + 1):
            at = pl.ds(x * levels, levels)
            cx[0, at, :] = fluxes[x]
            cx[1, at, :], cx[2, at, :] = face_terms(fluxes[x], inverses[x], inverses[x + 1])

    def y_terms(s):
        flux_at = (s * FIELDS + 2) * rows
        open_face = lax.broadcasted_iota(jnp.int32, (levels, lats), 1) < lats - 1
        for x in range(cells):
            at = pl.ds(x * levels, levels)
            flux = jnp.where(open_face, met[cell_rows(flux_at, x), :], 0.0)
            inverse = inverse_t[at, :]
            cy[0, at, :] = flux
            cy[1, at, :], cy[2, at, :] = face_terms(flux, inverse, pltpu.roll(inverse, lats - 1, 1))

    def z_terms(s):
        flux_at = (s * FIELDS + 3) * rows
        for k in range(levels - 1):
            at = pl.ds(k * cells, cells)
            flux = met[pl.ds(flux_at + k * cells, cells), :]
            cz[0, at, :] = flux
            cz[1, at, :], cz[2, at, :] = face_terms(
                flux, inverse_o[at, :], inverse_o[pl.ds((k + 1) * cells, cells), :])

    def padded_x(s, t):
        base = pl.multiple_of(t * rows, rows)
        q = [halo_in[s, 0, block(t * HALO + i, levels), :] for i in range(HALO)]
        q += [state[cell_rows(base, x), :] for x in range(cells)]
        return q + [halo_in[s, 1, block(t * HALO + i, levels), :] for i in range(HALO)]

    def shape_x(s, t):
        q = padded_x(s, t)
        rise = [q[i + 1] - q[i] for i in range(cells + 5)]
        up = [edge_rise(rise[i], rise[i + 1], rise[i + 2]) for i in range(cells + 3)]
        for i in range(cells + 2):
            at = block(t * (cells + 2) + i, levels)
            shapes[0, at, :], shapes[1, at, :] = limited(up[i + 1], rise[i + 1] - up[i])

    def sweep_x(s, t):
        q = padded_x(s, t)
        shape = []
        for i in range(cells + 2):
            at = block(t * (cells + 2) + i, levels)
            shape.append((shapes[0, at, :], shapes[1, at, :]))
        moved = []
        for j in range(cells + 1):
            at = pl.ds(j * levels, levels)
            moved.append(transport(
                cx[0, at, :], cx[1, at, :], cx[2, at, :],
                q[j + 2], *shape[j], q[j + 3], *shape[j + 1]))
        for x in range(cells):
            mid[block(t * cells + x, levels), :] = (
                q[x + 3] - (moved[x + 1] - moved[x]) * inverse_t[pl.ds(x * levels, levels), :])

    def sweep_y(x, q):
        at = pl.ds(x * levels, levels)
        inside = lax.broadcasted_iota(jnp.int32, (levels, lats), 1) < lats - 1

        def ahead(v):
            return pltpu.roll(v, lats - 1, 1)

        def behind(v):
            return pltpu.roll(v, 1, 1)

        q1 = ahead(q)
        rise = jnp.where(inside, q1 - q, 0.0)
        up = edge_rise(behind(rise), rise, ahead(rise))
        r, l = limited(up, behind(rise - up))
        moved = transport(cy[0, at, :], cy[1, at, :], cy[2, at, :], q, r, l, q1, ahead(r), ahead(l))
        return q - (moved - behind(moved)) * inverse_t[at, :]

    def sweep_ys(some):
        for x in range(cells):
            for t in some:
                swept[cell_rows(pl.multiple_of(t * rows, rows), x), :] = sweep_y(
                    x, mid[block(t * cells + x, levels), :])

    def sweep_z(s, t):
        base = pl.multiple_of(t * rows, rows)
        q = [swept[pl.ds(base + k * cells, cells), :] for k in range(levels)]
        zero = jnp.zeros_like(q[0])
        rise = [zero] + [q[k + 1] - q[k] for k in range(levels - 1)] + [zero]
        up = [zero] + [edge_rise(rise[k], rise[k + 1], rise[k + 2]) for k in range(levels - 1)]
        shape = [(zero, zero)]
        for k in range(1, levels - 1):
            shape.append(limited(up[k + 1], rise[k] - up[k]))
        shape.append((zero, zero))
        moved = [zero]
        for k in range(levels - 1):
            at = pl.ds(k * cells, cells)
            moved.append(transport(
                cz[0, at, :], cz[1, at, :], cz[2, at, :], q[k], *shape[k], q[k + 1], *shape[k + 1]))
        moved.append(zero)
        q = [
            q[k] - (moved[k + 1] - moved[k]) * inverse_o[pl.ds(k * cells, cells), :]
            for k in range(levels)
        ]
        for n in range(SUBSTEPS):
            gain = [
                lift[pl.ds((n * (levels - 1) + k) * cells, cells), :] * q[k] for k in range(levels - 1)
            ]
            q = [
                (q[k] + gain[k - 1] if k else q[k]) - (gain[k] if k < levels - 1 else 0.0)
                for k in range(levels)
            ]
        target = out_ref if s == steps - 1 else state
        for k in range(levels):
            target[pl.ds(base + k * cells, cells), :] = q[k]

    together = 2 if tracers % 2 == 0 else 1
    loops = tracers // together

    def each_group(body):
        def run(p, carry):
            body(p, [p * together + i for i in range(together)])
            return carry
        lax.fori_loop(0, loops, run, 0)

    def halo_arrives(s, some):
        for t in some:
            for side in (0, 1):
                halo_copy(s, side, t, 1).wait_recv()

    def rim_arrives(s):
        for side in (0, 1):
            rim_copy(s, side).wait_recv()

    def near_if(c):
        if c < chunk_total:
            near_step(c // (FIELDS * split), c)

    def shape_xs(s):
        each_group(lambda p, some: [shape_x(s, t) for t in some])

    def sweep_xs(s):
        each_group(lambda p, some: [sweep_x(s, t) for t in some])

    def sweep_zs(s):
        def run(p, some):
            for t in some:
                sweep_z(s, t)
            if s < steps - 1:
                for t in some:
                    pack_halo(s + 1, t, state, pl.multiple_of(t * rows, rows))
                    for side in (0, 1):
                        halo_copy(s + 1, side, t, 1).start()
        each_group(run)

    def link(f):
        s, field = divmod(f, FIELDS)
        for c in range(f * split, (f + 1) * split):
            near_if(c + LEAD)
            far_step(s, c)
        if field == 0 and s == 0:
            mass_terms(s)
        if field == 1:
            start_rim(s)

    def links(start, stop):
        for f in range(start, min(stop, steps * FIELDS)):
            link(f)

    for side in (0, 1):
        halo_copy(0, side, 0, tracers).wait_recv()
    near_if(0)
    shape_xs(0)
    pump(WINDOW + 3, chunk_total)
    for c in range(1, LEAD):
        near_if(c)
    links(0, FIELDS - (steps == 1))
    for s in range(steps):
        follow = (s + 1) * FIELDS
        last = range(chunk_total - split, chunk_total)
        final = s == steps - 1
        if s > 0:
            links(follow - 2, follow - final)
            mass_terms(s)
        if final:
            @pl.when(inner)
            def _():
                for c in last:
                    far_arrives(s, c)
        if s > 0:
            each_group(lambda p, some: halo_arrives(s, some))
            shape_xs(s)
        rim_arrives(s)
        x_terms(s)
        sweep_xs(s)
        y_terms(s)
        each_group(lambda p, some: sweep_ys(some))
        if final:
            @pl.when(at_end)
            def _():
                for c in last:
                    far_arrives(s, c)

            for c in last:
                choose(s, c)
        else:
            links(follow, follow + 1)
        z_terms(s)
        sweep_zs(s)
        if not final:
            links(follow + 1, follow + 2)

    for side in (0, 1):
        halo_copy(0, side, 0, tracers).wait_send()
        for s in range(steps):
            rim_copy(s, side).wait_send()
    for s in range(1, steps):
        for t in range(tracers):
            for side in (0, 1):
                halo_copy(s, side, t, 1).wait_send()
    for c in range(max(chunk_total - WINDOW, 0), chunk_total):
        chain_copy(c, near, near_to).wait_send()

    @pl.when(inner)
    def _():
        for c in range(chunk_total):
            if c < chunk_total - WINDOW:
                chain_copy(c, near, near_to).wait_send()
            chain_copy(c, far, far_to).wait_send()


def body(dims, tracers, flux_pool, mass_pool, owner, conv_cols, conv_steps, conv_rate):
    _, _, steps, count, levels, cells, lats = dims
    rows = levels * cells
    total = steps * FIELDS
    chunks = total * SPLIT
    flat = (count * rows, lats)
    hbm = pl.BlockSpec(memory_space=pl.ANY)
    f32 = jnp.float32
    operands = (
        owner.T, conv_cols, conv_steps, jnp.transpose(conv_rate, (1, 0, 2)), tracers.reshape(flat),
        flux_pool.reshape(steps * 3 * rows, lats), mass_pool.reshape(steps * rows, lats),
    )
    out = pl.pallas_call(
        functools.partial(kernel, dims),
        out_shape=pltpu.VMEM(flat, f32),
        in_specs=[hbm] * 7,
        out_specs=pl.BlockSpec(memory_space=pltpu.VMEM),
        scratch_shapes=[
            pltpu.SMEM((1, steps), jnp.int32),
            pltpu.VMEM(conv_cols.shape, jnp.int32),
            pltpu.VMEM(conv_steps.shape, jnp.int32),
            pltpu.VMEM((levels - 1, 1, conv_cols.shape[1]), f32),
            pltpu.VMEM((total * rows, lats), f32),
            pltpu.VMEM((2, total * rows, lats), f32),
            pltpu.VMEM((2, total * rows, lats), f32),
            pltpu.VMEM((total * rows, lats), f32),
            pltpu.VMEM(flat, f32),
            pltpu.VMEM(flat, f32),
            pltpu.VMEM(flat, f32),
            pltpu.VMEM((2, count * (cells + 2) * levels, lats), f32),
            pltpu.VMEM((steps, 2, count * HALO * levels, lats), f32),
            pltpu.VMEM((steps, 2, count * HALO * levels, lats), f32),
            pltpu.VMEM((steps, 3 * levels, lats), f32),
            pltpu.VMEM((steps, 3 * levels, lats), f32),
            pltpu.VMEM((3, (cells + 1) * levels, lats), f32),
            pltpu.VMEM((3, rows, lats), f32),
            pltpu.VMEM((3, (levels - 1) * cells, lats), f32),
            pltpu.VMEM((rows, lats), f32),
            pltpu.VMEM((rows, lats), f32),
            pltpu.VMEM((SUBSTEPS * (levels - 1) * cells, lats), f32),
            pltpu.SemaphoreType.DMA((2 * steps,)),
            pltpu.SemaphoreType.DMA,
            pltpu.SemaphoreType.DMA((4,)),
            pltpu.SemaphoreType.DMA((2, chunks)),
            pltpu.SemaphoreType.DMA((2, chunks)),
            pltpu.SemaphoreType.DMA((steps, 2, count)),
            pltpu.SemaphoreType.DMA((steps, 2, count)),
            pltpu.SemaphoreType.DMA((steps, 2)),
            pltpu.SemaphoreType.DMA((steps, 2)),
        ],
        compiler_params=pltpu.CompilerParams(collective_id=0, has_side_effects=True, vmem_limit_bytes=VMEM_BYTES),
    )(*(pltpu.with_memory_space_constraint(x, pltpu.HBM) for x in operands))
    return out.reshape(tracers.shape)


def solution(mesh):
    def local(tracers, flux_pool, *rest):
        dims = (mesh.shape["tile"], mesh.shape["trc"], flux_pool.shape[1]) + tracers.shape
        return body(dims, tracers, flux_pool, *rest)

    in_specs = (
        P("trc", None, "tile", None),
        P("trc", None, None, None, "tile", None),
        P("trc", None, None, "tile", None),
        P(None, "tile"),
        P("tile", None),
        P("tile", None),
        P("tile", None, None),
    )
    out_specs = P("trc", None, "tile", None)
    return jax.shard_map(local, mesh=mesh, in_specs=in_specs, out_specs=out_specs, check_vma=False)
```

```python
import functools

import jax
import jax.numpy as jnp
from jax import lax
from jax.experimental import pallas as pl
from jax.experimental.pallas import tpu as pltpu
from jax.sharding import PartitionSpec as P

FIELDS = 4
HALO = 3
SUBSTEPS = 3
VMEM_BYTES = 16 * 1024 * 1024
SPLIT = 1
WINDOW = 3
LEAD = 3 * SPLIT


def face_terms(flux, left_inverse, right_inverse):
    share = jnp.abs(flux) * jnp.where(flux > 0.0, left_inverse, right_inverse)
    half = 0.5 * flux * share
    bent = half * (3.0 - 2.0 * share)
    return flux - half - bent, half - bent


def edge_rise(before, here, after):
    raw = 0.5 * here + (1.0 / 12.0) * (before - after)
    return jnp.clip(raw, jnp.minimum(here, 0.0), jnp.maximum(here, 0.0))


def limited(up, down):
    up2 = up + up
    down2 = down + down
    right = jnp.clip(up, jnp.minimum(down2, 0.0), jnp.maximum(down2, 0.0))
    left = -jnp.clip(down, jnp.minimum(up2, 0.0), jnp.maximum(up2, 0.0))
    return right, left


def transport(flux, near, far, q0, right0, left0, q1, right1, left1):
    ahead = flux > 0.0
    return (
        flux * jnp.where(ahead, q0, q1)
        + near * jnp.where(ahead, right0, left1)
        + far * jnp.where(ahead, left0, right1)
    )


def kernel(
    dims,
    owner_hbm, cols_hbm, counts_hbm, rate_hbm, tracer_hbm, flux_hbm, mass_hbm,
    out_ref,
    owner_ref, cols_ref, counts_ref, rate_ref,
    own, inbox, relay, met, state, mid, swept, shapes, halo_out, halo_in, rim_out, rim_in,
    cx, cy, cz, inverse_t, inverse_o, lift,
    own_sem, state_sem, small_sem, chain_send, chain_recv, halo_send, halo_recv, rim_send, rim_recv,
):
    tiles, groups, steps, tracers, levels, cells, lats = dims
    rows = levels * cells
    tile = lax.axis_index("tile")
    me = lax.axis_index("trc")
    right = lax.rem(tile + 1, tiles)
    left = lax.rem(tile + tiles - 1, tiles)
    near = lax.div(2 * me, groups)
    far = 1 - near
    near_to = me + 1 - 2 * near
    far_to = me - 1 + 2 * near
    at_end = jnp.logical_or(me == 0, me == groups - 1)
    inner = jnp.logical_and(me > 0, me < groups - 1)
    split = SPLIT if levels % SPLIT == 0 else 1
    part = rows // split
    chunk_total = steps * FIELDS * split

    barrier = pltpu.get_barrier_semaphore()
    for neighbour in (left, right):
        pl.semaphore_signal(barrier, inc=1, device_id={"tile": neighbour}, device_id_type=pl.DeviceIdType.MESH)

    @pl.when(me > 0)
    def _():
        pl.semaphore_signal(barrier, inc=1, device_id={"trc": me - 1}, device_id_type=pl.DeviceIdType.MESH)

    @pl.when(me < groups - 1)
    def _():
        pl.semaphore_signal(barrier, inc=1, device_id={"trc": me + 1}, device_id_type=pl.DeviceIdType.MESH)

    load_state = pltpu.make_async_copy(tracer_hbm, state, state_sem)
    load_state.start()
    loads = []
    for s in range(steps):
        base = s * FIELDS * rows
        loads.append(pltpu.make_async_copy(
            mass_hbm.at[pl.ds(s * rows, rows)], own.at[pl.ds(base, rows)], own_sem.at[2 * s]))
        loads.append(pltpu.make_async_copy(
            flux_hbm.at[pl.ds(s * 3 * rows, 3 * rows)], own.at[pl.ds(base + rows, 3 * rows)],
            own_sem.at[2 * s + 1]))
    for load in loads:
        load.start()
    smalls = [
        pltpu.make_async_copy(source, target, small_sem.at[i])
        for i, (source, target) in enumerate((
            (owner_hbm, owner_ref), (cols_hbm, cols_ref), (counts_hbm, counts_ref), (rate_hbm, rate_ref)))
    ]
    for small in smalls:
        small.start()

    def cell_rows(base, x):
        return pl.ds(base + x, levels, stride=cells)

    def block(i, size):
        return pl.ds(pl.multiple_of(i * size, size), size)

    def pack_halo(s, t, source, base):
        for i in range(HALO):
            at = (t * HALO + i) * levels
            halo_out[s, 0, pl.ds(at, levels), :] = source[cell_rows(base, cells - HALO + i), :]
            halo_out[s, 1, pl.ds(at, levels), :] = source[cell_rows(base, i), :]

    def halo_copy(s, side, t, how_many):
        size = HALO * levels
        at = pl.ds(pl.multiple_of(t * size, size), how_many * size)
        return pltpu.make_async_remote_copy(
            src_ref=halo_out.at[s, side, at], dst_ref=halo_in.at[s, side, at],
            send_sem=halo_send.at[s, side, t], recv_sem=halo_recv.at[s, side, t],
            device_id={"tile": left if side else right}, device_id_type=pl.DeviceIdType.MESH)

    expected = 2 + jnp.where(me > 0, 1, 0) + jnp.where(me < groups - 1, 1, 0)
    pl.semaphore_wait(barrier, expected)

    def raw(c):
        s, field = divmod(c // split, FIELDS)
        start = c % split * part
        if field == 0:
            return mass_hbm.at[pl.ds(s * rows + start, part)]
        return flux_hbm.at[pl.ds((s * 3 + field - 1) * rows + start, part)]

    def chunk(c):
        return pl.ds(c * part, part)

    def chain_copy(c, way, to, source=None):
        at = chunk(c)
        return pltpu.make_async_remote_copy(
            src_ref=relay.at[way, at] if source is None else source, dst_ref=inbox.at[way, at],
            send_sem=chain_send.at[way, c], recv_sem=chain_recv.at[way, c],
            device_id={"trc": to}, device_id_type=pl.DeviceIdType.MESH)

    def pump(start, stop):
        @pl.when(at_end)
        def _():
            for c in range(min(start, chunk_total), min(stop, chunk_total)):
                if c >= WINDOW:
                    chain_copy(c - WINDOW, near, near_to, raw(c - WINDOW)).wait_send()
                chain_copy(c, near, near_to, raw(c)).start()

    pump(0, WINDOW)
    load_state.wait()
    for t in range(tracers):
        pack_halo(0, t, state, t * rows)
    for side in (0, 1):
        halo_copy(0, side, 0, tracers).start()

    pump(WINDOW, WINDOW + 1)
    for small in smalls:
        small.wait()
    cols = cols_ref[...]
    x_start = jnp.zeros_like(cols)
    for x in range(1, cells):
        x_start += jnp.where(cols >= x * lats, lats, 0)
    listed = cols.shape[1]
    at_x = x_start == lax.broadcasted_iota(jnp.int32, (cells, listed), 0) * lats
    at_y = ((cols - x_start) == lax.broadcasted_iota(jnp.int32, (lats, listed), 0)).astype(jnp.float32)
    spread = [jnp.where(at_x, counts_ref[...].astype(jnp.float32), 0.0)]
    for k in range(levels - 1):
        spread.append(jnp.where(at_x, rate_ref[k], 0.0))
    dense = lax.dot_general(
        jnp.concatenate(spread, axis=0), at_y, (((1,), (1,)), ((), ())),
        precision=lax.Precision.HIGHEST, preferred_element_type=jnp.float32)
    count = dense[:cells]
    for n in range(SUBSTEPS):
        for k in range(levels - 1):
            lift[pl.ds((n * (levels - 1) + k) * cells, cells), :] = jnp.where(
                count > n + 0.5, dense[(k + 1) * cells:(k + 2) * cells], 0.0)

    pump(WINDOW + 1, WINDOW + 3)
    for load in loads:
        load.wait()

    def owner_of(s):
        return jnp.full((part, lats), owner_ref[0, s], jnp.int32)

    def pass_on(s, c, way, to):
        at = chunk(c)
        relay[way, at, :] = jnp.where(owner_of(s) == me, own[at, :], inbox[way, at, :])
        chain_copy(c, way, to).start()

    def near_step(s, c):
        @pl.when(inner)
        def _():
            chain_copy(c, near, near_to).wait_recv()
            pass_on(s, c, near, near_to)

    def far_arrives(s, c):
        chain_copy(c, far, near_to).wait_recv()

        @pl.when(inner)
        def _():
            pass_on(s, c, far, far_to)

    def choose(s, c):
        at = chunk(c)
        holder = owner_of(s)
        met[at, :] = jnp.where(
            holder == me, own[at, :], jnp.where(holder < me, inbox[0, at, :], inbox[1, at, :]))

    def far_step(s, c):
        far_arrives(s, c)
        choose(s, c)

    def rim_copy(s, side):
        at = pl.ds(0, 2 * levels) if side == 0 else pl.ds(2 * levels, levels)
        return pltpu.make_async_remote_copy(
            src_ref=rim_out.at[s, at], dst_ref=rim_in.at[s, at],
            send_sem=rim_send.at[s, side], recv_sem=rim_recv.at[s, side],
            device_id={"tile": left if side else right}, device_id_type=pl.DeviceIdType.MESH)

    def start_rim(s):
        mass_at = s * FIELDS * rows
        rim_out[s, pl.ds(0, levels), :] = met[cell_rows(mass_at + rows, cells - 1), :]
        rim_out[s, pl.ds(levels, levels), :] = met[cell_rows(mass_at, cells - 1), :]
        rim_out[s, pl.ds(2 * levels, levels), :] = met[cell_rows(mass_at, 0), :]
        rim_copy(s, 0).start()
        rim_copy(s, 1).start()

    def mass_terms(s):
        mass_at = s * FIELDS * rows
        for k in range(levels):
            at = pl.ds(k * cells, cells)
            inverse_o[at, :] = 1.0 / met[pl.ds(mass_at + k * cells, cells), :]
        for x in range(cells):
            inverse_t[pl.ds(x * levels, levels), :] = inverse_o[cell_rows(0, x), :]

    def x_terms(s):
        mass_at = s * FIELDS * rows
        inverses = [1.0 / rim_in[s, pl.ds(levels, levels), :]]
        fluxes = [rim_in[s, pl.ds(0, levels), :]]
        for x in range(cells):
            inverses.append(inverse_t[pl.ds(x * levels, levels), :])
            fluxes.append(met[cell_rows(mass_at + rows, x), :])
        inverses.append(1.0 / rim_in[s, pl.ds(2 * levels, levels), :])
        for x in range(cells + 1):
            at = pl.ds(x * levels, levels)
            cx[0, at, :] = fluxes[x]
            cx[1, at, :], cx[2, at, :] = face_terms(fluxes[x], inverses[x], inverses[x + 1])

    def y_terms(s):
        flux_at = (s * FIELDS + 2) * rows
        open_face = lax.broadcasted_iota(jnp.int32, (levels, lats), 1) < lats - 1
        for x in range(cells):
            at = pl.ds(x * levels, levels)
            flux = jnp.where(open_face, met[cell_rows(flux_at, x), :], 0.0)
            inverse = inverse_t[at, :]
            cy[0, at, :] = flux
            cy[1, at, :], cy[2, at, :] = face_terms(flux, inverse, pltpu.roll(inverse, lats - 1, 1))

    def z_terms(s):
        flux_at = (s * FIELDS + 3) * rows
        for k in range(levels - 1):
            at = pl.ds(k * cells, cells)
            flux = met[pl.ds(flux_at + k * cells, cells), :]
            cz[0, at, :] = flux
            cz[1, at, :], cz[2, at, :] = face_terms(
                flux, inverse_o[at, :], inverse_o[pl.ds((k + 1) * cells, cells), :])

    def padded_x(s, t):
        base = pl.multiple_of(t * rows, rows)
        q = [halo_in[s, 0, block(t * HALO + i, levels), :] for i in range(HALO)]
        q += [state[cell_rows(base, x), :] for x in range(cells)]
        return q + [halo_in[s, 1, block(t * HALO + i, levels), :] for i in range(HALO)]

    def shape_x(s, t):
        q = padded_x(s, t)
        rise = [q[i + 1] - q[i] for i in range(cells + 5)]
        up = [edge_rise(rise[i], rise[i + 1], rise[i + 2]) for i in range(cells + 3)]
        for i in range(cells + 2):
            at = block(t * (cells + 2) + i, levels)
            shapes[0, at, :], shapes[1, at, :] = limited(up[i + 1], rise[i + 1] - up[i])

    def sweep_x(s, t):
        q = padded_x(s, t)
        shape = []
        for i in range(cells + 2):
            at = block(t * (cells + 2) + i, levels)
            shape.append((shapes[0, at, :], shapes[1, at, :]))
        moved = []
        for j in range(cells + 1):
            at = pl.ds(j * levels, levels)
            moved.append(transport(
                cx[0, at, :], cx[1, at, :], cx[2, at, :],
                q[j + 2], *shape[j], q[j + 3], *shape[j + 1]))
        for x in range(cells):
            mid[block(t * cells + x, levels), :] = (
                q[x + 3] - (moved[x + 1] - moved[x]) * inverse_t[pl.ds(x * levels, levels), :])

    def sweep_y(x, q):
        at = pl.ds(x * levels, levels)
        inside = lax.broadcasted_iota(jnp.int32, (levels, lats), 1) < lats - 1

        def ahead(v):
            return pltpu.roll(v, lats - 1, 1)

        def behind(v):
            return pltpu.roll(v, 1, 1)

        q1 = ahead(q)
        rise = jnp.where(inside, q1 - q, 0.0)
        up = edge_rise(behind(rise), rise, ahead(rise))
        r, l = limited(up, behind(rise - up))
        moved = transport(cy[0, at, :], cy[1, at, :], cy[2, at, :], q, r, l, q1, ahead(r), ahead(l))
        return q - (moved - behind(moved)) * inverse_t[at, :]

    def sweep_ys(some):
        for x in range(cells):
            for t in some:
                swept[cell_rows(pl.multiple_of(t * rows, rows), x), :] = sweep_y(
                    x, mid[block(t * cells + x, levels), :])

    def sweep_z(s, t):
        base = pl.multiple_of(t * rows, rows)
        q = [swept[pl.ds(base + k * cells, cells), :] for k in range(levels)]
        zero = jnp.zeros_like(q[0])
        rise = [zero] + [q[k + 1] - q[k] for k in range(levels - 1)] + [zero]
        up = [zero] + [edge_rise(rise[k], rise[k + 1], rise[k + 2]) for k in range(levels - 1)]
        shape = [(zero, zero)]
        for k in range(1, levels - 1):
            shape.append(limited(up[k + 1], rise[k] - up[k]))
        shape.append((zero, zero))
        moved = [zero]
        for k in range(levels - 1):
            at = pl.ds(k * cells, cells)
            moved.append(transport(
                cz[0, at, :], cz[1, at, :], cz[2, at, :], q[k], *shape[k], q[k + 1], *shape[k + 1]))
        moved.append(zero)
        q = [
            q[k] - (moved[k + 1] - moved[k]) * inverse_o[pl.ds(k * cells, cells), :]
            for k in range(levels)
        ]
        for n in range(SUBSTEPS):
            gain = [
                lift[pl.ds((n * (levels - 1) + k) * cells, cells), :] * q[k] for k in range(levels - 1)
            ]
            q = [
                (q[k] + gain[k - 1] if k else q[k]) - (gain[k] if k < levels - 1 else 0.0)
                for k in range(levels)
            ]
        target = out_ref if s == steps - 1 else state
        for k in range(levels):
            target[pl.ds(base + k * cells, cells), :] = q[k]

    together = next(n for n in (4, 2, 1) if tracers % n == 0)
    loops = tracers // together

    def each_group(body):
        def run(p, carry):
            body(p, [p * together + i for i in range(together)])
            return carry
        lax.fori_loop(0, loops, run, 0)

    def halo_arrives(s, some):
        for t in some:
            for side in (0, 1):
                halo_copy(s, side, t, 1).wait_recv()

    def rim_arrives(s):
        for side in (0, 1):
            rim_copy(s, side).wait_recv()

    def near_if(c):
        if c < chunk_total:
            near_step(c // (FIELDS * split), c)

    def shape_xs(s):
        each_group(lambda p, some: [shape_x(s, t) for t in some])

    def sweep_xs(s):
        each_group(lambda p, some: [sweep_x(s, t) for t in some])

    def sweep_zs(s):
        def run(p, some):
            for t in some:
                sweep_z(s, t)
            if s < steps - 1:
                for t in some:
                    pack_halo(s + 1, t, state, pl.multiple_of(t * rows, rows))
                    for side in (0, 1):
                        halo_copy(s + 1, side, t, 1).start()
        each_group(run)

    def link(f):
        s, field = divmod(f, FIELDS)
        for c in range(f * split, (f + 1) * split):
            near_if(c + LEAD)
            far_step(s, c)
        if field == 0 and s == 0:
            mass_terms(s)
        if field == 1:
            start_rim(s)

    def links(start, stop):
        for f in range(start, min(stop, steps * FIELDS)):
            link(f)

    for side in (0, 1):
        halo_copy(0, side, 0, tracers).wait_recv()
    near_if(0)
    shape_xs(0)
    pump(WINDOW + 3, chunk_total)
    for c in range(1, LEAD):
        near_if(c)
    links(0, FIELDS - (steps == 1))
    for s in range(steps):
        follow = (s + 1) * FIELDS
        last = range(chunk_total - split, chunk_total)
        final = s == steps - 1
        if s > 0:
            links(follow - 2, follow - final)
            mass_terms(s)
        if final:
            @pl.when(inner)
            def _():
                for c in last:
                    far_arrives(s, c)
        if s > 0:
            each_group(lambda p, some: halo_arrives(s, some))
            shape_xs(s)
        rim_arrives(s)
        x_terms(s)
        sweep_xs(s)
        y_terms(s)
        each_group(lambda p, some: sweep_ys(some))
        if final:
            @pl.when(at_end)
            def _():
                for c in last:
                    far_arrives(s, c)

            for c in last:
                choose(s, c)
        else:
            links(follow, follow + 1)
        z_terms(s)
        sweep_zs(s)
        if not final:
            links(follow + 1, follow + 2)

    for side in (0, 1):
        halo_copy(0, side, 0, tracers).wait_send()
        for s in range(steps):
            rim_copy(s, side).wait_send()
    for s in range(1, steps):
        for t in range(tracers):
            for side in (0, 1):
                halo_copy(s, side, t, 1).wait_send()
    for c in range(max(chunk_total - WINDOW, 0), chunk_total):
        chain_copy(c, near, near_to).wait_send()

    @pl.when(inner)
    def _():
        for c in range(chunk_total):
            if c < chunk_total - WINDOW:
                chain_copy(c, near, near_to).wait_send()
            chain_copy(c, far, far_to).wait_send()


def body(dims, tracers, flux_pool, mass_pool, owner, conv_cols, conv_steps, conv_rate):
    _, _, steps, count, levels, cells, lats = dims
    rows = levels * cells
    total = steps * FIELDS
    chunks = total * SPLIT
    flat = (count * rows, lats)
    hbm = pl.BlockSpec(memory_space=pl.ANY)
    f32 = jnp.float32
    operands = (
        owner.T, conv_cols, conv_steps, jnp.transpose(conv_rate, (1, 0, 2)), tracers.reshape(flat),
        flux_pool.reshape(steps * 3 * rows, lats), mass_pool.reshape(steps * rows, lats),
    )
    out = pl.pallas_call(
        functools.partial(kernel, dims),
        out_shape=pltpu.VMEM(flat, f32),
        in_specs=[hbm] * 7,
        out_specs=pl.BlockSpec(memory_space=pltpu.VMEM),
        scratch_shapes=[
            pltpu.SMEM((1, steps), jnp.int32),
            pltpu.VMEM(conv_cols.shape, jnp.int32),
            pltpu.VMEM(conv_steps.shape, jnp.int32),
            pltpu.VMEM((levels - 1, 1, conv_cols.shape[1]), f32),
            pltpu.VMEM((total * rows, lats), f32),
            pltpu.VMEM((2, total * rows, lats), f32),
            pltpu.VMEM((2, total * rows, lats), f32),
            pltpu.VMEM((total * rows, lats), f32),
            pltpu.VMEM(flat, f32),
            pltpu.VMEM(flat, f32),
            pltpu.VMEM(flat, f32),
            pltpu.VMEM((2, count * (cells + 2) * levels, lats), f32),
            pltpu.VMEM((steps, 2, count * HALO * levels, lats), f32),
            pltpu.VMEM((steps, 2, count * HALO * levels, lats), f32),
            pltpu.VMEM((steps, 3 * levels, lats), f32),
            pltpu.VMEM((steps, 3 * levels, lats), f32),
            pltpu.VMEM((3, (cells + 1) * levels, lats), f32),
            pltpu.VMEM((3, rows, lats), f32),
            pltpu.VMEM((3, (levels - 1) * cells, lats), f32),
            pltpu.VMEM((rows, lats), f32),
            pltpu.VMEM((rows, lats), f32),
            pltpu.VMEM((SUBSTEPS * (levels - 1) * cells, lats), f32),
            pltpu.SemaphoreType.DMA((2 * steps,)),
            pltpu.SemaphoreType.DMA,
            pltpu.SemaphoreType.DMA((4,)),
            pltpu.SemaphoreType.DMA((2, chunks)),
            pltpu.SemaphoreType.DMA((2, chunks)),
            pltpu.SemaphoreType.DMA((steps, 2, count)),
            pltpu.SemaphoreType.DMA((steps, 2, count)),
            pltpu.SemaphoreType.DMA((steps, 2)),
            pltpu.SemaphoreType.DMA((steps, 2)),
        ],
        compiler_params=pltpu.CompilerParams(collective_id=0, has_side_effects=True, vmem_limit_bytes=VMEM_BYTES),
    )(*(pltpu.with_memory_space_constraint(x, pltpu.HBM) for x in operands))
    return out.reshape(tracers.shape)


def solution(mesh):
    def local(tracers, flux_pool, *rest):
        dims = (mesh.shape["tile"], mesh.shape["trc"], flux_pool.shape[1]) + tracers.shape
        return body(dims, tracers, flux_pool, *rest)

    in_specs = (
        P("trc", None, "tile", None),
        P("trc", None, None, None, "tile", None),
        P("trc", None, None, "tile", None),
        P(None, "tile"),
        P("tile", None),
        P("tile", None),
        P("tile", None, None),
    )
    out_specs = P("trc", None, "tile", None)
    return jax.shard_map(local, mesh=mesh, in_specs=in_specs, out_specs=out_specs, check_vma=False)
```
